32 devices in a mesh: seq: 8 (over z, x), row: 4 (over y, core).
Axes of the slice: x: 2, y: 2, z: 4, core: 2. Of those that a mesh axis runs over, the one named last changes fastest.
Arguments:
- tokens: bfloat16 [8, 1024, 2048], P('row', 'seq'), may hold values from -6 to 6
- first_layer_values: bfloat16 [8, 1024, 2048], P('row', 'seq'), may hold values from -6 to 6
- document_lengths: int32 [8, 4], P('row'), may hold values from 1 to 512, 1024 in all within a row
- vectors: bfloat16 [19, 2048], P(None, ('seq', 'row')), may hold values from -6 to 3
- lowrank_down: bfloat16 [2048, 512], P(('seq', 'row')), may hold values from -0.125 to 0.125
- lowrank_up: bfloat16 [512, 2048], P(None, ('seq', 'row')), may hold values from -0.625 to 0.625
- square: bfloat16 [4, 2048, 2048], P(None, ('seq', 'row')), may hold values from -0.125 to 0.125
- channel_key_weight: bfloat16 [2048, 8192], P(('seq', 'row')), may hold values from -0.125 to 0.125
- channel_value_weight: bfloat16 [8192, 2048], P(('seq', 'row')), may hold values from -0.0625 to 0.0625
- output_gradient: bfloat16 [8, 1024, 2048], P('row', 'seq'), may hold values from -6 to 6
Outputs:
- mixed: bfloat16 [8, 1024, 2048], P('row', 'seq')
- tokens_grad: bfloat16 [8, 1024, 2048], P('row', 'seq')
- first_grad: bfloat16 [8, 1024, 2048], P('row', 'seq')
- vectors_gradient: float32 [19, 2048], P(None, ('seq', 'row'))
- lowrank_down_gradient: float32 [2048, 512], P(('seq', 'row'))
- lowrank_up_gradient: float32 [512, 2048], P(None, ('seq', 'row'))
- square_grad: float32 [4, 2048, 2048], P(None, ('seq', 'row'))
- key_grad: float32 [2048, 8192], P(('seq', 'row'))
- value_grad: float32 [8192, 2048], P(('seq', 'row'))
The draws below stay inside these ranges and needn't reach their ends.
All inputs are finite; a program needn't handle non-finite values.
Results may differ from the reference program's by a relative error of at most 0.015.
Values may be sent and summed in bfloat16 or wider, within the bound.
A program may use at most 448 MiB of HBM per device.

```python
import math
import jax
import jax.numpy as jnp
import numpy as np
from jax import lax

EMBED_DIMENSION = 2048
ATTENTION_SPLITS = 32
SPLIT_DIMENSION = 64
FF = 8192
DECAY_INNER = 96
LA = 96
LV = 64
NVEC = 19
BLOCK = 64
DOCS = 4
LENGTH = 1024
ROWS = 8
LOWRANK_TOTAL = 512


def draw_vectors(key, part):
    first_key, second_key = jax.random.split(jax.random.fold_in(key, 7))
    uniform_part = jax.random.uniform(first_key, (NVEC, EMBED_DIMENSION), jnp.float32)
    normal_draw_share = jnp.clip(jax.random.normal(second_key, (NVEC, EMBED_DIMENSION), jnp.float32), -3.0, 3.0)
    line_labels = jnp.arange(NVEC)[:, None]
    gains = 0.5 + uniform_part
    offsets = 0.3 * normal_draw_share
    decays = -6.0 + 8.0 * uniform_part
    extra_summand = 0.5 * normal_draw_share
    is_gain = (line_labels == 0) | (line_labels == 2) | (line_labels == 13) | (line_labels == 14) | (line_labels == 16)
    is_offset = (line_labels == 1) | (line_labels == 3) | (line_labels == 17)
    is_normal = (line_labels == 11) | (line_labels == 12)
    sublevel_outcome = jnp.where(is_gain, gains, uniform_part)
    sublevel_outcome = jnp.where(is_offset, offsets, sublevel_outcome)
    sublevel_outcome = jnp.where(is_normal, normal_draw_share, sublevel_outcome)
    sublevel_outcome = jnp.where(line_labels == 10, decays, sublevel_outcome)
    sublevel_outcome = jnp.where(line_labels == 15, extra_summand, sublevel_outcome)
    return sublevel_outcome.astype(jnp.bfloat16)


def level_of(key, extent, cuts, low, largest):
    level, own = 1.0, jax.random.fold_in(key, 6)
    for dim, shards_of in cuts:
        draws = jnp.exp(jax.random.uniform(jax.random.fold_in(own, dim), (shards_of,), jnp.float32, low / len(cuts), largest / len(cuts)))
        level = level * jnp.repeat(draws, extent[dim] // shards_of).reshape([-1 if axis == dim else 1 for axis in range(len(extent))])
    return level


def profile(amount, total, limit, lean):
    weights = [(1 << 20) // math.isqrt(rank ** lean) + 1 for rank in range(2, amount + 1)]
    surplus, holding = total - limit - (amount - 1), [1] * (amount - 1)
    while surplus > 0:
        movable = [i for i in range(amount - 1) if holding[i] < limit]
        whole, left = sum([weights[i] for i in movable]), surplus
        for i in movable:
            more = min(limit - holding[i], max(1, left * weights[i] // whole), surplus)
            holding[i] = holding[i] + more
            surplus = surplus - more
    return np.array([limit] + holding)


def uneven_parts(stream_key, number_of, total, reach, slope):
    if number_of == 2:
        one = jax.random.randint(stream_key, (), max(1, total - reach), min(reach, total - 1) + 1)
        return jnp.stack([one, total - one])
    sizes = jnp.asarray(profile(number_of, total, reach, slope), jnp.int32)
    twos = (number_of - 1) // 2
    giver, taker = sizes[1:1 + 2 * twos:2], sizes[2:2 + 2 * twos:2]
    margin = jnp.minimum(giver - 1, reach - taker)
    passed = jax.random.randint(jax.random.fold_in(stream_key, 1), (twos,), 0, 1 << 20) % (margin + 1)
    sizes = sizes.at[1:1 + 2 * twos:2].set(giver - passed).at[2:2 + 2 * twos:2].set(taker + passed)
    return sizes[jax.random.permutation(jax.random.fold_in(stream_key, 2), number_of)]


def normal_values(own_key, shape, deviation, limit, cuts=(), kind=jnp.bfloat16):
    factor_of = level_of(own_key, shape, cuts, -0.22, 0.18) if cuts else 1.0
    array = jax.random.normal(own_key, shape, jnp.float32) * deviation * factor_of
    return jnp.minimum(jnp.maximum(array, -limit), limit).astype(kind)


def setup_inputs(seed: int = 0) -> dict:
    seeds = jax.random.split(jax.random.key(seed), 11)
    return {
        "tokens": normal_values(seeds[0], (ROWS, LENGTH, EMBED_DIMENSION), 1.0, 6.0, ((0, 4), (1, 8))),
        "first_layer_values": normal_values(seeds[1], (ROWS, LENGTH, EMBED_DIMENSION), 1.0, 6.0, ((0, 4), (1, 8))),
        "document_lengths": jax.vmap(lambda own: uneven_parts(own, DOCS, LENGTH, LENGTH // 2, 2))(jax.random.split(seeds[2], ROWS)).reshape((ROWS, DOCS)).astype(jnp.int32),
        "vectors": draw_vectors(jax.random.fold_in(seeds[10], 71), 0),
        "lowrank_down": normal_values(seeds[4], (EMBED_DIMENSION, LOWRANK_TOTAL), EMBED_DIMENSION ** -0.5, 0.125, ((0, 32),)),
        "lowrank_up": normal_values(seeds[5], (LOWRANK_TOTAL, EMBED_DIMENSION), DECAY_INNER ** -0.5, 0.625, ((1, 32),)),
        "square": normal_values(seeds[6], (4, EMBED_DIMENSION, EMBED_DIMENSION), EMBED_DIMENSION ** -0.5, 0.125, ((1, 32),)),
        "channel_key_weight": normal_values(seeds[7], (EMBED_DIMENSION, FF), EMBED_DIMENSION ** -0.5, 0.125, ((0, 32),)),
        "channel_value_weight": normal_values(seeds[8], (FF, EMBED_DIMENSION), FF ** -0.5, 0.0625, ((0, 32),)),
        "output_gradient": normal_values(seeds[9], (ROWS, LENGTH, EMBED_DIMENSION), 1.0, 6.0, ((0, 4), (1, 8))),
    }


HIGHEST = lax.Precision.HIGHEST

@jax.custom_vjp
def lowrank_hidden(v):
    return lax.optimization_barrier(v.astype(jnp.bfloat16)).astype(jnp.float32)

@jax.custom_vjp
def lowrank_hidden_back(v):
    return v

def low_keep(v):
    return (lowrank_hidden(v), None)

def low_pass(kept, grad):
    return (grad,)

def back_keep(v):
    return (v, None)

def back_low(kept, grad):
    return (lowrank_hidden(grad),)
lowrank_hidden.defvjp(low_keep, low_pass)
lowrank_hidden_back.defvjp(back_keep, back_low)

def precise_product_matrix(left_side, right_side):
    return jnp.dot(left_side, right_side, precision=HIGHEST)

def layer_norm(layer_inputs, norm_gain, norm_bias):
    middle = lax.optimization_barrier(jnp.mean(layer_inputs, axis=-1, keepdims=True))
    centred = layer_inputs - middle
    spread = lax.optimization_barrier(jnp.mean(centred * centred, axis=-1, keepdims=True))
    return centred * lax.rsqrt(spread + 1e-05) * norm_gain + norm_bias

def send_value(layer_inputs):
    return lowrank_hidden_back(lowrank_hidden(layer_inputs))

def doc_marks(lengths, count):
    starts = (jnp.cumsum(lengths) - lengths).astype(jnp.int32)
    positions = jnp.arange(count, dtype=jnp.int32)
    return jnp.any(positions[:, None] == starts[None, :], axis=1).astype(jnp.float32)

def recurrence(acceptance_lines, log_forgetting, address_adjusted, content_lines, address_unitlength, recurrent_state_update, restart_markers):
    decay = jnp.exp(log_forgetting)
    beta_keys = address_unitlength * recurrent_state_update

    def token_step(carry_state, token_item):
        rec_now, decay_now, key_now, val_now, norm_now, beta_now, reset_now = token_item
        carry_state = carry_state * (1.0 - reset_now)
        removed = jnp.einsum('hij,hj->hi', carry_state, norm_now, precision=HIGHEST)
        carry_state = carry_state * decay_now[:, None, :] - removed[:, :, None] * beta_now[:, None, :] + val_now[:, :, None] * key_now[:, None, :]
        return (carry_state, jnp.einsum('hij,hj->hi', carry_state, rec_now, precision=HIGHEST))

    def block_run(carry_state, block_items):
        return lax.scan(token_step, carry_state, block_items)
    pieces = (acceptance_lines, decay, address_adjusted, content_lines, address_unitlength, beta_keys, restart_markers)
    block_items = tuple((portion_item.reshape((-1, BLOCK) + portion_item.shape[1:]) for portion_item in pieces))
    start_state = jnp.zeros((ATTENTION_SPLITS, SPLIT_DIMENSION, SPLIT_DIMENSION), jnp.float32)
    _, outputs = lax.scan(jax.checkpoint(block_run), start_state, block_items)
    return outputs.reshape(acceptance_lines.shape)

def split_tensor_layout(acceptance_lines, log_forgetting, address_adjusted, content_lines, address_unitlength, recurrent_state_update, restart_markers, cluster_standardize_scaling, cluster_standardize_offset, extra_coefficient):
    outputs = recurrence(acceptance_lines, log_forgetting, address_adjusted, content_lines, address_unitlength, recurrent_state_update, restart_markers)
    middle = lax.optimization_barrier(jnp.mean(outputs, axis=-1, keepdims=True))
    centred = outputs - middle
    spread = lax.optimization_barrier(jnp.mean(centred * centred, axis=-1, keepdims=True))
    standardized_lines = centred * lax.rsqrt(spread + 1.0) * cluster_standardize_scaling.reshape(ATTENTION_SPLITS, SPLIT_DIMENSION) + cluster_standardize_offset.reshape(ATTENTION_SPLITS, SPLIT_DIMENSION)
    extra_summed = lax.optimization_barrier(jnp.sum(acceptance_lines * address_adjusted * extra_coefficient.reshape(ATTENTION_SPLITS, SPLIT_DIMENSION), axis=-1, keepdims=True))
    return (standardized_lines + extra_summed * content_lines).reshape(-1, EMBED_DIMENSION)

def layer_row_pass(layer_inputs, first_layer_vals, restart_markers, vectors, lowrank_down, lowrank_up, square, channel_key_weight, channel_value_weight):
    keep_mask = (1.0 - restart_markers)[:, None]
    hidden_one = layer_norm(layer_inputs, vectors[0], vectors[1])
    shifted = jnp.concatenate([jnp.zeros_like(hidden_one[:1]), hidden_one[:-1]], axis=0) * keep_mask
    mixed_incoming = [lowrank_hidden(hidden_one + (shifted - hidden_one) * vectors[4 + member]) for member in range(6)]
    rec_proj = precise_product_matrix(mixed_incoming[0], square[0])
    key_proj = lowrank_hidden_back(precise_product_matrix(mixed_incoming[2], square[1]))
    val_proj = lowrank_hidden_back(precise_product_matrix(mixed_incoming[3], square[2]))
    trimmed_decay = DECAY_INNER
    trimmed_rate = DECAY_INNER + LA
    trimmed_mix = DECAY_INNER + LA + LV
    decay_lower_map = lowrank_hidden_back(precise_product_matrix(mixed_incoming[1], lowrank_down[:, :trimmed_decay]))
    decay_upper_map = lowrank_hidden_back(precise_product_matrix(lowrank_hidden(jnp.tanh(decay_lower_map)), lowrank_up[:trimmed_decay]))
    rate_lower_map = lowrank_hidden_back(precise_product_matrix(mixed_incoming[4], lowrank_down[:, trimmed_decay:trimmed_rate]))
    rate_upper_map = lowrank_hidden_back(precise_product_matrix(lowrank_hidden(rate_lower_map), lowrank_up[trimmed_decay:trimmed_rate]))
    residual_lower_map = lowrank_hidden_back(precise_product_matrix(mixed_incoming[3], lowrank_down[:, trimmed_rate:trimmed_mix]))
    residual_upper_map = lowrank_hidden_back(precise_product_matrix(lowrank_hidden(residual_lower_map), lowrank_up[trimmed_rate:trimmed_mix]))
    gate_lower_map = lowrank_hidden_back(precise_product_matrix(mixed_incoming[5], lowrank_down[:, trimmed_mix:]))
    gate_upper_map = lowrank_hidden_back(precise_product_matrix(lowrank_hidden(jax.nn.sigmoid(gate_lower_map)), lowrank_up[trimmed_mix:]))
    log_forgetting = -0.606531 * jax.nn.sigmoid(vectors[10] + decay_upper_map)
    recurrent_state_update = jax.nn.sigmoid(vectors[11] + rate_upper_map)
    val_gate = jax.nn.sigmoid(vectors[12] + residual_upper_map)
    values_mixed = val_proj + (first_layer_vals - val_proj) * val_gate
    key_scaled = (key_proj * vectors[13]).reshape(-1, ATTENTION_SPLITS, SPLIT_DIMENSION)
    address_unitlength = (key_scaled * lax.rsqrt(lax.optimization_barrier(jnp.sum(key_scaled * key_scaled, axis=-1, keepdims=True)) + 1e-06)).reshape(-1, EMBED_DIMENSION)
    address_adjusted = key_proj * (1.0 + (recurrent_state_update - 1.0) * vectors[14])
    sent = [send_value(portion_item).reshape(-1, ATTENTION_SPLITS, SPLIT_DIMENSION) for portion_item in (rec_proj, log_forgetting, address_adjusted, values_mixed, address_unitlength, recurrent_state_update)]
    heads_out = split_tensor_layout(sent[0], sent[1], sent[2], sent[3], sent[4], sent[5], restart_markers, vectors[16], vectors[17], vectors[15])
    back_sent = send_value(heads_out)
    gated = lowrank_hidden(back_sent * gate_upper_map)
    attended = lowrank_hidden_back(precise_product_matrix(gated, square[3]))
    after_mix = layer_inputs + attended
    hidden_two = layer_norm(after_mix, vectors[2], vectors[3])
    shifted_two = jnp.concatenate([jnp.zeros_like(hidden_two[:1]), hidden_two[:-1]], axis=0) * keep_mask
    key_in = lowrank_hidden(hidden_two + (shifted_two - hidden_two) * vectors[18])
    key_act = lowrank_hidden_back(precise_product_matrix(key_in, channel_key_weight))
    squared = lowrank_hidden(jnp.square(jax.nn.relu(key_act)))
    ffn_out = lowrank_hidden_back(precise_product_matrix(squared, channel_value_weight))
    return after_mix + ffn_out

def reference(tokens, first_layer_values, document_lengths, vectors, lowrank_down, lowrank_up, square, channel_key_weight, channel_value_weight, output_gradient):
    parameter_set = tuple((portion_item.astype(jnp.float32) for portion_item in (vectors, lowrank_down, lowrank_up, square, channel_key_weight, channel_value_weight)))

    def one_row(totals, row_items):
        row_tokens, row_first, row_lengths, row_grad = row_items
        restart_markers = doc_marks(row_lengths, row_tokens.shape[0])

        def forward(layer_inputs, first_layer_vals, vec_in, down_in, up_in, square_in, key_in, value_in):
            return layer_row_pass(layer_inputs, first_layer_vals, restart_markers, vec_in, down_in, up_in, square_in, key_in, value_in)
        sublevel_outcome, pullback = jax.vjp(forward, row_tokens.astype(jnp.float32), row_first.astype(jnp.float32), *parameter_set)
        grads = pullback(row_grad.astype(jnp.float32))
        totals = tuple((earlier + later for earlier, later in zip(totals, grads[2:])))
        return (totals, (sublevel_outcome.astype(jnp.bfloat16), grads[0].astype(jnp.bfloat16), grads[1].astype(jnp.bfloat16)))
    zeros_start = tuple((jnp.zeros(portion_item.shape, jnp.float32) for portion_item in parameter_set))
    totals, row_outs = lax.scan(one_row, zeros_start, (tokens, first_layer_values, document_lengths, output_gradient))
    return (row_outs[0], row_outs[1], row_outs[2], totals[0], totals[1], totals[2], totals[3], totals[4], totals[5])
```

```python
import jax
import jax.numpy as jnp
from jax import lax
from jax.experimental import pallas as pl
from jax.experimental.pallas import tpu as pltpu
from jax.sharding import Mesh, PartitionSpec as P

DECAY_INNER = 96
LA = 96
LV = 64

BF=jnp.bfloat16; F32=jnp.float32
SD=64; BLK=64
NN=(((1,),(0,)),((),())); NT=(((1,),(1,)),((),())); TN=(((0,),(0,)),((),()))

def mm(a,b,d): return lax.dot_general(a,b,d,preferred_element_type=F32)

class Geo:
    def __init__(s, gc):
        s.gc=gc; s.gh=gc//SD
        lane=lax.broadcasted_iota(jnp.int32,(1,gc),1)
        s.head=lane//SD
        s.lm=[(s.head==h).astype(BF) for h in range(s.gh)]
        row=lax.broadcasted_iota(jnp.int32,(BLK,gc),0)
        col=lax.broadcasted_iota(jnp.int32,(BLK,gc),1)%SD
        s.below=row>col; s.upto=row>=col
    def blk(s,x):
        return jnp.concatenate([x*m for m in s.lm],axis=0) if s.gh>1 else x
    def ext(s,x):
        out=x[:BLK]
        for h in range(1,s.gh):
            out=jnp.where(s.head==h,x[h*BLK:(h+1)*BLK],out)
        return out

def headsum(x,ones):
    hi=x.astype(BF); lo=(x-hi.astype(F32)).astype(BF)
    return mm(hi,ones,NN)+mm(lo,ones,NN)

def decayed(geo,ws,tri):
    w=ws.astype(F32)
    cum=mm(tri,ws,NN)
    return w,cum,jnp.exp(cum-w),jnp.exp(cum),jnp.exp(-cum)

def first_kernel(rp,kp,vp,uw,ua,uv,fl,vec,meta,segrow,tri,ones,rs,ws,ks,vs,qs,as_,ab):
    C=rp.shape[1]; gc=min(C,256); geo=Geo(gc)
    same=meta[:,0:1]==segrow[0]
    strict=geo.below&same
    for g in range(C//gc):
        sl=slice(g*gc,(g+1)*gc)
        V=lambda i: vec[i:i+1,sl]
        k0=kp[:,sl]; v0=vp[:,sl]
        lw=-0.606531*jax.nn.sigmoid(V(0)+uw[:,sl])
        al=jax.nn.sigmoid(V(1)+ua[:,sl])
        vm=jax.nn.sigmoid(V(2)+uv[:,sl])
        v=v0+(fl[:,sl].astype(F32)-v0)*vm
        kn=k0*V(3)
        kk=kn*lax.rsqrt(headsum(kn*kn,ones[...])+1e-6)
        km=k0*(1.0+(al-1.0)*V(4))
        q_=kk.astype(BF); w_=lw.astype(BF); a_=al.astype(BF)
        rs[:,sl]=rp[:,sl].astype(BF); ws[:,sl]=w_; ks[:,sl]=km.astype(BF)
        vs[:,sl]=v.astype(BF); qs[:,sl]=q_; as_[:,sl]=a_
        w,cum,eP,eC,eN=decayed(geo,w_,tri[...])
        q=q_.astype(F32)
        qu=(q*eP).astype(BF); bb=(q*a_.astype(F32)*eN).astype(BF)
        ab[:,sl]=jnp.where(strict,mm(qu,geo.blk(bb),NT),0.0)

def solve_kernel(a,t):
    n=a.shape[0]
    t[...]=jnp.zeros_like(t)
    cidx=lax.broadcasted_iota(jnp.int32,t.shape[1:],0)
    def outer(i,_):
        def inner(jb,acc):
            for jj in range(8):
                j=jb*8+jj
                acc=acc-a[i,pl.ds(j,1),:]*t[j]
            return acc
        acc=lax.fori_loop(0,i//8+1,inner,(cidx==i).astype(F32))
        t[i]=acc
        return 0
    lax.fori_loop(0,n,outer,0)

def forward_kernel(rs,ws,ks,vs,qs,as_,tt,vec,meta,segrow,tri,ones,y,o_out,u_out,s_out,state):
    C=rs.shape[1]; gc=min(C,256); geo=Geo(gc)
    @pl.when(pl.program_id(0)==0)
    def _(): state[...]=jnp.zeros_like(state)
    same=meta[:,0:1]==segrow[0]
    carried=meta[:,1:2]; live=meta[:,2:3]; last=meta[BLK-1:BLK,1:2]
    strict=geo.below&same; incl=geo.upto&same
    for g in range(C//gc):
        sl=slice(g*gc,(g+1)*gc)
        V=lambda i: vec[i:i+1,sl]
        w,cum,eP,eC,eN=decayed(geo,ws[:,sl],tri[...])
        q=qs[:,sl].astype(F32); r=rs[:,sl].astype(F32); k=ks[:,sl].astype(F32)
        vb=vs[:,sl]; v=vb.astype(F32); a=as_[:,sl].astype(F32)
        qq=jnp.concatenate([(q*eP).astype(BF),(r*eC).astype(BF)],axis=0)
        kb=(k*eN).astype(BF); bb=(q*a*eN).astype(BF)
        mk=mm(qq,geo.blk(kb),NT)
        al=jnp.concatenate([jnp.where(strict,mk[:BLK],0.0).astype(BF),jnp.where(incl,mk[BLK:],0.0).astype(BF)],axis=0)
        lb=jnp.where(incl,mm(qq[BLK:],geo.blk(bb),NT),0.0).astype(BF)
        s0=state[g]; sb=s0.astype(BF)
        s_out[0,g]=sb
        qst=mm(qq,sb,NT)
        av=mm(al,geo.blk(vb),NN)
        rhs=carried*qst[:BLK]+av[:BLK]
        u=mm(tt[:,sl],geo.blk(rhs.astype(BF)),NN)
        ub=u.astype(BF)
        u_out[:,sl]=ub
        o=carried*qst[BLK:]+av[BLK:]-mm(lb,geo.blk(ub),NN)
        vu=jnp.concatenate([(v*live).astype(BF),(u*(-live)).astype(BF)],axis=0)
        ds=mm(vu,jnp.concatenate([kb,bb],axis=0),TN)
        tail=eC[BLK-1:BLK]
        state[g]=(last*s0+ds*ones[...].astype(F32))*tail
        o_out[:,sl]=o
        mean=headsum(o,ones[...])*(1.0/SD)
        cen=o-mean
        var=headsum(cen*cen,ones[...])*(1.0/SD)
        extra=headsum(r*k*V(5),ones[...])
        y[:,sl]=(cen*lax.rsqrt(var+1.0)*V(6)+V(7)+extra*v).astype(BF)

def backward_kernel(dy,o_in,rs,ws,ks,vs,qs,as_,tt,u_in,s_in,rp,kp,vp,uw,ua,uv,fl,vec,meta,segrow,tri,tru,ones,
                    drp,dkp,dvp,duw,dua,duv,dfl,dvec,state):
    C=rs.shape[1]; gc=min(C,256); geo=Geo(gc)
    @pl.when(pl.program_id(0)==0)
    def _():
        state[...]=jnp.zeros_like(state)
        dvec[...]=jnp.zeros_like(dvec)
    same=meta[:,0:1]==segrow[0]
    carried=meta[:,1:2]; live=meta[:,2:3]; last=meta[BLK-1:BLK,1:2]
    strict=geo.below&same; incl=geo.upto&same
    cat=lambda *x: jnp.concatenate(x,axis=0)
    rsum=lambda x: jnp.sum(x,axis=0,keepdims=True)
    for g in range(C//gc):
        sl=slice(g*gc,(g+1)*gc)
        V=lambda i: vec[i:i+1,sl]
        on=ones[...]
        w,cum,eP,eC,eN=decayed(geo,ws[:,sl],tri[...])
        q=qs[:,sl].astype(F32); r=rs[:,sl].astype(F32); k=ks[:,sl].astype(F32)
        vb=vs[:,sl]; v=vb.astype(F32); a=as_[:,sl].astype(F32)
        d=dy[:,sl].astype(F32); o=o_in[:,sl]
        mean=headsum(o,on)*(1.0/SD); cen=o-mean
        rstd=lax.rsqrt(headsum(cen*cen,on)*(1.0/SD)+1.0)
        nrm=cen*rstd
        extra=headsum(r*k*V(5),on)
        de=headsum(d*v,on)
        dn=d*V(6)
        do=rstd*(dn-headsum(dn,on)*(1.0/SD)-nrm*(headsum(dn*nrm,on)*(1.0/SD)))
        g17=rsum(d); g16=rsum(d*nrm); g15=rsum(de*r*k)
        dr=de*k*V(5); dk=de*r*V(5); dv=d*extra
        qq=cat((q*eP).astype(BF),(r*eC).astype(BF))
        kb=(k*eN).astype(BF); bb=(q*a*eN).astype(BF)
        kblk=geo.blk(kb); bblk=geo.blk(bb)
        mk=mm(qq,kblk,NT)
        al=cat(jnp.where(strict,mk[:BLK],0.0).astype(BF),jnp.where(incl,mk[BLK:],0.0).astype(BF))
        lb=jnp.where(incl,mm(qq[BLK:],bblk,NT),0.0).astype(BF)
        ub=u_in[:,sl]; s0=s_in[0,g]
        tail=eC[BLK-1:BLK]
        ds1=state[g]*tail; dsb=ds1.astype(BF)
        kbs=mm(cat(kb,bb),dsb,NT)
        dob=do.astype(BF)
        du=-geo.ext(mm(lb,dob,TN))-live*kbs[BLK:]
        yy=geo.ext(mm(tt[:,sl],du.astype(BF),TN))
        yo=cat(yy.astype(BF),dob)
        cyo=cat((carried*yy).astype(BF),(carried*do).astype(BF))
        mv=mm(yo,geo.blk(vb),NT); mu=mm(yo,geo.blk(ub),NT)
        dkm=cat(jnp.where(strict,mv[:BLK],0.0).astype(BF),jnp.where(incl,mv[BLK:],0.0).astype(BF))
        dbm=cat(jnp.where(strict,-mu[:BLK],0.0).astype(BF),jnp.where(incl,-mu[BLK:],0.0).astype(BF))
        dqq=mm(cyo,s0,NN)+mm(dkm,kblk,NN)+mm(dbm,bblk,NN)
        vus=mm(cat(vb,ub),dsb,NN)
        kst=live*vus[:BLK]; bst=-(live*vus[BLK:])
        dkb=geo.ext(mm(dkm,qq,TN))+kst
        dbb=geo.ext(mm(dbm,qq,TN))+bst
        dv=dv+geo.ext(mm(al,yo,TN))+live*kbs[:BLK]
        kf=kb.astype(F32); bf=bb.astype(F32); qf=qq.astype(F32)
        dlast=last*rsum(ds1*s0.astype(F32))+rsum(kf*kst+bf*bst)
        state[g]=mm(cyo,qq,TN)*on.astype(F32)+last*ds1
        dqu=dqq[:BLK]*qf[:BLK]
        dcum=dqu+dqq[BLK:]*qf[BLK:]-dkb*kf-dbb*bf
        hi=dcum.astype(BF); rest=dcum-hi.astype(F32); lo=rest.astype(BF)
        lo2=(rest-lo.astype(F32)).astype(BF)
        dw=mm(tru[...],hi,NN)+mm(tru[...],lo,NN)+mm(tru[...],lo2,NN)+dlast-dqu
        dben=dbb*eN
        dq=dqq[:BLK]*eP+dben*a
        da=dben*q
        dr=dr+dqq[BLK:]*eC
        dk=dk+dkb*eN
        k0=kp[:,sl]; v0=vp[:,sl]
        sg=jax.nn.sigmoid(V(0)+uw[:,sl]); af=jax.nn.sigmoid(V(1)+ua[:,sl]); vm=jax.nn.sigmoid(V(2)+uv[:,sl])
        kn=k0*V(3)
        ri=lax.rsqrt(headsum(kn*kn,on)+1e-6)
        kk=kn*ri
        gw=(-0.606531)*dw*sg*(1.0-sg)
        gv=dv*(fl[:,sl].astype(F32)-v0)*vm*(1.0-vm)
        da=da+dk*k0*V(4)
        ga=da*af*(1.0-af)
        dkn=ri*(dq-kk*headsum(dq*kk,on))
        drp[:,sl]=dr.astype(BF)
        dkp[:,sl]=(dk*(1.0+(af-1.0)*V(4))+dkn*V(3)).astype(BF)
        dvp[:,sl]=(dv*(1.0-vm)).astype(BF)
        duw[:,sl]=gw.astype(BF); dua[:,sl]=ga.astype(BF); duv[:,sl]=gv.astype(BF)
        dfl[:,sl]=(dv*vm).astype(BF)
        dvec[:,sl]+=cat(rsum(gw),rsum(ga),rsum(gv),rsum(dkn*k0),rsum(dk*k0*(af-1.0)),g15,g16,g17)

def consts(C):
    gc=min(C,256)
    i=jnp.arange(BLK); tri=(i[:,None]>=i[None,:]).astype(BF); tru=(i[:,None]<=i[None,:]).astype(BF)
    j=jnp.arange(gc)//SD; ones=(j[:,None]==j[None,:]).astype(BF)
    return tri,tru,ones

VM=60*2**20
def params(): return pltpu.CompilerParams(vmem_limit_bytes=VM)

def recurrence_forward(ins,vec,meta,segrow):
    L,C=ins[0].shape; NB=L//BLK; gc=min(C,256); G=C//gc; H=C//SD
    tri,tru,ones=consts(C)
    rowb=pl.BlockSpec((BLK,C),lambda i:(i,0)); fix=lambda s: pl.BlockSpec(s,lambda i:(0,)*len(s))
    metab=pl.BlockSpec((BLK,meta.shape[1]),lambda i:(i,0)); segb=pl.BlockSpec((1,1,gc),lambda i:(i,0,0))
    sd=lambda dt: jax.ShapeDtypeStruct((L,C),dt)
    *six,ab=pl.pallas_call(first_kernel,grid=(NB,),
        in_specs=[rowb]*7+[fix((8,C)),metab,segb,fix((BLK,BLK)),fix((gc,gc))],
        out_specs=[rowb]*7,out_shape=[sd(BF)]*6+[sd(F32)],compiler_params=params())(*ins,vec,meta,segrow,tri,ones)
    at=ab.reshape(NB,BLK,H,SD).transpose(1,3,0,2).reshape(BLK,SD,NB*H)
    t=pl.pallas_call(solve_kernel,out_shape=jax.ShapeDtypeStruct(at.shape,F32),compiler_params=params())(at)
    tt=t.astype(BF).reshape(BLK,SD,NB,H).transpose(2,0,3,1).reshape(L,C)
    y,o,u,s=pl.pallas_call(forward_kernel,grid=(NB,),
        in_specs=[rowb]*7+[fix((8,C)),metab,segb,fix((BLK,BLK)),fix((gc,gc))],
        out_specs=[rowb]*3+[pl.BlockSpec((1,G,gc,gc),lambda i:(i,0,0,0))],
        out_shape=[sd(BF),sd(F32),sd(BF),jax.ShapeDtypeStruct((NB,G,gc,gc),BF)],
        scratch_shapes=[pltpu.VMEM((G,gc,gc),F32)],compiler_params=params())(*six,tt,vec,meta,segrow,tri,ones)
    return y,(o,*six,tt,u,s)

def recurrence_backward(dy,saved,ins,vec,meta,segrow):
    L,C=ins[0].shape; NB=L//BLK; gc=min(C,256); G=C//gc
    tri,tru,ones=consts(C)
    rev=lambda i: NB-1-i
    rowb=pl.BlockSpec((BLK,C),lambda i:(rev(i),0)); fix=lambda s: pl.BlockSpec(s,lambda i:(0,)*len(s))
    metab=pl.BlockSpec((BLK,meta.shape[1]),lambda i:(rev(i),0)); segb=pl.BlockSpec((1,1,gc),lambda i:(rev(i),0,0))
    sb=pl.BlockSpec((1,G,gc,gc),lambda i:(rev(i),0,0,0))
    return pl.pallas_call(backward_kernel,grid=(NB,),
        in_specs=[rowb]*10+[sb]+[rowb]*7+[fix((8,C)),metab,segb,fix((BLK,BLK)),fix((BLK,BLK)),fix((gc,gc))],
        out_specs=[rowb]*7+[fix((8,C))],
        out_shape=[jax.ShapeDtypeStruct((L,C),BF)]*7+[jax.ShapeDtypeStruct((8,C),F32)],
        scratch_shapes=[pltpu.VMEM((G,gc,gc),F32)],compiler_params=params())(dy,*saved,*ins,vec,meta,segrow,tri,tru,ones)


def mix_tile(x, vec, first_row, keep):
    cen = x - jnp.mean(x, axis=-1, keepdims=True)
    hat = cen * lax.rsqrt(jnp.mean(cen * cen, axis=-1, keepdims=True) + 1e-05)
    h = hat * vec[0:1] + vec[1:2]
    row = lax.broadcasted_iota(jnp.int32, h.shape, 0)
    shifted = jnp.where(row == 0, first_row, pltpu.roll(h, 1, 0))
    return hat, h, shifted * keep - h


def mix_forward_kernel(x, meta, vec, sq, low, up, *refs):
    xm, (rp, kp, vp, uw, ua, uv, ug, mid, midb, carry) = refs[:6], refs[6:]

    @pl.when(pl.program_id(0) == 0)
    def _():
        carry[...] = jnp.zeros_like(carry)

    _, h, delta = mix_tile(x[...].astype(F32), vec, carry[0:1], meta[:, 3:4])
    carry[0:1] = h[h.shape[0] - 1 :]
    m = []
    for i in range(6):
        m.append((h + delta * vec[4 + i : 5 + i]).astype(BF))
        xm[i][...] = m[i]
    rp[...] = mm(m[0], sq[0], NN)
    kp[...] = mm(m[2], sq[1], NN)
    vp[...] = mm(m[3], sq[2], NN)
    for out, i, lo, hi, act in ((uw, 1, 0, 128, jnp.tanh), (ua, 4, 128, 256, None), (uv, 3, 256, 384, None), (ug, 5, 384, 640, jax.nn.sigmoid)):
        d = mm(m[i], low[:, lo:hi], NN)
        if act is not None:
            d = act(d)
        b = d.astype(BF)
        mid[:, lo:hi] = d
        midb[:, lo:hi] = b
        out[...] = mm(b, up[:, lo:hi], NT)


def mix_backward_kernel(drp, dkp, dvp, duw, dua, duv, dug, x, above, meta, mid, vec, sq, low, up, dh, dd, gv, carry, hat_s):
    n, D = x.shape
    step = min(D, 512)

    @pl.when(pl.program_id(0) == 0)
    def _():
        carry[...] = jnp.zeros_like(carry)
        gv[...] = jnp.zeros_like(gv)

    def normalized(v):
        v = v.astype(F32)
        cen = v - jnp.mean(v, axis=-1, keepdims=True)
        return cen * lax.rsqrt(jnp.mean(cen * cen, axis=-1, keepdims=True) + 1e-05)

    hat_s[...] = normalized(x[...])
    prev = normalized(above[...])[above.shape[0] - 1 :]
    keep = meta[:, 3:4]
    dw = (mm(duw[...], up[:, 0:128], NN) * (1.0 - mid[:, 0:128] * mid[:, 0:128])).astype(BF)
    da = mm(dua[...], up[:, 128:256], NN).astype(BF)
    dv = mm(duv[...], up[:, 256:384], NN).astype(BF)
    s = mid[:, 384:640]
    dg = (mm(dug[...], up[:, 384:640], NN) * s * (1.0 - s)).astype(BF)
    dd[:, 0:128] = dw
    dd[:, 128:256] = da
    dd[:, 256:384] = dv
    dd[:, 384:640] = dg
    row = lax.broadcasted_iota(jnp.int32, (n, step), 0)
    for k in range(D // step):
        sl = slice(k * step, (k + 1) * step)
        gain, bias = vec[0:1, sl], vec[1:2, sl]
        hat = hat_s[:, sl]
        h = hat * gain + bias
        delta = jnp.where(row == 0, prev[:, sl] * gain + bias, pltpu.roll(h, 1, 0)) * keep - h
        total = ds = None
        for i in range(6):
            if i == 0:
                d = mm(drp[...], sq[0, sl], NT)
            elif i == 1:
                d = mm(dw, low[sl, 0:128], NT)
            elif i == 2:
                d = mm(dkp[...], sq[1, sl], NT)
            elif i == 3:
                d = mm(dvp[...], sq[2, sl], NT) + mm(dv, low[sl, 256:384], NT)
            elif i == 4:
                d = mm(da, low[sl, 128:256], NT)
            else:
                d = mm(dg, low[sl, 384:640], NT)
            gv[i : i + 1, sl] += jnp.sum(d * delta, axis=0, keepdims=True)
            scaled = d * vec[4 + i : 5 + i, sl]
            total = d if total is None else total + d
            ds = scaled if ds is None else ds + scaled
        back = ds * keep
        moved = jnp.where(row == n - 1, carry[0:1, sl], pltpu.roll(back, n - 1, 0))
        carry[0:1, sl] = back[0:1]
        g = total - ds + moved
        dh[:, sl] = g.astype(BF)
        gv[6:7, sl] += jnp.sum(g * hat, axis=0, keepdims=True)
        gv[7:8, sl] += jnp.sum(g, axis=0, keepdims=True)


def weight_kernel(x0, x1, x2, x3, x4, x5, drp, dkp, dvp, dd, duw, dua, duv, dug, mid, z, dt, sq, down, up, sq3):
    sq[0] = mm(x0[...], drp[...], TN).astype(BF)
    sq[1] = mm(x2[...], dkp[...], TN).astype(BF)
    sq[2] = mm(x3[...], dvp[...], TN).astype(BF)
    for x, lo, hi in ((x1, 0, 128), (x4, 128, 256), (x3, 256, 384), (x5, 384, 640)):
        down[:, lo:hi] = mm(x[...], dd[:, lo:hi], TN).astype(BF)
    sq3[...] = mm(z[...], dt[...], TN).astype(BF)

    @pl.when(pl.program_id(0) == 0)
    def _():
        for d, lo, hi in ((duw, 0, 128), (dua, 128, 256), (duv, 256, 384), (dug, 384, 640)):
            up[:, lo:hi] = mm(d[...], mid[:, lo:hi], TN).astype(BF)


def weight_grads(xm, grads, dd, mid, z, dt):
    L, D = xm[0].shape
    C, wide = z.shape[1], mid.shape[1]
    n = 256 if L <= 1024 else 128
    feat = pl.BlockSpec((L, n), lambda i: (0, i))
    fix = lambda m: pl.BlockSpec((L, m), lambda i: (0, 0))
    sd = jax.ShapeDtypeStruct
    return pl.pallas_call(
        weight_kernel,
        grid=(D // n,),
        in_specs=[feat] * 6 + [fix(C)] * 3 + [fix(wide)] + [fix(C)] * 4 + [fix(wide), fix(C), feat],
        out_specs=[
            pl.BlockSpec((3, n, C), lambda i: (0, i, 0)),
            pl.BlockSpec((n, wide), lambda i: (i, 0)),
            pl.BlockSpec((C, wide), lambda i: (0, 0)),
            pl.BlockSpec((C, n), lambda i: (0, i)),
        ],
        out_shape=[sd((3, D, C), BF), sd((D, wide), BF), sd((C, wide), BF), sd((C, D), BF)],
        compiler_params=params(),
    )(*xm, *grads[:3], dd, *grads[3:], mid, z, dt)


TILE = 128


def mix_forward(x, meta, vec, sq, low, up):
    L, D = x.shape
    C = up.shape[0]
    wide = low.shape[1]
    tok = lambda n: pl.BlockSpec((TILE, n), lambda i: (i, 0))
    fix = lambda s: pl.BlockSpec(s, lambda i: (0,) * len(s))
    sd = jax.ShapeDtypeStruct
    out = pl.pallas_call(
        mix_forward_kernel,
        grid=(L // TILE,),
        in_specs=[tok(D), tok(meta.shape[1]), fix(vec.shape), fix(sq.shape), fix(low.shape), fix(up.shape)],
        out_specs=[tok(D)] * 6 + [tok(C)] * 7 + [tok(wide)] * 2,
        out_shape=[sd((L, D), BF)] * 6 + [sd((L, C), F32)] * 7 + [sd((L, wide), F32), sd((L, wide), BF)],
        scratch_shapes=[pltpu.VMEM((8, D), F32)],
        compiler_params=params(),
    )(x, meta, vec, sq, low, up)
    return out[:6], out[6:13], out[13], out[14]


def mix_backward(grads, x, meta, mid, vec, sq, low, up):
    L, D = x.shape
    C = up.shape[0]
    wide = low.shape[1]
    n = L // TILE
    rev = lambda i: n - 1 - i
    tok = lambda m: pl.BlockSpec((TILE, m), lambda i: (rev(i), 0))
    fix = lambda s: pl.BlockSpec(s, lambda i: (0,) * len(s))
    above = pl.BlockSpec((16, D), lambda i: (jnp.maximum(rev(i) * (TILE // 16) - 1, 0), 0))
    sd = jax.ShapeDtypeStruct
    return pl.pallas_call(
        mix_backward_kernel,
        grid=(n,),
        in_specs=[tok(C)] * 7
        + [tok(D), above, tok(meta.shape[1]), tok(wide), fix(vec.shape), fix(sq.shape), fix(low.shape), fix(up.shape)],
        out_specs=[tok(D), tok(wide), fix((8, D))],
        out_shape=[sd((L, D), BF), sd((L, wide), BF), sd((8, D), F32)],
        scratch_shapes=[pltpu.VMEM((8, D), F32), pltpu.VMEM((TILE, D), F32)],
        compiler_params=params(),
    )(*grads, x, x, meta, mid, vec, sq, low, up)


AXES = ("sa", "sb", "ra", "rc")
PLANE = ("sb", "ra", "rc")
MESH = pl.DeviceIdType.MESH
HBM = pl.BlockSpec(memory_space=pl.ANY)


class Net:
    def __init__(self, local_sem, send_sem, recv_sem):
        self.sems = local_sem, send_sem, recv_sem
        self.size = tuple(lax.axis_size(k) for k in AXES)
        self.me = tuple(lax.axis_index(k) for k in AXES)
        self.locals, self.n, self.k = [], 0, 0

    def at(self, shift):
        return tuple(lax.rem(m + d, n) if d else m for m, d, n in zip(self.me, shift, self.size))

    def greet(self, shifts):
        bar = pltpu.get_barrier_semaphore()
        for s in shifts:
            pl.semaphore_signal(bar, inc=1, device_id=self.at(s), device_id_type=MESH)
        pl.semaphore_wait(bar, len(shifts))

    def keep(self, src, dst):
        copy = pltpu.make_async_copy(src, dst, self.sems[0].at[self.k])
        self.k += 1
        copy.start()
        self.locals.append(copy)

    def send(self, src, dst, shift):
        copy = pltpu.make_async_remote_copy(
            src, dst, self.sems[1].at[self.n], self.sems[2].at[self.n], device_id=self.at(shift), device_id_type=MESH
        )
        self.n += 1
        copy.start()
        return copy

    def settle(self):
        for copy in self.locals:
            copy.wait()


def call_net(body, arrays, out_shapes, cid, n_local, n_send, scratch=()):
    n = len(arrays)
    m = n + len(out_shapes)

    def kernel(*refs):
        body(refs[:n], refs[n:m], refs[m + 3 :], Net(*refs[m : m + 3]))

    return pl.pallas_call(
        kernel,
        out_shape=out_shapes,
        in_specs=[HBM] * n,
        out_specs=[HBM] * len(out_shapes),
        scratch_shapes=[
            pltpu.SemaphoreType.DMA((max(n_local, 1),)),
            pltpu.SemaphoreType.DMA((n_send,)),
            pltpu.SemaphoreType.DMA((n_send,)),
            *scratch,
        ],
        compiler_params=pltpu.CompilerParams(collective_id=cid, has_side_effects=True, vmem_limit_bytes=VM),
    )(*arrays)


def line_shifts():
    return [(d, 0, 0, 0) for d in range(1, lax.axis_size("sa"))]


def seq_shifts():
    A, B = lax.axis_size("sa"), lax.axis_size("sb")
    return [(i // B, i % B, 0, 0) for i in range(1, A * B)]


CHIPS = [(0, 1, 0, 0), (0, 0, 1, 0), (0, 1, 1, 0)]
OTHER_CORE = (0, 0, 0, 1)


def plane_gather_first(net, src, view):
    slot = net.me[1:]
    net.keep(src, view(*slot))
    far = [net.send(src, view(*slot), s) for s in CHIPS]
    return far, [net.send(src, view(*slot), OTHER_CORE)]


def plane_gather_second(net, view, far, near):
    for s, copy in zip(CHIPS, far):
        copy.wait_recv()
        slot = net.at(s)[1:]
        near.append(net.send(view(*slot), view(*slot), OTHER_CORE))


def plane_gather_end(far, near):
    for copy in far:
        copy.wait_send()
    for copy in near:
        copy.wait()


def line_exchange(arrays, cid):
    def body(ins, outs, _, net):
        shifts = line_shifts()
        net.greet(shifts)
        a = net.me[0]
        open_ = []
        for x, o in zip(ins, outs):
            open_ += [net.send(x.at[net.at(s)[0]], o.at[a], s) for s in shifts]
            net.keep(x.at[a], o.at[a])
        for copy in open_:
            copy.wait()
        net.settle()

    shapes = [jax.ShapeDtypeStruct(x.shape, x.dtype) for x in arrays]
    return call_net(body, arrays, shapes, cid, len(arrays), (lax.axis_size("sa") - 1) * len(arrays))


def swap_first(net, x, o):
    b = net.me[1]
    net.keep(x.at[b], o.at[b])
    return [net.send(x.at[net.at(CHIPS[0])[1]], o.at[b], CHIPS[0])]


def plane_gather(x, cid):
    def body(ins, outs, _, net):
        (x,), (o,) = ins, outs
        view = lambda i, j, k: o.at[i, j, k]
        net.greet(CHIPS + [OTHER_CORE])
        far, near = plane_gather_first(net, x, view)
        plane_gather_second(net, view, far, near)
        plane_gather_end(far, near)
        net.settle()

    sizes = tuple(lax.axis_size(k) for k in PLANE)
    return call_net(body, [x], [jax.ShapeDtypeStruct(sizes + x.shape, x.dtype)], cid, 1, 7)[0]


def plane_shifts():
    return [(0, i // 4, i // 2 % 2, i % 2) for i in range(1, 8)]


def start_exchange(tokens, first_sliced, out_grad, sq, low, up, key, cid):
    A, B = lax.axis_size("sa"), lax.axis_size("sb")
    S = A * B
    sizes = tuple(lax.axis_size(k) for k in PLANE)

    def body(ins, outs, scratch, net):
        x, f, g, q, lo, u, ke = ins
        xo, fo, go, qo, loo, uo, ko, q_line, lo_line = outs
        q_view = lambda i, j, k: qo.at[:, :, i, j, k]
        lo_view = lambda i, j, k: loo.at[:, i, j, k]
        u_view = lambda i, j, k: uo.at[i, j, k]
        g_view = lambda i, j, k: go.at[i, j, k]
        line, seq = line_shifts(), seq_shifts()
        net.greet(seq + [s for s in plane_shifts() if s != CHIPS[0]])
        a, b = net.me[:2]
        me = a * B + b
        first = []
        for s in line:
            first.append(net.send(q.at[net.at(s)[0]], q_line.at[:, a], s))
            first.append(net.send(lo, lo_line.at[a], s))
        net.keep(q.at[a], q_line.at[:, a])
        net.keep(lo, lo_line.at[a])
        rest = []
        for s in seq:
            rest.append(net.send(x.at[net.at(s)[1]], xo.at[me], s))
        for s in seq:
            to = net.at(s)
            rest.append(net.send(f.at[to[1], to[0]], fo.at[me], s))
        for copy in first:
            copy.wait()
        net.settle()
        net.locals = []
        net.keep(x.at[b], xo.at[me])
        net.keep(f.at[b, a], fo.at[me])
        q_open = plane_gather_first(net, q_line, q_view)
        lo_open = plane_gather_first(net, lo_line, lo_view)
        u_open = plane_gather_first(net, u, u_view)
        g_open = plane_gather_first(net, g, g_view)
        slot = net.me[1:]
        rest += [net.send(ke.at[net.at(s)[1:]], ko.at[slot], s) for s in plane_shifts()]
        net.keep(ke.at[slot], ko.at[slot])
        plane_gather_second(net, q_view, *q_open)
        plane_gather_second(net, lo_view, *lo_open)
        plane_gather_second(net, u_view, *u_open)
        plane_gather_second(net, g_view, *g_open)
        for o in (u_open, q_open, lo_open, g_open):
            plane_gather_end(*o)
        for copy in rest:
            copy.wait()
        net.settle()

    sd = lambda shape, like: jax.ShapeDtypeStruct(shape, like.dtype)
    shapes = [
        sd((S,) + tokens.shape[1:], tokens),
        sd((S,) + first_sliced.shape[2:], first_sliced),
        sd(sizes + out_grad.shape, out_grad),
        sd(sq.shape[1:2] + (A,) + sizes + sq.shape[2:], sq),
        sd((A,) + sizes + low.shape, low),
        sd(sizes + up.shape, up),
        sd(key.shape, key),
        sd(sq.shape[1:2] + (A,) + sq.shape[2:], sq),
        sd((A,) + low.shape, low),
    ]
    n_send = 2 * (A - 1) + 2 * (S - 1) + 5 * 7
    return call_net(body, [tokens, first_sliced, out_grad, sq, low, up, key], shapes, cid, 9, n_send)[:7]


def tail_exchange(dh, dfl, sq, down, wide, up, sq3, narrow, ffn, cid):
    A, B = lax.axis_size("sa"), lax.axis_size("sb")
    leads = [2, 1, 1, 0, 0, 0, 0]
    arrays = [sq, down, wide, up, sq3, narrow, ffn]
    blocks = [x.shape[:n] + x.shape[n + 3 :] for x, n in zip(arrays, leads)]
    n = len(arrays)

    def body(ins, outs, scratch, net):
        d, f, ps = ins[0], ins[1], ins[2:]
        do, fo, pos = outs[0], outs[1], outs[2:]
        own, other, chips = scratch[:n], scratch[n : 2 * n], scratch[2 * n :]
        seq = seq_shifts()
        net.greet(seq + CHIPS[1:] + [OTHER_CORE])
        a, b, y, c = net.me
        there = net.at(OTHER_CORE)[3]
        pairs = [(i // 2, i % 2) for i in range(4)]

        def block(t, i, j, k):
            return ps[t].at[(slice(None),) * leads[t] + (i, j, k)]

        cores, mine = [], []
        for t in range(n):
            cores.append([net.send(block(t, i, j, there), other[t].at[2 * i + j], OTHER_CORE) for i, j in pairs])
            for i, j in pairs:
                net.keep(block(t, i, j, c), own[t].at[2 * i + j])
            mine.append(net.locals)
            net.locals = []
        open_ = [net.send(d.at[net.at(s)[0]], do.at[a], s) for s in line_shifts()]
        net.keep(d.at[a], do.at[a])
        net.keep(f.at[a * B + b], fo.at[b, a])

        def add(t, k, terms):
            shape = blocks[t]
            step = min(shape[-2], 16)
            per = shape[-2] // step
            count = per
            for size in shape[:-2]:
                count = count * size

            @pl.loop(0, count)
            def _(r):
                index = []
                rest = r // per
                for size in reversed(shape[:-2]):
                    index.insert(0, rest % size)
                    rest = rest // size
                at = (*index, pl.ds(pl.multiple_of(r % per * step, step), step))
                total = own[t][(k, *at)].astype(F32)
                for ref, i in terms:
                    total = total + ref[(i, *at)].astype(F32)
                own[t][(k, *at)] = total.astype(BF)

        sent = []
        for t in range(n):
            for copy in cores[t] + mine[t]:
                copy.wait()
            for k, s in enumerate(CHIPS):
                to = net.at(s)
                slot = 2 * to[1] + to[2]
                add(t, slot, [(other[t], slot)])
                sent.append(net.send(own[t].at[slot], chips[t].at[k], s))
        for s in seq:
            to = net.at(s)
            open_.append(net.send(f.at[to[0] * B + to[1]], fo.at[b, a], s))
        me = 2 * b + y
        for t in range(n):
            for copy in sent[3 * t : 3 * t + 3]:
                copy.wait_recv()
            add(t, me, [(other[t], me)] + [(chips[t], k) for k in range(3)])
            net.keep(own[t].at[me], pos[t])
        for copy in sent:
            copy.wait_send()
        for copy in open_:
            copy.wait()
        net.settle()

    sd = jax.ShapeDtypeStruct
    shapes = [sd(dh.shape, dh.dtype), sd((B, A) + dfl.shape[1:], dfl.dtype)] + [sd(s, BF) for s in blocks]
    scratch = [pltpu.VMEM((m,) + s, BF) for m in (4, 4, 3) for s in blocks]
    n_send = (A - 1) + (A * B - 1) + 7 * n
    return call_net(body, [dh, dfl, *arrays], shapes, cid, 2 + 5 * n, n_send, scratch)


def last_exchange(swaps, sq, lines, cid):
    m = len(swaps)

    def body(ins, outs, _, net):
        net.greet(line_shifts() + [CHIPS[0]])
        a = net.me[0]
        open_ = []
        for i, (x, o) in enumerate(zip(ins, outs)):
            if i < m:
                open_ += swap_first(net, x, o)
                continue
            view = (lambda x, k: x.at[:, k]) if i == m else (lambda x, k: x.at[k])
            open_ += [net.send(view(x, net.at(s)[0]), o.at[a], s) for s in line_shifts()]
            net.keep(view(x, a), o.at[a])
        for copy in open_:
            copy.wait()
        net.settle()

    sd = jax.ShapeDtypeStruct
    arrays = [*swaps, sq, *lines]
    shapes = [sd(x.shape, x.dtype) for x in arrays]
    shapes[m] = sd((sq.shape[1], sq.shape[0]) + sq.shape[2:], sq.dtype)
    n_send = m + (1 + len(lines)) * (lax.axis_size("sa") - 1)
    return call_net(body, arrays, shapes, cid, len(arrays), n_send)


def layer_norm(x, gain, bias):
    cen = x - jnp.mean(x, axis=-1, keepdims=True)
    var = jnp.mean(cen * cen, axis=-1, keepdims=True)
    return cen * lax.rsqrt(var + 1e-05) * gain + bias


def next_line(value, steps):
    count = lax.axis_size("sa")
    first, last = max(0, -steps), min(count, count - steps)
    return lax.ppermute(value, "sa", [(i, i + steps) for i in range(first, last)])


def after(value, *others):
    return lax.optimization_barrier((value, *others))[0]


def per_device(tokens, first_values, lengths, vectors, down, up, square, key_w, value_w, out_grad):
    rows_here, seg, D = tokens.shape
    SA, SB, RA, RC = (lax.axis_size(k) for k in AXES)
    a, b = lax.axis_index("sa"), lax.axis_index("sb")
    S, F = SA * SB, SB * RA * RC
    L = seg * S
    C = D // SA
    NB = L // BLK
    gc = min(C, 256)
    T = SB * seg
    w = square.shape[1]
    n_low, n_vec = down.shape[1], vectors.shape[0]
    FS = key_w.shape[1] // (S * RA * RC)

    lens = lax.dynamic_index_in_dim(lengths, b, 0, keepdims=False)
    count = lens.shape[0]
    lower = jnp.arange(count)[:, None] > jnp.arange(count)[None, :]
    starts = jnp.sum(jnp.where(lower, lens[None, :], 0), axis=1)
    pos = jnp.arange(L, dtype=jnp.int32)
    reset = jnp.any(pos[:, None] == starts[None, :], axis=1).astype(F32)
    segid = jnp.sum((pos[:, None] >= starts[None, :]).astype(F32), axis=1) - 1.0
    blocks = segid.reshape(NB, BLK)
    before = blocks[:, :1] - reset.reshape(NB, BLK)[:, :1]
    carried = (blocks == before).astype(F32).reshape(L)
    live = (blocks == blocks[:, -1:]).astype(F32).reshape(L)
    meta = jnp.stack([segid, carried, live, 1.0 - reset], axis=1)
    segrow = jnp.tile(blocks.reshape(NB, 1, BLK), (1, 1, gc // SD))
    keep_row = (1.0 - reset)[:, None]
    keep_own = lax.dynamic_slice(keep_row, (a * T, 0), (T, 1))

    sq3 = lax.all_gather(square[3], AXES, axis=0, tiled=True)
    first_sliced = first_values.reshape(rows_here, seg, SA, C).transpose(0, 2, 1, 3)
    cuts = [0, DECAY_INNER, DECAY_INNER + LA, DECAY_INNER + LA + LV, n_low]

    def widen(m):
        pieces = [m[:, i:j] for i, j in zip(cuts[:-1], cuts[1:])]
        return jnp.concatenate([jnp.pad(p, ((0, 0), (0, -p.shape[1] % 128))) for p in pieces], axis=1)

    wide_at = [0, 128, 256, 384]
    low_mine = jnp.concatenate([widen(down), jnp.pad(vectors.T, ((0, 0), (0, 128 - n_vec)))], axis=1)
    sq_mine = square[:3].reshape(3, w, SA, C).transpose(2, 0, 1, 3)
    half = SA * FS
    key_mine = key_w.reshape(w, SA, F, FS).transpose(2, 0, 1, 3).reshape(SB, RA, RC, w, half)
    x_row, first_row, g_plane, sq, low, up_heads, key_line = start_exchange(
        tokens, first_sliced, out_grad, sq_mine, low_mine, widen(up.T), key_mine, 1
    )
    x_row = x_row.reshape(L, D)
    first_row = first_row.reshape(L, C)
    sq = sq.reshape(3, D, C)
    low = low.reshape(D, 768)
    low_w = low[:, :640]
    up_w = up_heads.reshape(C, 640)
    vec = low[:, 640 : 640 + n_vec].astype(F32).T
    vec_heads = lax.dynamic_slice(vec, (10, a * C), (8, C))
    FW = F * w
    halves = [slice(i * half, (i + 1) * half) for i in range(D // half)]
    kv = jnp.concatenate([key_line.reshape(FW, half), *(value_w[:, s] for s in halves)], axis=0)
    kv_all = lax.all_gather(kv, "sa", axis=0)
    key_all = kv_all[:, :FW].reshape(D, half)
    value_all = jnp.concatenate(
        [kv_all[:, FW + i * FS : FW + (i + 1) * FS].reshape(half, half) for i in range(D // half)], axis=1
    )
    g_all = g_plane.transpose(3, 1, 2, 0, 4, 5).reshape(F * T, D)
    slot = (b * RA + lax.axis_index("ra")) * RC + lax.axis_index("rc")
    g_own = lax.dynamic_slice(g_all, (slot * T, 0), (T, D)).astype(F32)

    xm, (rp, kp, vp, uw, ua, uv, ug), mid, mid_low = mix_forward(x_row, meta, vec, sq, low_w, up_w)
    ins = (rp, kp, vp, uw, ua, uv, first_row)
    y, saved = recurrence_forward(ins, vec_heads, meta, segrow)
    z = (y.astype(F32) * ug).astype(BF)
    (z_own,) = line_exchange([z.reshape(SA, T, C)], 2)
    z_own = z_own.transpose(1, 0, 2).reshape(T, D)

    x_own = lax.dynamic_slice(x_row, (a * T, 0), (T, D)).astype(F32)
    x1 = x_own + mm(z_own, sq3, NN)
    h2, norm2_pull = jax.vjp(layer_norm, x1, vec[2], vec[3])
    edge2 = next_line(h2[-1:], 1)

    def channel_mix(h, edge, mix):
        s = jnp.concatenate([edge, h[:-1]], axis=0) * keep_own
        return h + (s - h) * mix

    xc, cmix_pull = jax.vjp(channel_mix, h2, edge2, vec[18])
    xc_all = plane_gather(xc.astype(BF), 3).reshape(F * T, D)
    kc = jax.nn.relu(mm(xc_all, key_all, NN))
    q = (kc * kc).astype(BF)
    dkc = (mm(g_all, value_all, NT) * 2.0 * kc).astype(BF)
    dxc = lax.psum_scatter(mm(dkc, key_all, NT).astype(BF), PLANE, scatter_dimension=0, tiled=True)
    ffn_part = mm(q, value_all, NN).astype(BF)
    value_part = mm(q, g_all, TN).astype(BF).reshape(SA, FS, D)
    key_part = mm(xc_all, dkc, TN).astype(BF).reshape(SA, FW, half)
    kv_part = jnp.concatenate([key_part, *(value_part[:, :, s] for s in halves)], axis=1)
    dxc, kv_part, ffn_part = lax.optimization_barrier((dxc, kv_part, ffn_part))

    dh2, dedge2, g18 = cmix_pull(dxc.astype(F32))
    dh2 = dh2.at[-1:].add(next_line(dedge2, -1))
    dx1n, g2, g3 = norm2_pull(dh2)
    dx1 = g_own + dx1n
    dt = dx1.astype(BF)
    dz = mm(dt, sq3, NT).astype(BF)
    (dz_row,) = line_exchange([dz.reshape(T, SA, C).transpose(1, 0, 2)], 4)
    dt_row = lax.all_gather(dt, "sa", axis=0, tiled=True)
    kv_grad = lax.psum_scatter(after(kv_part, dz).reshape(-1, half), "sa", scatter_dimension=0, tiled=True)
    dz_row = dz_row.reshape(L, C).astype(F32)

    dy = (dz_row * ug).astype(BF)
    dug = (dz_row * y.astype(F32)).astype(BF)
    drp, dkp, dvp, duw, dua, duv, dfl, dvec = recurrence_backward(dy, saved, ins, vec_heads, meta, segrow)
    dh1, dd, gmix = mix_backward((drp, dkp, dvp, duw, dua, duv, dug), x_row, meta, mid, vec, sq, low_w, up_w)
    g0, g1 = gmix[6], gmix[7]

    sq_part, down_part, up_part, sq3_part = weight_grads(xm, (drp, dkp, dvp, duw, dua, duv, dug), dd, mid_low, z, dt_row)
    wide = jnp.stack([g0, g1, g2, g3, *(gmix[i] for i in range(6)), g18] + [jnp.zeros_like(g0)] * 5).astype(BF)
    wide = jnp.pad(wide.T, ((0, 0), (0, 112)))
    narrow = jnp.pad(dvec.astype(BF).T, ((0, 0), (0, 120)))
    plane = (SB, RA, RC, w)
    dh1_own, dfl_own, sq_sum, down_sum, wide_sum, up_sum, sq3_sum, narrow_sum, ffn = tail_exchange(
        dh1.reshape(SA, T, D),
        dfl.reshape(S, seg, C),
        sq_part.reshape((3, SA) + plane + (C,)),
        down_part.reshape((SA,) + plane + (640,)),
        wide.reshape((SA,) + plane + (128,)),
        up_part.reshape(plane + (640,)),
        sq3_part.reshape(plane + (D,)),
        narrow.reshape(plane + (128,)),
        ffn_part.reshape(SB, RA, RC, T, D),
        5,
    )
    dh1_own = jnp.sum(dh1_own.astype(F32), axis=0)
    _, norm1_pull = jax.vjp(lambda x: layer_norm(x, vec[0], vec[1]), x_own)
    (dx0,) = norm1_pull(dh1_own)
    mixed = (x1 + ffn.astype(F32)).astype(BF)
    tokens_grad, mixed_out, sq_sum, down_sum, wide_sum = last_exchange(
        [(dx1 + dx0).astype(BF).reshape(SB, seg, D), mixed.reshape(SB, seg, D)], sq_sum, [down_sum, wide_sum], 6
    )
    first_grad = dfl_own.transpose(0, 2, 1, 3).reshape(rows_here, seg, D)
    square_grad = jnp.concatenate([sq_sum.transpose(1, 2, 0, 3).reshape(3, w, D), sq3_sum[None]], axis=0).astype(F32)
    narrow_pieces = lambda m: [m[:, i : i + q - p] for i, p, q in zip(wide_at, cuts[:-1], cuts[1:])]
    down_grad = jnp.concatenate(narrow_pieces(jnp.sum(down_sum.astype(F32), axis=0)), axis=1)
    up_grad = jnp.concatenate(narrow_pieces(up_sum.astype(F32)), axis=1).T
    wide_t = jnp.sum(wide_sum.astype(F32), axis=0)[:, :16].T
    narrow_t = narrow_sum[:, :8].astype(F32).T
    vectors_gradient = jnp.concatenate([wide_t[:10], narrow_t, wide_t[10:11]], axis=0)
    value_grad = jnp.concatenate([kv_grad[FW + i * FS : FW + (i + 1) * FS] for i in range(D // half)], axis=1)
    value_grad = value_grad.astype(F32)
    key_grad = lax.all_to_all(kv_grad[:FW].reshape(F, w, half), PLANE, split_axis=0, concat_axis=0, tiled=True)
    key_grad = key_grad.reshape(F, w, SA, FS).transpose(1, 2, 0, 3).reshape(w, -1).astype(F32)
    return (
        mixed_out,
        tokens_grad,
        first_grad,
        vectors_gradient,
        down_grad,
        up_grad,
        square_grad,
        key_grad,
        value_grad,
    )


def solution(mesh):
    seq, row = mesh.shape["seq"], mesh.shape["row"]
    fine = Mesh(mesh.devices.reshape(seq // 2, 2, row // 2, 2), AXES)
    S, R = ("sa", "sb"), ("ra", "rc")
    in_specs = (
        P(R, S, None),
        P(R, S, None),
        P(R, None),
        P(None, S + R),
        P(S + R, None),
        P(None, S + R),
        P(None, S + R, None),
        P(S + R, None),
        P(S + R, None),
        P(R, S, None),
    )
    out_specs = (
        P(R, S, None),
        P(R, S, None),
        P(R, S, None),
        P(None, S + R),
        P(S + R, None),
        P(None, S + R),
        P(None, S + R, None),
        P(S + R, None),
        P(S + R, None),
    )
    return jax.shard_map(per_device, mesh=fine, in_specs=in_specs, out_specs=out_specs, check_vma=False)
```

```python
import functools

import jax
import jax.numpy as jnp
from jax import lax
from jax.experimental import pallas as pl
from jax.experimental.pallas import tpu as pltpu
from jax.sharding import Mesh, PartitionSpec as P

DECAY_INNER = 96
LA = 96
LV = 64

BF=jnp.bfloat16; F32=jnp.float32
SD=64; BLK=64
NN=(((1,),(0,)),((),())); NT=(((1,),(1,)),((),())); TN=(((0,),(0,)),((),()))

def mm(a,b,d): return lax.dot_general(a,b,d,preferred_element_type=F32)

class Geo:
    def __init__(s, gc):
        s.gc=gc; s.gh=gc//SD
        lane=lax.broadcasted_iota(jnp.int32,(1,gc),1)
        s.head=lane//SD
        s.lm=[(s.head==h).astype(BF) for h in range(s.gh)]
        row=lax.broadcasted_iota(jnp.int32,(BLK,gc),0)
        col=lax.broadcasted_iota(jnp.int32,(BLK,gc),1)%SD
        s.below=row>col; s.upto=row>=col
    def blk(s,x):
        return jnp.concatenate([x*m for m in s.lm],axis=0) if s.gh>1 else x
    def ext(s,x):
        out=x[:BLK]
        for h in range(1,s.gh):
            out=jnp.where(s.head==h,x[h*BLK:(h+1)*BLK],out)
        return out

def headsums(ones, *xs):
    hi = [x.astype(BF) for x in xs]
    lo = [(x - h.astype(F32)).astype(BF) for x, h in zip(xs, hi)]
    s = mm(jnp.concatenate(hi + lo, axis=0), ones, NN)
    n = len(xs) * BLK
    return [s[i * BLK : (i + 1) * BLK] + s[n + i * BLK : n + (i + 1) * BLK] for i in range(len(xs))]

def decayed(geo,ws,tri):
    w=ws.astype(F32)
    cum=mm(tri,ws,NN)
    return w,cum,jnp.exp(cum-w),jnp.exp(cum),jnp.exp(-cum)

def first_block(rp,kp,vp,uw,ua,uv,fl,vec,meta,segrow,tri,ones,rs,ws,ks,vs,qs,as_,ri_out,ab):
    C=rp.shape[1]; gc=min(C,256); geo=Geo(gc)
    same=meta[:,0:1]==segrow[0]
    strict=geo.below&same
    for g in range(C//gc):
        sl=slice(g*gc,(g+1)*gc)
        V=lambda i: vec[i:i+1,sl]
        k0=kp[:,sl]; v0=vp[:,sl]
        lw=-0.606531*jax.nn.sigmoid(V(0)+uw[:,sl])
        al=jax.nn.sigmoid(V(1)+ua[:,sl])
        vm=jax.nn.sigmoid(V(2)+uv[:,sl])
        v=v0+(fl[:,sl].astype(F32)-v0)*vm
        kn=k0*V(3)
        ri=lax.rsqrt(headsums(ones[...],kn*kn)[0]+1e-6)
        ri_out[:,sl]=ri
        kk=kn*ri
        km=k0*(1.0+(al-1.0)*V(4))
        q_=kk.astype(BF); w_=lw.astype(BF); a_=al.astype(BF)
        rs[:,sl]=rp[:,sl].astype(BF); ws[:,sl]=w_; ks[:,sl]=km.astype(BF)
        vs[:,sl]=v.astype(BF); qs[:,sl]=q_; as_[:,sl]=a_
        w,cum,eP,eC,eN=decayed(geo,w_,tri[...])
        q=q_.astype(F32)
        qu=(q*eP).astype(BF); bb=(q*a_.astype(F32)*eN).astype(BF)
        put128(ab,g,jnp.where(strict,mm(qu,geo.blk(bb),NT),0.0))

def put128(ref, g, x):
    if x.shape[1] < 128:
        x = jnp.concatenate([x, jnp.zeros_like(x)], axis=1)
    n = x.shape[1] // 128
    for k in range(n):
        ref[g * n + k] = x[:, k * 128 : (k + 1) * 128]


def get128(ref, g, gc):
    n = max(gc // 128, 1)
    x = jnp.concatenate([ref[g * n + k] for k in range(n)], axis=1) if n > 1 else ref[g]
    return x[:, :gc].astype(BF)


def solve_kernel(ab, tt, a, t):
    G, L, _ = ab.shape
    NB = L // BLK
    B = NB * G * 2

    @pl.loop(0, BLK, unroll=8)
    def _(i):
        rows = [ab[g, pl.ds(i, NB, stride=BLK), :] for g in range(G)]
        a[i] = jnp.concatenate([r[:, k * SD : (k + 1) * SD] for r in rows for k in range(2)], axis=0).T

    t[...] = jnp.zeros_like(t)
    cidx = lax.broadcasted_iota(jnp.int32, (SD, B), 0)

    @pl.loop(0, BLK)
    def _(i):
        def inner(jb, acc):
            for jj in range(8):
                j = jb * 8 + jj
                acc = acc - a[i, pl.ds(j, 1), :] * t[j]
            return acc

        t[i] = lax.fori_loop(0, i // 8 + 1, inner, (cidx == i).astype(F32))

    @pl.loop(0, BLK, unroll=8)
    def _(i):
        rows = t[i].T
        for g in range(G):
            pair = [rows[(2 * g + k) * NB : (2 * g + k + 1) * NB] for k in range(2)]
            tt[g, pl.ds(i, NB, stride=BLK), :] = jnp.concatenate(pair, axis=1)


def forward_block(rs,ws,ks,vs,qs,as_,tt,vec,meta,segrow,tri,ones,y,nrm_out,rstd_out,extra_out,u_out,al_out,lb_out,s_out,state):
    C=rs.shape[1]; gc=min(C,256); geo=Geo(gc)
    same=meta[:,0:1]==segrow[0]
    carried=meta[:,1:2]; live=meta[:,2:3]; last=meta[BLK-1:BLK,1:2]
    strict=geo.below&same; incl=geo.upto&same
    for g in range(C//gc):
        sl=slice(g*gc,(g+1)*gc)
        V=lambda i: vec[i:i+1,sl]
        w,cum,eP,eC,eN=decayed(geo,ws[:,sl],tri[...])
        q=qs[:,sl].astype(F32); r=rs[:,sl].astype(F32); k=ks[:,sl].astype(F32)
        vb=vs[:,sl]; v=vb.astype(F32); a=as_[:,sl].astype(F32)
        qq=jnp.concatenate([(q*eP).astype(BF),(r*eC).astype(BF)],axis=0)
        kb=(k*eN).astype(BF); bb=(q*a*eN).astype(BF)
        mk=mm(qq,geo.blk(kb),NT)
        al=jnp.concatenate([jnp.where(strict,mk[:BLK],0.0).astype(BF),jnp.where(incl,mk[BLK:],0.0).astype(BF)],axis=0)
        lb=jnp.where(incl,mm(qq[BLK:],geo.blk(bb),NT),0.0).astype(BF)
        s0=state[g]; sb=s0.astype(BF)
        s_out[0,g]=sb
        qst=mm(qq,sb,NT)
        av=mm(al,geo.blk(vb),NN)
        rhs=carried*qst[:BLK]+av[:BLK]
        u=mm(get128(tt,g,gc),geo.blk(rhs.astype(BF)),NN)
        ub=u.astype(BF)
        u_out[:,sl]=ub
        o=carried*qst[BLK:]+av[BLK:]-mm(lb,geo.blk(ub),NN)
        vu=jnp.concatenate([(v*live).astype(BF),(u*(-live)).astype(BF)],axis=0)
        ds=mm(vu,jnp.concatenate([kb,bb],axis=0),TN)
        tail=eC[BLK-1:BLK]
        state[g]=(last*s0+ds*ones[...].astype(F32))*tail
        al_out[:,sl]=al; lb_out[:,sl]=lb
        mean,extra=headsums(ones[...],o,r*k*V(5))
        cen=o-mean*(1.0/SD)
        rstd=lax.rsqrt(headsums(ones[...],cen*cen)[0]*(1.0/SD)+1.0)
        nrm=cen*rstd
        nrm_out[:,sl]=nrm; rstd_out[:,sl]=rstd; extra_out[:,sl]=extra
        y[:,sl]=(nrm*V(6)+V(7)+extra*v).astype(BF)

def backward_block(dy,nrm_in,rstd_in,extra_in,rs,ws,ks,vs,qs,as_,tt,u_in,al_in,lb_in,s_in,ri_in,rp,kp,vp,uw,ua,uv,fl,vec,meta,segrow,tri,tru,ones,
                    drp,dkp,dvp,duw,dua,duv,dfl,dvec,state):
    C=rs.shape[1]; gc=min(C,256); geo=Geo(gc)
    same=meta[:,0:1]==segrow[0]
    carried=meta[:,1:2]; live=meta[:,2:3]; last=meta[BLK-1:BLK,1:2]
    strict=geo.below&same; incl=geo.upto&same
    cat=lambda *x: jnp.concatenate(x,axis=0)
    rsum=lambda x: jnp.sum(x,axis=0,keepdims=True)
    for g in range(C//gc):
        sl=slice(g*gc,(g+1)*gc)
        V=lambda i: vec[i:i+1,sl]
        on=ones[...]
        w,cum,eP,eC,eN=decayed(geo,ws[:,sl],tri[...])
        q=qs[:,sl].astype(F32); r=rs[:,sl].astype(F32); k=ks[:,sl].astype(F32)
        vb=vs[:,sl]; v=vb.astype(F32); a=as_[:,sl].astype(F32)
        d=dy[:,sl].astype(F32); nrm=nrm_in[:,sl]; extra=extra_in[:,sl]
        dn=d*V(6)
        de,dn1,dn2=headsums(on,d*v,dn,dn*nrm)
        do=rstd_in[:,sl]*(dn-dn1*(1.0/SD)-nrm*(dn2*(1.0/SD)))
        g17=rsum(d); g16=rsum(d*nrm); g15=rsum(de*r*k)
        dr=de*k*V(5); dk=de*r*V(5); dv=d*extra
        qq=cat((q*eP).astype(BF),(r*eC).astype(BF))
        kb=(k*eN).astype(BF); bb=(q*a*eN).astype(BF)
        kblk=geo.blk(kb); bblk=geo.blk(bb)
        al=al_in[:,sl]; lb=lb_in[:,sl]
        ub=u_in[:,sl]; s0=s_in[0,g]
        tail=eC[BLK-1:BLK]
        ds1=state[g]*tail; dsb=ds1.astype(BF)
        kbs=mm(cat(kb,bb),dsb,NT)
        dob=do.astype(BF)
        du=-geo.ext(mm(lb,dob,TN))-live*kbs[BLK:]
        yy=geo.ext(mm(get128(tt,g,gc),du.astype(BF),TN))
        yo=cat(yy.astype(BF),dob)
        cyo=cat((carried*yy).astype(BF),(carried*do).astype(BF))
        mv=mm(yo,geo.blk(vb),NT); mu=mm(yo,geo.blk(ub),NT)
        dkm=cat(jnp.where(strict,mv[:BLK],0.0).astype(BF),jnp.where(incl,mv[BLK:],0.0).astype(BF))
        dbm=cat(jnp.where(strict,-mu[:BLK],0.0).astype(BF),jnp.where(incl,-mu[BLK:],0.0).astype(BF))
        dqq=mm(cyo,s0,NN)+mm(dkm,kblk,NN)+mm(dbm,bblk,NN)
        vus=mm(cat(vb,ub),dsb,NN)
        kst=live*vus[:BLK]; bst=-(live*vus[BLK:])
        dkb=geo.ext(mm(dkm,qq,TN))+kst
        dbb=geo.ext(mm(dbm,qq,TN))+bst
        dv=dv+geo.ext(mm(al,yo,TN))+live*kbs[:BLK]
        kf=kb.astype(F32); bf=bb.astype(F32); qf=qq.astype(F32)
        dlast=last*rsum(ds1*s0.astype(F32))+rsum(kf*kst+bf*bst)
        state[g]=mm(cyo,qq,TN)*on.astype(F32)+last*ds1
        dqu=dqq[:BLK]*qf[:BLK]
        dcum=dqu+dqq[BLK:]*qf[BLK:]-dkb*kf-dbb*bf
        hi=dcum.astype(BF); rest=dcum-hi.astype(F32); lo=rest.astype(BF)
        lo2=(rest-lo.astype(F32)).astype(BF)
        dw=mm(tru[...],hi,NN)+mm(tru[...],lo,NN)+mm(tru[...],lo2,NN)+dlast-dqu
        dben=dbb*eN
        dq=dqq[:BLK]*eP+dben*a
        da=dben*q
        dr=dr+dqq[BLK:]*eC
        dk=dk+dkb*eN
        k0=kp[:,sl]; v0=vp[:,sl]
        sg=jax.nn.sigmoid(V(0)+uw[:,sl]); af=jax.nn.sigmoid(V(1)+ua[:,sl]); vm=jax.nn.sigmoid(V(2)+uv[:,sl])
        kn=k0*V(3)
        ri=ri_in[:,sl]
        kk=kn*ri
        gw=(-0.606531)*dw*sg*(1.0-sg)
        gv=dv*(fl[:,sl].astype(F32)-v0)*vm*(1.0-vm)
        da=da+dk*k0*V(4)
        ga=da*af*(1.0-af)
        dkn=ri*(dq-kk*headsums(on,dq*kk)[0])
        drp[:,sl]=dr.astype(BF)
        dkp[:,sl]=(dk*(1.0+(af-1.0)*V(4))+dkn*V(3)).astype(BF)
        dvp[:,sl]=(dv*(1.0-vm)).astype(BF)
        duw[:,sl]=gw.astype(BF); dua[:,sl]=ga.astype(BF); duv[:,sl]=gv.astype(BF)
        dfl[:,sl]=(dv*vm).astype(BF)
        dvec[:,sl]+=cat(rsum(gw),rsum(ga),rsum(gv),rsum(dkn*k0),rsum(dk*k0*(af-1.0)),g15,g16,g17)

def per_block(ref, kind, i):
    if kind is None:
        return ref
    size = {"n": 1, "pair": 2 * BLK}.get(kind, BLK)
    at = pl.ds(i * size, size)
    return ref.at[:, at] if kind == "inv" else ref.at[at]


def blocks_kernel(body, kinds, order, zeroed, *refs):
    @pl.when(pl.program_id(0) == 0)
    def _():
        for i in zeroed:
            refs[i][...] = jnp.zeros_like(refs[i])

    for i in order:
        body(*(per_block(r, k, i) for r, k in zip(refs, kinds)))


def consts(C):
    gc=min(C,256)
    i=jnp.arange(BLK); tri=(i[:,None]>=i[None,:]).astype(BF); tru=(i[:,None]<=i[None,:]).astype(BF)
    j=jnp.arange(gc)//SD; ones=(j[:,None]==j[None,:]).astype(BF)
    return tri,tru,ones

VM=60*2**20
def takes(us): return pl.CostEstimate(flops=int(us*6e8), bytes_accessed=1<<20, transcendentals=0)
UNROLL=2
def params(): return pltpu.CompilerParams(vmem_limit_bytes=VM)

def recurrence_forward(ins, vec, meta, segrow):
    L, C = ins[0].shape
    NB, gc = L // BLK, min(C, 256)
    G = C // gc
    tri, tru, ones = consts(C)
    inv = jax.ShapeDtypeStruct((-(-C // 128), L, 128), F32)
    n = UNROLL
    rowb = pl.BlockSpec((n * BLK, C), lambda i: (i, 0))
    fix = lambda s: pl.BlockSpec(s, lambda i: (0,) * len(s))
    metab = pl.BlockSpec((n * BLK, meta.shape[1]), lambda i: (i, 0))
    segb = pl.BlockSpec((n, 1, gc), lambda i: (i, 0, 0))
    invb = pl.BlockSpec((inv.shape[0], n * BLK, 128), lambda i: (0, i, 0))
    sd = lambda dt: jax.ShapeDtypeStruct((L, C), dt)
    tail = [fix((8, C)), metab, segb, fix((BLK, BLK)), fix((gc, gc))]
    tail_kinds = [None, "row", "n", None, None]
    *six, ri, ab = pl.pallas_call(
        functools.partial(blocks_kernel, first_block, ["row"] * 7 + tail_kinds + ["row"] * 7 + ["inv"], range(n), ()),
        grid=(NB // n,),
        in_specs=[rowb] * 7 + tail,
        out_specs=[rowb] * 7 + [invb],
        out_shape=[sd(BF)] * 6 + [sd(F32), inv],
        compiler_params=params(),
    )(*ins, vec, meta, segrow, tri, ones)
    lanes = inv.shape[0] * 2 * NB
    tt = pl.pallas_call(
        solve_kernel, out_shape=inv, scratch_shapes=[pltpu.VMEM((BLK, SD, lanes), F32)] * 2, compiler_params=params()
    )(ab)
    kinds = ["row"] * 6 + ["inv"] + tail_kinds + ["row"] * 5 + ["pair", "row", "n", None]
    pairb = pl.BlockSpec((2 * n * BLK, C), lambda i: (i, 0))
    y, nrm, rstd, extra, u, al, lb, s = pl.pallas_call(
        functools.partial(blocks_kernel, forward_block, kinds, range(n), (len(kinds) - 1,)),
        grid=(NB // n,),
        in_specs=[rowb] * 6 + [invb] + tail,
        out_specs=[rowb] * 5 + [pairb, rowb, pl.BlockSpec((n, G, gc, gc), lambda i: (i, 0, 0, 0))],
        out_shape=[sd(BF)] + [sd(F32)] * 3 + [sd(BF), jax.ShapeDtypeStruct((2 * L, C), BF), sd(BF), jax.ShapeDtypeStruct((NB, G, gc, gc), BF)],
        scratch_shapes=[pltpu.VMEM((G, gc, gc), F32)],
        compiler_params=params(),
    )(*six, tt, vec, meta, segrow, tri, ones)
    return y, (nrm, rstd, extra, *six, tt, u, al, lb, s, ri)


def recurrence_backward(dy, saved, ins, vec, meta, segrow):
    L, C = ins[0].shape
    NB, gc = L // BLK, min(C, 256)
    G = C // gc
    tri, tru, ones = consts(C)
    n = UNROLL
    rev = lambda i: NB // n - 1 - i
    rowb = pl.BlockSpec((n * BLK, C), lambda i: (rev(i), 0))
    fix = lambda s: pl.BlockSpec(s, lambda i: (0,) * len(s))
    metab = pl.BlockSpec((n * BLK, meta.shape[1]), lambda i: (rev(i), 0))
    segb = pl.BlockSpec((n, 1, gc), lambda i: (rev(i), 0, 0))
    sb = pl.BlockSpec((n, G, gc, gc), lambda i: (rev(i), 0, 0, 0))
    invb = pl.BlockSpec((-(-C // 128), n * BLK, 128), lambda i: (0, rev(i), 0))
    kinds = ["row"] * 10 + ["inv", "row", "pair", "row", "n"] + ["row"] * 8 + [None, "row", "n", None, None, None] + ["row"] * 7 + [None] * 2
    last = len(kinds) - 1
    return pl.pallas_call(
        functools.partial(blocks_kernel, backward_block, kinds, range(n - 1, -1, -1), (last - 1, last)),
        grid=(NB // n,),
        in_specs=[rowb] * 10
        + [invb, rowb, pl.BlockSpec((2 * n * BLK, C), lambda i: (rev(i), 0)), rowb, sb]
        + [rowb] * 8
        + [fix((8, C)), metab, segb, fix((BLK, BLK)), fix((BLK, BLK)), fix((gc, gc))],
        out_specs=[rowb] * 7 + [fix((8, C))],
        out_shape=[jax.ShapeDtypeStruct((L, C), BF)] * 7 + [jax.ShapeDtypeStruct((8, C), F32)],
        scratch_shapes=[pltpu.VMEM((G, gc, gc), F32)],
        compiler_params=params(),
    )(dy, *saved, *ins, vec, meta, segrow, tri, tru, ones)


def mix_tile(x, vec, first_row, keep):
    cen = x - jnp.mean(x, axis=-1, keepdims=True)
    hat = cen * lax.rsqrt(jnp.mean(cen * cen, axis=-1, keepdims=True) + 1e-05)
    h = hat * vec[0:1] + vec[1:2]
    row = lax.broadcasted_iota(jnp.int32, h.shape, 0)
    shifted = jnp.where(row == 0, first_row, pltpu.roll(h, 1, 0))
    return hat, h, shifted * keep - h


def mix_forward_kernel(x, meta, vec, sq, low, up, *refs):
    xm, (rp, kp, vp, uw, ua, uv, ug, mid, midb, carry) = refs[:6], refs[6:]

    @pl.when(pl.program_id(0) == 0)
    def _():
        carry[...] = jnp.zeros_like(carry)

    _, h, delta = mix_tile(x[...].astype(F32), vec, carry[0:1], meta[:, 3:4])
    carry[0:1] = h[h.shape[0] - 1 :]
    m = []
    for i in range(6):
        m.append((h + delta * vec[4 + i : 5 + i]).astype(BF))
        xm[i][...] = m[i]
    rp[...] = mm(m[0], sq[0], NN)
    kp[...] = mm(m[2], sq[1], NN)
    vp[...] = mm(m[3], sq[2], NN)
    for out, i, lo, hi, act in ((uw, 1, 0, 128, jnp.tanh), (ua, 4, 128, 256, None), (uv, 3, 256, 384, None), (ug, 5, 384, 640, jax.nn.sigmoid)):
        d = mm(m[i], low[:, lo:hi], NN)
        if act is not None:
            d = act(d)
        b = d.astype(BF)
        mid[:, lo:hi] = d
        midb[:, lo:hi] = b
        out[...] = mm(b, up[:, lo:hi], NT)


def mix_backward_kernel(drp, dkp, dvp, duw, dua, duv, dug, x, above, meta, mid, vec, sq, low, up, dh, dd, gv, carry, hat_s):
    n, D = x.shape
    step = min(D, 512)

    @pl.when(pl.program_id(0) == 0)
    def _():
        carry[...] = jnp.zeros_like(carry)
        gv[...] = jnp.zeros_like(gv)

    def normalized(v):
        v = v.astype(F32)
        cen = v - jnp.mean(v, axis=-1, keepdims=True)
        return cen * lax.rsqrt(jnp.mean(cen * cen, axis=-1, keepdims=True) + 1e-05)

    hat_s[...] = normalized(x[...])
    prev = normalized(above[...])[above.shape[0] - 1 :]
    keep = meta[:, 3:4]
    dw = (mm(duw[...], up[:, 0:128], NN) * (1.0 - mid[:, 0:128] * mid[:, 0:128])).astype(BF)
    da = mm(dua[...], up[:, 128:256], NN).astype(BF)
    dv = mm(duv[...], up[:, 256:384], NN).astype(BF)
    s = mid[:, 384:640]
    dg = (mm(dug[...], up[:, 384:640], NN) * s * (1.0 - s)).astype(BF)
    dd[:, 0:128] = dw
    dd[:, 128:256] = da
    dd[:, 256:384] = dv
    dd[:, 384:640] = dg
    row = lax.broadcasted_iota(jnp.int32, (n, step), 0)
    for k in range(D // step):
        sl = slice(k * step, (k + 1) * step)
        gain, bias = vec[0:1, sl], vec[1:2, sl]
        hat = hat_s[:, sl]
        h = hat * gain + bias
        delta = jnp.where(row == 0, prev[:, sl] * gain + bias, pltpu.roll(h, 1, 0)) * keep - h
        total = ds = None
        for i in range(6):
            if i == 0:
                d = mm(drp[...], sq[0, sl], NT)
            elif i == 1:
                d = mm(dw, low[sl, 0:128], NT)
            elif i == 2:
                d = mm(dkp[...], sq[1, sl], NT)
            elif i == 3:
                d = mm(dvp[...], sq[2, sl], NT) + mm(dv, low[sl, 256:384], NT)
            elif i == 4:
                d = mm(da, low[sl, 128:256], NT)
            else:
                d = mm(dg, low[sl, 384:640], NT)
            gv[i : i + 1, sl] += jnp.sum(d * delta, axis=0, keepdims=True)
            scaled = d * vec[4 + i : 5 + i, sl]
            total = d if total is None else total + d
            ds = scaled if ds is None else ds + scaled
        back = ds * keep
        moved = jnp.where(row == n - 1, carry[0:1, sl], pltpu.roll(back, n - 1, 0))
        carry[0:1, sl] = back[0:1]
        g = total - ds + moved
        dh[:, sl] = g.astype(BF)
        gv[6:7, sl] += jnp.sum(g * hat, axis=0, keepdims=True)
        gv[7:8, sl] += jnp.sum(g, axis=0, keepdims=True)


def weight_kernel(x0, x1, x2, x3, x4, x5, drp, dkp, dvp, dd, duw, dua, duv, dug, mid, z, dt, sq, down, up, sq3):
    sq[0] = mm(x0[...], drp[...], TN).astype(BF)
    sq[1] = mm(x2[...], dkp[...], TN).astype(BF)
    sq[2] = mm(x3[...], dvp[...], TN).astype(BF)
    for x, lo, hi in ((x1, 0, 128), (x4, 128, 256), (x3, 256, 384), (x5, 384, 640)):
        down[:, lo:hi] = mm(x[...], dd[:, lo:hi], TN).astype(BF)
    sq3[...] = mm(z[...], dt[...], TN).astype(BF)

    @pl.when(pl.program_id(0) == 0)
    def _():
        for d, lo, hi in ((duw, 0, 128), (dua, 128, 256), (duv, 256, 384), (dug, 384, 640)):
            up[:, lo:hi] = mm(d[...], mid[:, lo:hi], TN).astype(BF)


def weight_grads(xm, grads, dd, mid, z, dt):
    L, D = xm[0].shape
    C, wide = grads[0].shape[1], mid.shape[1]
    n = 256 if L <= 1024 else 128
    tok, own = z.shape
    feat = pl.BlockSpec((L, n), lambda i: (0, i))
    fix = lambda m: pl.BlockSpec((L, m), lambda i: (0, 0))
    sd = jax.ShapeDtypeStruct
    return pl.pallas_call(
        weight_kernel,
        grid=(D // n,),
        in_specs=[feat] * 6 + [fix(C)] * 3 + [fix(wide)] + [fix(C)] * 4 + [fix(wide), pl.BlockSpec((tok, own), lambda i: (0, 0)), pl.BlockSpec((tok, n), lambda i: (0, i))],
        out_specs=[
            pl.BlockSpec((3, n, C), lambda i: (0, i, 0)),
            pl.BlockSpec((n, wide), lambda i: (i, 0)),
            pl.BlockSpec((C, wide), lambda i: (0, 0)),
            pl.BlockSpec((own, n), lambda i: (0, i)),
        ],
        out_shape=[sd((3, D, C), BF), sd((D, wide), BF), sd((C, wide), BF), sd((own, D), BF)],
        cost_estimate=takes(26),
        compiler_params=params(),
    )(*xm, *grads[:3], dd, *grads[3:], mid, z, dt)


TILE = 128


def mix_forward(x, meta, vec, sq, low, up):
    L, D = x.shape
    C = up.shape[0]
    wide = up.shape[1]
    tok = lambda n: pl.BlockSpec((TILE, n), lambda i: (i, 0))
    fix = lambda s: pl.BlockSpec(s, lambda i: (0,) * len(s))
    sd = jax.ShapeDtypeStruct
    out = pl.pallas_call(
        mix_forward_kernel,
        grid=(L // TILE,),
        in_specs=[tok(D), tok(meta.shape[1]), fix(vec.shape), fix(sq.shape), fix((D, wide)), fix(up.shape)],
        out_specs=[tok(D)] * 6 + [tok(C)] * 7 + [tok(wide)] * 2,
        out_shape=[sd((L, D), BF)] * 6 + [sd((L, C), F32)] * 7 + [sd((L, wide), F32), sd((L, wide), BF)],
        scratch_shapes=[pltpu.VMEM((8, D), F32)],
        cost_estimate=takes(30),
        compiler_params=params(),
    )(x, meta, vec, sq, low, up)
    return out[:6], out[6:13], out[13], out[14]


def mix_backward(grads, x, meta, mid, vec, sq, low, up):
    L, D = x.shape
    C = up.shape[0]
    wide = up.shape[1]
    n = L // TILE
    rev = lambda i: n - 1 - i
    tok = lambda m: pl.BlockSpec((TILE, m), lambda i: (rev(i), 0))
    fix = lambda s: pl.BlockSpec(s, lambda i: (0,) * len(s))
    above = pl.BlockSpec((16, D), lambda i: (jnp.maximum(rev(i) * (TILE // 16) - 1, 0), 0))
    sd = jax.ShapeDtypeStruct
    return pl.pallas_call(
        mix_backward_kernel,
        grid=(n,),
        in_specs=[tok(C)] * 7
        + [tok(D), above, tok(meta.shape[1]), tok(wide), fix(vec.shape), fix(sq.shape), fix((D, wide)), fix(up.shape)],
        out_specs=[tok(D), tok(wide), fix((8, D))],
        out_shape=[sd((L, D), BF), sd((L, wide), BF), sd((8, D), F32)],
        scratch_shapes=[pltpu.VMEM((8, D), F32), pltpu.VMEM((TILE, D), F32)],
        cost_estimate=takes(35),
        compiler_params=params(),
    )(*grads, x, x, meta, mid, vec, sq, low, up)


AXES = ("sa", "sb", "ra", "rc")
PLANE = ("sb", "ra", "rc")
MESH = pl.DeviceIdType.MESH
HBM = pl.BlockSpec(memory_space=pl.ANY)


class Net:
    def __init__(self, local_sem, send_sem, recv_sem):
        self.sems = local_sem, send_sem, recv_sem
        self.size = tuple(lax.axis_size(k) for k in AXES)
        self.me = tuple(lax.axis_index(k) for k in AXES)
        self.locals, self.n, self.k = [], 0, 0

    def at(self, shift):
        return tuple(lax.rem(m + d, n) if d else m for m, d, n in zip(self.me, shift, self.size))

    def greet(self, shifts):
        bar = pltpu.get_barrier_semaphore()
        for s in shifts:
            pl.semaphore_signal(bar, inc=1, device_id=self.at(s), device_id_type=MESH)
        pl.semaphore_wait(bar, len(shifts))

    def keep(self, src, dst):
        copy = pltpu.make_async_copy(src, dst, self.sems[0].at[self.k])
        self.k += 1
        copy.start()
        self.locals.append(copy)

    def send(self, src, dst, shift):
        copy = pltpu.make_async_remote_copy(
            src, dst, self.sems[1].at[self.n], self.sems[2].at[self.n], device_id=self.at(shift), device_id_type=MESH
        )
        self.n += 1
        copy.start()
        return copy

    def settle(self):
        for copy in self.locals:
            copy.wait()


def call_net(body, arrays, out_shapes, cid, n_local, n_send, scratch=()):
    n = len(arrays)
    m = n + len(out_shapes)

    def kernel(*refs):
        body(refs[:n], refs[n:m], refs[m + 3 :], Net(*refs[m : m + 3]))

    return pl.pallas_call(
        kernel,
        out_shape=out_shapes,
        in_specs=[HBM] * n,
        out_specs=[HBM] * len(out_shapes),
        scratch_shapes=[
            pltpu.SemaphoreType.DMA((max(n_local, 1),)),
            pltpu.SemaphoreType.DMA((n_send,)),
            pltpu.SemaphoreType.DMA((n_send,)),
            *scratch,
        ],
        compiler_params=pltpu.CompilerParams(collective_id=cid, has_side_effects=True, vmem_limit_bytes=VM),
    )(*arrays)


def line_shifts():
    return [(d, 0, 0, 0) for d in range(1, lax.axis_size("sa"))]


CHIPS = [(0, 1, 0, 0), (0, 0, 1, 0), (0, 1, 1, 0)]
OTHER_CORE = (0, 0, 0, 1)


class Gather:
    def __init__(self, net, src, view, half=None):
        self.net, self.src, self.view, self.half = net, src, view, half

    def slot(self, shift):
        return self.net.at(shift)[1:]

    def hand(self, view, shift):
        copy = self.net.send(view, view, shift)
        self.out.append(copy)
        return copy

    def first(self):
        net = self.net
        here = self.view(*net.me[1:])
        net.keep(self.src, here)
        self.near = [net.send(self.src, here, s) for s in CHIPS[:2]]
        self.far = [] if self.half else [net.send(self.src, here, CHIPS[2])]
        self.out = self.near + self.far
        self.core = [net.send(self.src, here, OTHER_CORE)]

    def to_core(self, shift):
        view = self.view(*self.slot(shift))
        self.core.append(self.net.send(view, view, OTHER_CORE))

    def second(self):
        for h, copy in enumerate(self.near):
            copy.wait_recv()
            if self.half:
                self.far.append(self.hand(self.half(*self.slot(CHIPS[h]), h), CHIPS[1 - h]))
            self.to_core(CHIPS[h])

    def third(self):
        for copy in self.far:
            copy.wait_recv()
        self.to_core(CHIPS[2])

    def end(self):
        for copy in self.out:
            copy.wait_send()
        for copy in self.core:
            copy.wait()


def gather_body(net, gathers):
    for step in ("second", "third", "end"):
        for g in gathers:
            getattr(g, step)()


def line_exchange(arrays, gathers, cid, shares=()):
    m = len(arrays)
    n = m + len(gathers)

    def body(ins, outs, _, net):
        shifts = line_shifts()
        net.greet(shifts + (plane_shifts() if shares else CHIPS[:2] + [OTHER_CORE] if gathers else []))
        a = net.me[0]
        open_ = []
        for x, o in zip(ins[:m], outs):
            open_ += [net.send(x.at[net.at(s)[0]], o.at[a], s) for s in shifts]
            net.keep(x.at[a], o.at[a])
        planes = [
            Gather(net, x, functools.partial(g[2], o), functools.partial(g[3], o))
            for x, o, g in zip(ins[m:], outs[m:], gathers)
        ]
        for g in planes:
            g.first()
        mine = net.me[1:]
        for x, o in zip(ins[n:], outs[n:]):
            open_ += [net.send(x.at[net.at(s)[1:]], o.at[mine], s) for s in plane_shifts()]
            net.keep(x.at[mine], o.at[mine])
        gather_body(net, planes)
        for copy in open_:
            copy.wait()
        net.settle()

    sd = jax.ShapeDtypeStruct
    shapes = [sd(x.shape, x.dtype) for x in arrays] + [sd(g[1], g[0].dtype) for g in gathers]
    shapes += [sd(x.shape, x.dtype) for x in shares]
    n_send = (lax.axis_size("sa") - 1) * m + 8 * len(gathers) + 7 * len(shares)
    operands = [*arrays, *(g[0] for g in gathers), *shares]
    return call_net(body, operands, shapes, cid, len(operands), n_send)


def rows_gather(x):
    sizes = tuple(lax.axis_size(k) for k in PLANE)
    half = x.shape[0] // 2
    return (
        x,
        sizes + x.shape,
        lambda o, b, y, c: o.at[b, y, c],
        lambda o, b, y, c, h: o.at[b, y, c, pl.ds(h * half, half)],
    )


def swap_first(net, x, o):
    b = net.me[1]
    net.keep(x.at[b], o.at[b])
    return [net.send(x.at[net.at(CHIPS[0])[1]], o.at[b], CHIPS[0])]


def plane_shifts():
    return [(0, i // 4, i // 2 % 2, i % 2) for i in range(1, 8)]


def start_exchange(tokens, sq, low, up, key, cid):
    A, B = lax.axis_size("sa"), lax.axis_size("sb")
    S, hops = A * B, A - 1
    sizes = tuple(lax.axis_size(k) for k in PLANE)
    n_fixed = 2 * hops + 8 + 8 + 7 + 7 + 1

    def body(ins, outs, scratch, net):
        x, q, lo, u, ke = ins
        xo, qo, loo, uo, ko, q_line, lo_line = outs
        line = line_shifts()
        net.greet(line + plane_shifts())
        a, b, y, c = net.me
        me = a * B + b
        ssem, rsem = net.sems[1:]

        def block(i, k):
            return xo.at[i * B + (b if k == 0 else 1 - b)]

        def index(way, t, k):
            return n_fixed + (way * hops + t) * 2 + k

        def origin(way, t):
            return a - t if way == 0 else a + t

        def have(way, t):
            return a >= t if way == 0 else a <= A - 1 - t

        def can(way):
            return a < A - 1 if way == 0 else a > 0

        def relay(way, t, k):
            dst = block(origin(way, t), k)
            i = index(way, t, k)
            to = (a + 1 if way == 0 else a - 1, b, y, c)
            src = x.at[b] if t == 0 and k == 0 else dst
            return pltpu.make_async_remote_copy(src, dst, ssem.at[i], rsem.at[i], device_id=to, device_id_type=MESH)

        def relay_start(t, k):
            for way in range(2):

                @pl.when(have(way, t) & can(way))
                def _(way=way):
                    relay(way, t, k).start()

        def relay_arrived(t, k):
            for way in range(2):

                @pl.when(have(way, t))
                def _(way=way):
                    dst, i = block(origin(way, t), k), index(way, t - 1, k)
                    pltpu.make_async_remote_copy(
                        dst, dst, ssem.at[i], rsem.at[i], device_id=net.at(OTHER_CORE), device_id_type=MESH
                    ).wait_recv()

        first = []
        for s in line:
            first.append(net.send(q.at[net.at(s)[0]], q_line.at[:, a], s))
            first.append(net.send(lo, lo_line.at[a], s))
        relay_start(0, 0)
        across = net.send(x.at[1 - b], xo.at[me], CHIPS[0])
        net.keep(q.at[a], q_line.at[:, a])
        net.keep(lo, lo_line.at[a])
        planes = [Gather(net, u, lambda i, j, k: uo.at[i, j, k])]
        planes[0].first()
        across.wait_recv()
        relay_start(0, 1)
        for copy in first:
            copy.wait()
        net.settle()
        net.locals = []
        net.keep(x.at[b], xo.at[me])
        h = A // 2
        planes.append(
            Gather(net, q_line, lambda i, j, k: qo.at[:, :, i, j, k], lambda i, j, k, p: qo.at[:, pl.ds(p * h, h), i, j, k])
        )
        planes.append(Gather(net, lo_line, lambda i, j, k: loo.at[:, i, j, k], lambda i, j, k, p: loo.at[pl.ds(p * h, h), i, j, k]))
        planes[1].first()
        planes[2].first()
        mine = net.me[1:]
        rest = [net.send(ke.at[net.at(s)[1:]], ko.at[mine], s) for s in plane_shifts()]
        net.keep(ke.at[mine], ko.at[mine])
        for t in range(1, hops):
            for k in range(2):
                relay_arrived(t, k)
                relay_start(t, k)
            if t == 1:
                for g in planes:
                    g.second()
        for g in planes:
            g.third()
        for k in range(2):
            relay_arrived(hops, k)
        for t in range(hops):
            for k in range(2):
                for way in range(2):

                    @pl.when(have(way, t) & can(way))
                    def _(way=way, t=t, k=k):
                        relay(way, t, k).wait_send()

        across.wait_send()
        for g in planes:
            g.end()
        for copy in rest:
            copy.wait()
        net.settle()

    sd = lambda shape, like: jax.ShapeDtypeStruct(shape, like.dtype)
    shapes = [
        sd((S,) + tokens.shape[1:], tokens),
        sd(sq.shape[1:2] + (A,) + sizes + sq.shape[2:], sq),
        sd((A,) + sizes + low.shape, low),
        sd(sizes + up.shape, up),
        sd(key.shape, key),
        sd(sq.shape[1:2] + (A,) + sq.shape[2:], sq),
        sd((A,) + low.shape, low),
    ]
    return call_net(body, [tokens, sq, low, up, key], shapes, cid, 9, n_fixed + 4 * hops)[:5]


def tail_exchange(dh, sq3, sq, down, wide, up, narrow, ffn, cid):
    A = lax.axis_size("sa")
    leads = [2, 1, 1, 0, 0, 0]
    arrays = [sq, down, wide, up, narrow, ffn]
    blocks = [x.shape[:n] + x.shape[n + 3 :] for x, n in zip(arrays, leads)]
    n = len(arrays)

    def body(ins, outs, scratch, net):
        ps, pos = ins[2:], outs[2:]
        own, other, chips = scratch[:n], scratch[n : 2 * n], scratch[2 * n :]
        line = line_shifts()
        net.greet(line + CHIPS + [OTHER_CORE])
        a, b, y, c = net.me
        there = net.at(OTHER_CORE)[3]
        pairs = [(i // 2, i % 2) for i in range(4)]

        def block(t, i, j, k):
            return ps[t].at[(slice(None),) * leads[t] + (i, j, k)]

        cores, mine = [], []
        for t in range(n):
            cores.append([net.send(block(t, i, j, there), other[t].at[2 * i + j], OTHER_CORE) for i, j in pairs])
            for i, j in pairs:
                net.keep(block(t, i, j, c), own[t].at[2 * i + j])
            mine.append(net.locals)
            net.locals = []
        open_ = []
        for x, o in zip(ins[:2], outs[:2]):
            open_ += [net.send(x.at[net.at(s)[0]], o.at[a], s) for s in line]
            net.keep(x.at[a], o.at[a])

        def add(t, k, terms):
            shape = blocks[t]
            step = min(shape[-2], 16)
            per = shape[-2] // step
            count = per
            for size in shape[:-2]:
                count = count * size

            @pl.loop(0, count)
            def _(r):
                index = []
                rest = r // per
                for size in reversed(shape[:-2]):
                    index.insert(0, rest % size)
                    rest = rest // size
                at = (*index, pl.ds(pl.multiple_of(r % per * step, step), step))
                total = own[t][(k, *at)].astype(F32)
                for ref, i in terms:
                    total = total + ref[(i, *at)].astype(F32)
                own[t][(k, *at)] = total.astype(BF)

        sent = []
        for t in range(n):
            for copy in cores[t] + mine[t]:
                copy.wait()
            for k, s in enumerate(CHIPS):
                to = net.at(s)
                slot = 2 * to[1] + to[2]
                add(t, slot, [(other[t], slot)])
                sent.append(net.send(own[t].at[slot], chips[t].at[k], s))
        me = 2 * b + y
        for t in range(n):
            for copy in sent[3 * t : 3 * t + 3]:
                copy.wait_recv()
            add(t, me, [(other[t], me)] + [(chips[t], k) for k in range(3)])
            net.keep(own[t].at[me], pos[t])
        for copy in sent:
            copy.wait_send()
        for copy in open_:
            copy.wait()
        net.settle()

    sd = jax.ShapeDtypeStruct
    shapes = [sd(dh.shape, BF), sd(sq3.shape, BF)] + [sd(s, BF) for s in blocks]
    scratch = [pltpu.VMEM((m,) + s, BF) for m in (4, 4, 3) for s in blocks]
    n_send = 2 * (A - 1) + 7 * n
    return call_net(body, [dh, sq3, *arrays], shapes, cid, 2 + 5 * n, n_send, scratch)


def last_exchange(swaps, sq, lines, key, cid):
    m = len(swaps)
    n = m + 1 + len(lines)

    def body(ins, outs, _, net):
        line, plane = line_shifts(), plane_shifts()
        net.greet(line + plane)
        a = net.me[0]
        mine = net.me[1:]
        open_ = []
        for i, (x, o) in enumerate(zip(ins[:n], outs)):
            if i < m:
                open_ += swap_first(net, x, o)
                continue
            view = (lambda x, k: x.at[:, k]) if i == m else (lambda x, k: x.at[k])
            open_ += [net.send(view(x, net.at(s)[0]), o.at[a], s) for s in line]
            net.keep(view(x, a), o.at[a])
        open_ += [net.send(ins[n].at[net.at(s)[1:]], outs[n].at[mine], s) for s in plane]
        net.keep(ins[n].at[mine], outs[n].at[mine])
        for copy in open_:
            copy.wait()
        net.settle()

    sd = jax.ShapeDtypeStruct
    arrays = [*swaps, sq, *lines, key]
    shapes = [sd(x.shape, x.dtype) for x in arrays]
    shapes[m] = sd((sq.shape[1], sq.shape[0]) + sq.shape[2:], sq.dtype)
    n_send = m + (1 + len(lines)) * (lax.axis_size("sa") - 1) + 7
    return call_net(body, arrays, shapes, cid, len(arrays), n_send)


def layer_norm(x, gain, bias):
    cen = x - jnp.mean(x, axis=-1, keepdims=True)
    var = jnp.mean(cen * cen, axis=-1, keepdims=True)
    return cen * lax.rsqrt(var + 1e-05) * gain + bias


def next_line(value, steps):
    count = lax.axis_size("sa")
    first, last = max(0, -steps), min(count, count - steps)
    return lax.ppermute(value, "sa", [(i, i + steps) for i in range(first, last)])


def after(value, *others):
    return lax.optimization_barrier((value, *others))[0]


def per_device(tokens, first_values, lengths, vectors, down, up, square, key_w, value_w, out_grad):
    rows_here, seg, D = tokens.shape
    SA, SB, RA, RC = (lax.axis_size(k) for k in AXES)
    a, b = lax.axis_index("sa"), lax.axis_index("sb")
    S, F = SA * SB, SB * RA * RC
    L = seg * S
    C = D // SA
    NB = L // BLK
    gc = min(C, 256)
    T = SB * seg
    w = square.shape[1]
    n_low, n_vec = down.shape[1], vectors.shape[0]
    FS = key_w.shape[1] // (S * RA * RC)

    lens = lax.dynamic_index_in_dim(lengths, b, 0, keepdims=False)
    count = lens.shape[0]
    lower = jnp.arange(count)[:, None] > jnp.arange(count)[None, :]
    starts = jnp.sum(jnp.where(lower, lens[None, :], 0), axis=1)
    pos = jnp.arange(L, dtype=jnp.int32)
    reset = jnp.any(pos[:, None] == starts[None, :], axis=1).astype(F32)
    segid = jnp.sum((pos[:, None] >= starts[None, :]).astype(F32), axis=1) - 1.0
    blocks = segid.reshape(NB, BLK)
    before = blocks[:, :1] - reset.reshape(NB, BLK)[:, :1]
    carried = (blocks == before).astype(F32).reshape(L)
    live = (blocks == blocks[:, -1:]).astype(F32).reshape(L)
    meta = jnp.stack([segid, carried, live, 1.0 - reset], axis=1)
    segrow = jnp.tile(blocks.reshape(NB, 1, BLK), (1, 1, gc // SD))
    keep_row = (1.0 - reset)[:, None]
    keep_own = lax.dynamic_slice(keep_row, (a * T, 0), (T, 1))

    sq3 = lax.all_gather(square[3], AXES, axis=0, tiled=True)
    first_sliced = first_values.reshape(rows_here, seg, SA, C).transpose(2, 0, 1, 3).reshape(S, seg, C)
    first_row = lax.all_to_all(first_sliced, ("sa", "sb"), split_axis=0, concat_axis=0, tiled=True).reshape(L, C)
    cuts = [0, DECAY_INNER, DECAY_INNER + LA, DECAY_INNER + LA + LV, n_low]

    def widen(m):
        pieces = [m[:, i:j] for i, j in zip(cuts[:-1], cuts[1:])]
        return jnp.concatenate([jnp.pad(p, ((0, 0), (0, -p.shape[1] % 128))) for p in pieces], axis=1)

    wide_at = [0, 128, 256, 384]
    low_mine = jnp.concatenate([widen(down), jnp.pad(vectors.T, ((0, 0), (0, 128 - n_vec)))], axis=1)
    sq_mine = square[:3].reshape(3, w, SA, C).transpose(2, 0, 1, 3)
    half = SA * FS
    key_mine = key_w.reshape(w, SA, F, FS).transpose(2, 0, 1, 3).reshape(SB, RA, RC, w, half)
    x_row, sq, low, up_heads, key_line = start_exchange(tokens, sq_mine, low_mine, widen(up.T), key_mine, 1)
    x_row = x_row.reshape(L, D)
    sq = sq.reshape(3, D, C)
    low = low.reshape(D, 768)
    up_w = up_heads.reshape(C, 640)
    vec = low[:, 640 : 640 + n_vec].astype(F32).T
    vec_heads = lax.dynamic_slice(vec, (10, a * C), (8, C))
    FW = F * w
    halves = [slice(i * half, (i + 1) * half) for i in range(D // half)]
    kv = jnp.concatenate([key_line.reshape(FW, half), *(value_w[:, s] for s in halves)], axis=0)
    kv_all = lax.all_gather(kv, "sa", axis=0)
    key_all = kv_all[:, :FW].reshape(D, half)
    value_all = jnp.concatenate(
        [kv_all[:, FW + i * FS : FW + (i + 1) * FS].reshape(half, half) for i in range(D // half)], axis=1
    )

    xm, (rp, kp, vp, uw, ua, uv, ug), mid, mid_low = mix_forward(x_row, meta, vec, sq, low, up_w)
    ins = (rp, kp, vp, uw, ua, uv, first_row)
    y, saved = recurrence_forward(ins, vec_heads, meta, segrow)
    z = (y.astype(F32) * ug).astype(BF)
    gather_g = (
        out_grad,
        (SB, RA, RC, SB, seg, D),
        lambda o, i, j, k: o.at[:, j, k, i],
        lambda o, i, j, k, h: o.at[h, j, k, i],
    )
    z_own, g_all = line_exchange([z.reshape(SA, T, C)], [gather_g], 2)
    g_all = g_all.reshape(F * T, D)
    z_own = z_own.transpose(1, 0, 2).reshape(T, D)
    z_share = z_own.reshape(T, SA, F, w).transpose(2, 0, 1, 3).reshape(SB, RA, RC, T, SA * w)

    x_own = lax.dynamic_slice(x_row, (a * T, 0), (T, D)).astype(F32)
    x1 = x_own + mm(z_own, sq3, NN)
    h2, norm2_pull = jax.vjp(layer_norm, x1, vec[2], vec[3])
    edge2 = next_line(h2[-1:], 1)

    def channel_mix(h, edge, mix):
        s = jnp.concatenate([edge, h[:-1]], axis=0) * keep_own
        return h + (s - h) * mix

    xc, cmix_pull = jax.vjp(channel_mix, h2, edge2, vec[18])
    (xc_all,) = line_exchange([], [rows_gather(xc.astype(BF))], 3)
    xc_all = xc_all.reshape(F * T, D)
    kc = jax.nn.relu(mm(xc_all, key_all, NN))
    q = (kc * kc).astype(BF)
    dkc = (mm(g_all, value_all, NT) * 2.0 * kc).astype(BF)
    dxc = lax.psum_scatter(mm(dkc, key_all, NT).astype(BF), PLANE, scatter_dimension=0, tiled=True)
    ffn_part = mm(q, value_all, NN).astype(BF)
    value_part = mm(q, g_all, TN).astype(BF).reshape(SA, FS, D)
    key_part = mm(xc_all, dkc, TN).astype(BF).reshape(SA, FW, half)
    kv_part = jnp.concatenate([key_part, *(value_part[:, :, s] for s in halves)], axis=1)
    dxc, kv_part, ffn_part = lax.optimization_barrier((dxc, kv_part, ffn_part))

    dh2, dedge2, g18 = cmix_pull(dxc.astype(F32))
    dh2 = dh2.at[-1:].add(next_line(dedge2, -1))
    dx1n, g2, g3 = norm2_pull(dh2)
    slot = (b * RA + lax.axis_index("ra")) * RC + lax.axis_index("rc")
    dx1 = lax.dynamic_slice(g_all, (slot * T, 0), (T, D)).astype(F32) + dx1n
    dt = dx1.astype(BF)
    dz = mm(dt, sq3, NT).astype(BF)
    dz_row, dt_all, z_share = line_exchange(
        [dz.reshape(T, SA, C).transpose(1, 0, 2)], [rows_gather(dt)], 4, [z_share]
    )
    kv_grad = lax.psum_scatter(after(kv_part, dz).reshape(-1, half), "sa", scatter_dimension=0, tiled=True)
    dz_row = dz_row.reshape(L, C).astype(F32)

    dy = (dz_row * ug).astype(BF)
    dug = (dz_row * y.astype(F32)).astype(BF)
    drp, dkp, dvp, duw, dua, duv, dfl, dvec = recurrence_backward(dy, saved, ins, vec_heads, meta, segrow)
    dfl = lax.all_to_all(dfl.reshape(S, seg, C), ("sa", "sb"), split_axis=0, concat_axis=0, tiled=True)
    dh1, dd, gmix = mix_backward((drp, dkp, dvp, duw, dua, duv, dug), x_row, meta, mid, vec, sq, low, up_w)
    g0, g1 = gmix[6], gmix[7]

    sq_part, down_part, up_part, sq3_part = weight_grads(
        xm, (drp, dkp, dvp, duw, dua, duv, dug), dd, mid_low, z_share.reshape(F * T, SA * w), dt_all.reshape(F * T, D)
    )
    dfl, sq_part = lax.optimization_barrier((dfl, sq_part))
    first_grad = dfl.reshape(SA, SB, seg, C).transpose(1, 2, 0, 3).reshape(rows_here, seg, D)
    wide = jnp.stack([g0, g1, g2, g3, *(gmix[i] for i in range(6)), g18] + [jnp.zeros_like(g0)] * 5).astype(BF)
    wide = jnp.pad(wide.T, ((0, 0), (0, 112)))
    narrow = jnp.pad(dvec.astype(BF).T, ((0, 0), (0, 120)))
    plane = (SB, RA, RC, w)
    dh1_own, sq3_sum, sq_sum, down_sum, wide_sum, up_sum, narrow_sum, ffn = tail_exchange(
        dh1.reshape(SA, T, D),
        sq3_part.reshape(SA, w, D),
        sq_part.reshape((3, SA) + plane + (C,)),
        down_part.reshape((SA,) + plane + (640,)),
        wide.reshape((SA,) + plane + (128,)),
        up_part.reshape(plane + (640,)),
        narrow.reshape(plane + (128,)),
        ffn_part.reshape(SB, RA, RC, T, D),
        5,
    )
    dh1_own = jnp.sum(dh1_own.astype(F32), axis=0)
    _, norm1_pull = jax.vjp(lambda x: layer_norm(x, vec[0], vec[1]), x_own)
    (dx0,) = norm1_pull(dh1_own)
    mixed = (x1 + ffn.astype(F32)).astype(BF)
    tokens_grad, mixed_out, sq_sum, down_sum, wide_sum, key_grad = last_exchange(
        [(dx1 + dx0).astype(BF).reshape(SB, seg, D), mixed.reshape(SB, seg, D)],
        sq_sum,
        [down_sum, wide_sum],
        kv_grad[:FW].reshape(SB, RA, RC, w, half),
        6,
    )
    sq3_sum = jnp.sum(sq3_sum.astype(F32), axis=0)
    square_grad = jnp.concatenate([sq_sum.transpose(1, 2, 0, 3).reshape(3, w, D).astype(F32), sq3_sum[None]], axis=0)
    narrow_pieces = lambda m: [m[:, i : i + q - p] for i, p, q in zip(wide_at, cuts[:-1], cuts[1:])]
    down_grad = jnp.concatenate(narrow_pieces(jnp.sum(down_sum.astype(F32), axis=0)), axis=1)
    up_grad = jnp.concatenate(narrow_pieces(up_sum.astype(F32)), axis=1).T
    wide_t = jnp.sum(wide_sum.astype(F32), axis=0)[:, :16].T
    narrow_t = narrow_sum[:, :8].astype(F32).T
    vectors_gradient = jnp.concatenate([wide_t[:10], narrow_t, wide_t[10:11]], axis=0)
    value_grad = jnp.concatenate([kv_grad[FW + i * FS : FW + (i + 1) * FS] for i in range(D // half)], axis=1)
    value_grad = value_grad.astype(F32)
    key_grad = key_grad.reshape(F, w, SA, FS).transpose(1, 2, 0, 3).reshape(w, -1).astype(F32)
    return (
        mixed_out,
        tokens_grad,
        first_grad,
        vectors_gradient,
        down_grad,
        up_grad,
        square_grad,
        key_grad,
        value_grad,
    )


def solution(mesh):
    seq, row = mesh.shape["seq"], mesh.shape["row"]
    fine = Mesh(mesh.devices.reshape(seq // 2, 2, row // 2, 2), AXES)
    S, R = ("sa", "sb"), ("ra", "rc")
    in_specs = (
        P(R, S, None),
        P(R, S, None),
        P(R, None),
        P(None, S + R),
        P(S + R, None),
        P(None, S + R),
        P(None, S + R, None),
        P(S + R, None),
        P(S + R, None),
        P(R, S, None),
    )
    out_specs = (
        P(R, S, None),
        P(R, S, None),
        P(R, S, None),
        P(None, S + R),
        P(S + R, None),
        P(None, S + R),
        P(None, S + R, None),
        P(S + R, None),
        P(S + R, None),
    )
    return jax.shard_map(per_device, mesh=fine, in_specs=in_specs, out_specs=out_specs, check_vma=False)
```

```python
import functools

import jax
import jax.numpy as jnp
from jax import lax
from jax.experimental import pallas as pl
from jax.experimental.pallas import tpu as pltpu
from jax.sharding import Mesh, PartitionSpec as P

DECAY_INNER = 96
LA = 96
LV = 64

BF=jnp.bfloat16; F32=jnp.float32
SD=64; BLK=64
NN=(((1,),(0,)),((),())); NT=(((1,),(1,)),((),())); TN=(((0,),(0,)),((),()))

def mm(a,b,d): return lax.dot_general(a,b,d,preferred_element_type=F32)

class Geo:
    def __init__(s, gc):
        s.gc=gc; s.gh=gc//SD
        lane=lax.broadcasted_iota(jnp.int32,(1,gc),1)
        s.head=lane//SD
        s.lm=[(s.head==h).astype(BF) for h in range(s.gh)]
        row=lax.broadcasted_iota(jnp.int32,(BLK,gc),0)
        col=lax.broadcasted_iota(jnp.int32,(BLK,gc),1)%SD
        s.below=row>col; s.upto=row>=col
    def blk(s,x):
        return jnp.concatenate([x*m for m in s.lm],axis=0) if s.gh>1 else x
    def ext(s,x):
        out=x[:BLK]
        for h in range(1,s.gh):
            out=jnp.where(s.head==h,x[h*BLK:(h+1)*BLK],out)
        return out

def headsums(ones, *xs):
    hi = [x.astype(BF) for x in xs]
    lo = [(x - h.astype(F32)).astype(BF) for x, h in zip(xs, hi)]
    s = mm(jnp.concatenate(hi + lo, axis=0), ones, NN)
    n = len(xs) * BLK
    return [s[i * BLK : (i + 1) * BLK] + s[n + i * BLK : n + (i + 1) * BLK] for i in range(len(xs))]

def decayed(geo,ws,tri):
    w=ws.astype(F32)
    cum=mm(tri,ws,NN)
    return w,cum,jnp.exp(cum-w),jnp.exp(cum),jnp.exp(-cum)

def first_block(rp,kp,vp,uw,ua,uv,fl,vec,meta,segrow,tri,ones,rs,ws,ks,vs,qs,as_,ri_out,ab):
    C=rp.shape[1]; gc=min(C,256); geo=Geo(gc)
    same=meta[:,0:1]==segrow[0]
    strict=geo.below&same
    for g in range(C//gc):
        sl=slice(g*gc,(g+1)*gc)
        V=lambda i: vec[i:i+1,sl]
        k0=kp[:,sl]; v0=vp[:,sl]
        lw=-0.606531*jax.nn.sigmoid(V(0)+uw[:,sl])
        al=jax.nn.sigmoid(V(1)+ua[:,sl])
        vm=jax.nn.sigmoid(V(2)+uv[:,sl])
        v=v0+(fl[:,sl].astype(F32)-v0)*vm
        kn=k0*V(3)
        ri=lax.rsqrt(headsums(ones[...],kn*kn)[0]+1e-6)
        ri_out[:,sl]=ri
        kk=kn*ri
        km=k0*(1.0+(al-1.0)*V(4))
        q_=kk.astype(BF); w_=lw.astype(BF); a_=al.astype(BF)
        rs[:,sl]=rp[:,sl].astype(BF); ws[:,sl]=w_; ks[:,sl]=km.astype(BF)
        vs[:,sl]=v.astype(BF); qs[:,sl]=q_; as_[:,sl]=a_
        w,cum,eP,eC,eN=decayed(geo,w_,tri[...])
        q=q_.astype(F32)
        qu=(q*eP).astype(BF); bb=(q*a_.astype(F32)*eN).astype(BF)
        put128(ab,g,jnp.where(strict,mm(qu,geo.blk(bb),NT),0.0))

def put128(ref, g, x):
    if x.shape[1] < 128:
        x = jnp.concatenate([x, jnp.zeros_like(x)], axis=1)
    n = x.shape[1] // 128
    for k in range(n):
        ref[g * n + k] = x[:, k * 128 : (k + 1) * 128]


def get128(ref, g, gc):
    n = max(gc // 128, 1)
    x = jnp.concatenate([ref[g * n + k] for k in range(n)], axis=1) if n > 1 else ref[g]
    return x[:, :gc].astype(BF)


def solve_kernel(ab, tt, a, t):
    G, L, _ = ab.shape
    NB = L // BLK
    B = NB * G * 2

    @pl.loop(0, BLK, unroll=8)
    def _(i):
        rows = [ab[g, pl.ds(i, NB, stride=BLK), :] for g in range(G)]
        a[i] = jnp.concatenate([r[:, k * SD : (k + 1) * SD] for r in rows for k in range(2)], axis=0).T

    t[...] = jnp.zeros_like(t)
    cidx = lax.broadcasted_iota(jnp.int32, (SD, B), 0)

    @pl.loop(0, BLK)
    def _(i):
        def inner(jb, acc):
            for jj in range(8):
                j = jb * 8 + jj
                acc = acc - a[i, pl.ds(j, 1), :] * t[j]
            return acc

        t[i] = lax.fori_loop(0, i // 8 + 1, inner, (cidx == i).astype(F32))

    @pl.loop(0, BLK, unroll=8)
    def _(i):
        rows = t[i].T
        for g in range(G):
            pair = [rows[(2 * g + k) * NB : (2 * g + k + 1) * NB] for k in range(2)]
            tt[g, pl.ds(i, NB, stride=BLK), :] = jnp.concatenate(pair, axis=1)


def forward_block(rs,ws,ks,vs,qs,as_,tt,vec,meta,segrow,tri,ones,y,nrm_out,rstd_out,extra_out,u_out,al_out,lb_out,s_out,state):
    C=rs.shape[1]; gc=min(C,256); geo=Geo(gc)
    same=meta[:,0:1]==segrow[0]
    carried=meta[:,1:2]; live=meta[:,2:3]; last=meta[BLK-1:BLK,1:2]
    strict=geo.below&same; incl=geo.upto&same
    for g in range(C//gc):
        sl=slice(g*gc,(g+1)*gc)
        V=lambda i: vec[i:i+1,sl]
        w,cum,eP,eC,eN=decayed(geo,ws[:,sl],tri[...])
        q=qs[:,sl].astype(F32); r=rs[:,sl].astype(F32); k=ks[:,sl].astype(F32)
        vb=vs[:,sl]; v=vb.astype(F32); a=as_[:,sl].astype(F32)
        qq=jnp.concatenate([(q*eP).astype(BF),(r*eC).astype(BF)],axis=0)
        kb=(k*eN).astype(BF); bb=(q*a*eN).astype(BF)
        mk=mm(qq,geo.blk(kb),NT)
        al=jnp.concatenate([jnp.where(strict,mk[:BLK],0.0).astype(BF),jnp.where(incl,mk[BLK:],0.0).astype(BF)],axis=0)
        lb=jnp.where(incl,mm(qq[BLK:],geo.blk(bb),NT),0.0).astype(BF)
        s0=state[g]; sb=s0.astype(BF)
        s_out[0,g]=sb
        qst=mm(qq,sb,NT)
        av=mm(al,geo.blk(vb),NN)
        rhs=carried*qst[:BLK]+av[:BLK]
        u=mm(get128(tt,g,gc),geo.blk(rhs.astype(BF)),NN)
        ub=u.astype(BF)
        u_out[:,sl]=ub
        o=carried*qst[BLK:]+av[BLK:]-mm(lb,geo.blk(ub),NN)
        vu=jnp.concatenate([(v*live).astype(BF),(u*(-live)).astype(BF)],axis=0)
        ds=mm(vu,jnp.concatenate([kb,bb],axis=0),TN)
        tail=eC[BLK-1:BLK]
        state[g]=(last*s0+ds*ones[...].astype(F32))*tail
        al_out[:,sl]=al; lb_out[:,sl]=lb
        mean,extra=headsums(ones[...],o,r*k*V(5))
        cen=o-mean*(1.0/SD)
        rstd=lax.rsqrt(headsums(ones[...],cen*cen)[0]*(1.0/SD)+1.0)
        nrm=cen*rstd
        nrm_out[:,sl]=nrm; rstd_out[:,sl]=rstd; extra_out[:,sl]=extra
        y[:,sl]=(nrm*V(6)+V(7)+extra*v).astype(BF)

def backward_block(dy,nrm_in,rstd_in,extra_in,rs,ws,ks,vs,qs,as_,tt,u_in,al_in,lb_in,s_in,ri_in,rp,kp,vp,uw,ua,uv,fl,vec,meta,segrow,tri,tru,ones,
                    drp,dkp,dvp,duw,dua,duv,dfl,dvec,state):
    C=rs.shape[1]; gc=min(C,256); geo=Geo(gc)
    same=meta[:,0:1]==segrow[0]
    carried=meta[:,1:2]; live=meta[:,2:3]; last=meta[BLK-1:BLK,1:2]
    strict=geo.below&same; incl=geo.upto&same
    cat=lambda *x: jnp.concatenate(x,axis=0)
    rsum=lambda x: jnp.sum(x,axis=0,keepdims=True)
    for g in range(C//gc):
        sl=slice(g*gc,(g+1)*gc)
        V=lambda i: vec[i:i+1,sl]
        on=ones[...]
        w,cum,eP,eC,eN=decayed(geo,ws[:,sl],tri[...])
        q=qs[:,sl].astype(F32); r=rs[:,sl].astype(F32); k=ks[:,sl].astype(F32)
        vb=vs[:,sl]; v=vb.astype(F32); a=as_[:,sl].astype(F32)
        d=dy[:,sl].astype(F32); nrm=nrm_in[:,sl]; extra=extra_in[:,sl]
        dn=d*V(6)
        de,dn1,dn2=headsums(on,d*v,dn,dn*nrm)
        do=rstd_in[:,sl]*(dn-dn1*(1.0/SD)-nrm*(dn2*(1.0/SD)))
        g17=rsum(d); g16=rsum(d*nrm); g15=rsum(de*r*k)
        dr=de*k*V(5); dk=de*r*V(5); dv=d*extra
        qq=cat((q*eP).astype(BF),(r*eC).astype(BF))
        kb=(k*eN).astype(BF); bb=(q*a*eN).astype(BF)
        kblk=geo.blk(kb); bblk=geo.blk(bb)
        al=al_in[:,sl]; lb=lb_in[:,sl]
        ub=u_in[:,sl]; s0=s_in[0,g]
        tail=eC[BLK-1:BLK]
        ds1=state[g]*tail; dsb=ds1.astype(BF)
        kbs=mm(cat(kb,bb),dsb,NT)
        dob=do.astype(BF)
        du=-geo.ext(mm(lb,dob,TN))-live*kbs[BLK:]
        yy=geo.ext(mm(get128(tt,g,gc),du.astype(BF),TN))
        yo=cat(yy.astype(BF),dob)
        cyo=cat((carried*yy).astype(BF),(carried*do).astype(BF))
        mv=mm(yo,geo.blk(vb),NT); mu=mm(yo,geo.blk(ub),NT)
        dkm=cat(jnp.where(strict,mv[:BLK],0.0).astype(BF),jnp.where(incl,mv[BLK:],0.0).astype(BF))
        dbm=cat(jnp.where(strict,-mu[:BLK],0.0).astype(BF),jnp.where(incl,-mu[BLK:],0.0).astype(BF))
        dqq=mm(cyo,s0,NN)+mm(dkm,kblk,NN)+mm(dbm,bblk,NN)
        vus=mm(cat(vb,ub),dsb,NN)
        kst=live*vus[:BLK]; bst=-(live*vus[BLK:])
        dkb=geo.ext(mm(dkm,qq,TN))+kst
        dbb=geo.ext(mm(dbm,qq,TN))+bst
        dv=dv+geo.ext(mm(al,yo,TN))+live*kbs[:BLK]
        kf=kb.astype(F32); bf=bb.astype(F32); qf=qq.astype(F32)
        dlast=last*rsum(ds1*s0.astype(F32))+rsum(kf*kst+bf*bst)
        state[g]=mm(cyo,qq,TN)*on.astype(F32)+last*ds1
        dqu=dqq[:BLK]*qf[:BLK]
        dcum=dqu+dqq[BLK:]*qf[BLK:]-dkb*kf-dbb*bf
        hi=dcum.astype(BF); rest=dcum-hi.astype(F32); lo=rest.astype(BF)
        lo2=(rest-lo.astype(F32)).astype(BF)
        dw=mm(tru[...],hi,NN)+mm(tru[...],lo,NN)+mm(tru[...],lo2,NN)+dlast-dqu
        dben=dbb*eN
        dq=dqq[:BLK]*eP+dben*a
        da=dben*q
        dr=dr+dqq[BLK:]*eC
        dk=dk+dkb*eN
        k0=kp[:,sl]; v0=vp[:,sl]
        sg=jax.nn.sigmoid(V(0)+uw[:,sl]); af=jax.nn.sigmoid(V(1)+ua[:,sl]); vm=jax.nn.sigmoid(V(2)+uv[:,sl])
        kn=k0*V(3)
        ri=ri_in[:,sl]
        kk=kn*ri
        gw=(-0.606531)*dw*sg*(1.0-sg)
        gv=dv*(fl[:,sl].astype(F32)-v0)*vm*(1.0-vm)
        da=da+dk*k0*V(4)
        ga=da*af*(1.0-af)
        dkn=ri*(dq-kk*headsums(on,dq*kk)[0])
        drp[:,sl]=dr.astype(BF)
        dkp[:,sl]=(dk*(1.0+(af-1.0)*V(4))+dkn*V(3)).astype(BF)
        dvp[:,sl]=(dv*(1.0-vm)).astype(BF)
        duw[:,sl]=gw.astype(BF); dua[:,sl]=ga.astype(BF); duv[:,sl]=gv.astype(BF)
        dfl[:,sl]=(dv*vm).astype(BF)
        dvec[:,sl]+=cat(rsum(gw),rsum(ga),rsum(gv),rsum(dkn*k0),rsum(dk*k0*(af-1.0)),g15,g16,g17)

def per_block(ref, kind, i):
    if kind is None:
        return ref
    size = {"n": 1, "pair": 2 * BLK}.get(kind, BLK)
    at = pl.ds(i * size, size)
    return ref.at[:, at] if kind == "inv" else ref.at[at]


def blocks_kernel(body, kinds, order, zeroed, *refs):
    @pl.when(pl.program_id(0) == 0)
    def _():
        for i in zeroed:
            refs[i][...] = jnp.zeros_like(refs[i])

    for i in order:
        body(*(per_block(r, k, i) for r, k in zip(refs, kinds)))


def consts(C):
    gc=min(C,256)
    i=jnp.arange(BLK); tri=(i[:,None]>=i[None,:]).astype(BF); tru=(i[:,None]<=i[None,:]).astype(BF)
    j=jnp.arange(gc)//SD; ones=(j[:,None]==j[None,:]).astype(BF)
    return tri,tru,ones

VM=60*2**20
def takes(us): return pl.CostEstimate(flops=int(us*6e8), bytes_accessed=1<<20, transcendentals=0)
UNROLL=2
def params(): return pltpu.CompilerParams(vmem_limit_bytes=VM)

def recurrence_forward(ins, vec, meta, segrow):
    L, C = ins[0].shape
    NB, gc = L // BLK, min(C, 256)
    G = C // gc
    tri, tru, ones = consts(C)
    inv = jax.ShapeDtypeStruct((-(-C // 128), L, 128), F32)
    n = UNROLL
    rowb = pl.BlockSpec((n * BLK, C), lambda i: (i, 0))
    fix = lambda s: pl.BlockSpec(s, lambda i: (0,) * len(s))
    metab = pl.BlockSpec((n * BLK, meta.shape[1]), lambda i: (i, 0))
    segb = pl.BlockSpec((n, 1, gc), lambda i: (i, 0, 0))
    invb = pl.BlockSpec((inv.shape[0], n * BLK, 128), lambda i: (0, i, 0))
    sd = lambda dt: jax.ShapeDtypeStruct((L, C), dt)
    tail = [fix((8, C)), metab, segb, fix((BLK, BLK)), fix((gc, gc))]
    tail_kinds = [None, "row", "n", None, None]
    *six, ri, ab = pl.pallas_call(
        functools.partial(blocks_kernel, first_block, ["row"] * 7 + tail_kinds + ["row"] * 7 + ["inv"], range(n), ()),
        grid=(NB // n,),
        in_specs=[rowb] * 7 + tail,
        out_specs=[rowb] * 7 + [invb],
        out_shape=[sd(BF)] * 6 + [sd(F32), inv],
        compiler_params=params(),
    )(*ins, vec, meta, segrow, tri, ones)
    lanes = inv.shape[0] * 2 * NB
    tt = pl.pallas_call(
        solve_kernel, out_shape=inv, scratch_shapes=[pltpu.VMEM((BLK, SD, lanes), F32)] * 2, compiler_params=params()
    )(ab)
    kinds = ["row"] * 6 + ["inv"] + tail_kinds + ["row"] * 5 + ["pair", "row", "n", None]
    pairb = pl.BlockSpec((2 * n * BLK, C), lambda i: (i, 0))
    y, nrm, rstd, extra, u, al, lb, s = pl.pallas_call(
        functools.partial(blocks_kernel, forward_block, kinds, range(n), (len(kinds) - 1,)),
        grid=(NB // n,),
        in_specs=[rowb] * 6 + [invb] + tail,
        out_specs=[rowb] * 5 + [pairb, rowb, pl.BlockSpec((n, G, gc, gc), lambda i: (i, 0, 0, 0))],
        out_shape=[sd(BF)] + [sd(F32)] * 3 + [sd(BF), jax.ShapeDtypeStruct((2 * L, C), BF), sd(BF), jax.ShapeDtypeStruct((NB, G, gc, gc), BF)],
        scratch_shapes=[pltpu.VMEM((G, gc, gc), F32)],
        compiler_params=params(),
    )(*six, tt, vec, meta, segrow, tri, ones)
    return y, (nrm, rstd, extra, *six, tt, u, al, lb, s, ri)


def recurrence_backward(dy, saved, ins, vec, meta, segrow):
    L, C = ins[0].shape
    NB, gc = L // BLK, min(C, 256)
    G = C // gc
    tri, tru, ones = consts(C)
    n = UNROLL
    rev = lambda i: NB // n - 1 - i
    rowb = pl.BlockSpec((n * BLK, C), lambda i: (rev(i), 0))
    fix = lambda s: pl.BlockSpec(s, lambda i: (0,) * len(s))
    metab = pl.BlockSpec((n * BLK, meta.shape[1]), lambda i: (rev(i), 0))
    segb = pl.BlockSpec((n, 1, gc), lambda i: (rev(i), 0, 0))
    sb = pl.BlockSpec((n, G, gc, gc), lambda i: (rev(i), 0, 0, 0))
    invb = pl.BlockSpec((-(-C // 128), n * BLK, 128), lambda i: (0, rev(i), 0))
    kinds = ["row"] * 10 + ["inv", "row", "pair", "row", "n"] + ["row"] * 8 + [None, "row", "n", None, None, None] + ["row"] * 7 + [None] * 2
    last = len(kinds) - 1
    return pl.pallas_call(
        functools.partial(blocks_kernel, backward_block, kinds, range(n - 1, -1, -1), (last - 1, last)),
        grid=(NB // n,),
        in_specs=[rowb] * 10
        + [invb, rowb, pl.BlockSpec((2 * n * BLK, C), lambda i: (rev(i), 0)), rowb, sb]
        + [rowb] * 8
        + [fix((8, C)), metab, segb, fix((BLK, BLK)), fix((BLK, BLK)), fix((gc, gc))],
        out_specs=[rowb] * 7 + [fix((8, C))],
        out_shape=[jax.ShapeDtypeStruct((L, C), BF)] * 7 + [jax.ShapeDtypeStruct((8, C), F32)],
        scratch_shapes=[pltpu.VMEM((G, gc, gc), F32)],
        compiler_params=params(),
    )(dy, *saved, *ins, vec, meta, segrow, tri, tru, ones)


def mix_tile(x, vec, first_row, keep):
    cen = x - jnp.mean(x, axis=-1, keepdims=True)
    hat = cen * lax.rsqrt(jnp.mean(cen * cen, axis=-1, keepdims=True) + 1e-05)
    h = hat * vec[0:1] + vec[1:2]
    row = lax.broadcasted_iota(jnp.int32, h.shape, 0)
    shifted = jnp.where(row == 0, first_row, pltpu.roll(h, 1, 0))
    return hat, h, shifted * keep - h


def mix_forward_kernel(x, meta, vec, sq, low, up, *refs):
    xm, (rp, kp, vp, uw, ua, uv, ug, mid, midb, carry) = refs[:6], refs[6:]

    @pl.when(pl.program_id(0) == 0)
    def _():
        carry[...] = jnp.zeros_like(carry)

    _, h, delta = mix_tile(x[...].astype(F32), vec, carry[0:1], meta[:, 3:4])
    carry[0:1] = h[h.shape[0] - 1 :]
    m = []
    for i in range(6):
        m.append((h + delta * vec[4 + i : 5 + i]).astype(BF))
        xm[i][...] = m[i]
    rp[...] = mm(m[0], sq[0], NN)
    kp[...] = mm(m[2], sq[1], NN)
    vp[...] = mm(m[3], sq[2], NN)
    for out, i, lo, hi, act in ((uw, 1, 0, 128, jnp.tanh), (ua, 4, 128, 256, None), (uv, 3, 256, 384, None), (ug, 5, 384, 640, jax.nn.sigmoid)):
        d = mm(m[i], low[:, lo:hi], NN)
        if act is not None:
            d = act(d)
        b = d.astype(BF)
        mid[:, lo:hi] = d
        midb[:, lo:hi] = b
        out[...] = mm(b, up[:, lo:hi], NT)


def mix_backward_kernel(drp, dkp, dvp, duw, dua, duv, dug, x, above, meta, mid, vec, sq, low, up, dh, dd, gv, carry, hat_s):
    n, D = x.shape
    step = min(D, 512)

    @pl.when(pl.program_id(0) == 0)
    def _():
        carry[...] = jnp.zeros_like(carry)
        gv[...] = jnp.zeros_like(gv)

    def normalized(v):
        v = v.astype(F32)
        cen = v - jnp.mean(v, axis=-1, keepdims=True)
        return cen * lax.rsqrt(jnp.mean(cen * cen, axis=-1, keepdims=True) + 1e-05)

    hat_s[...] = normalized(x[...])
    prev = normalized(above[...])[above.shape[0] - 1 :]
    keep = meta[:, 3:4]
    dw = (mm(duw[...], up[:, 0:128], NN) * (1.0 - mid[:, 0:128] * mid[:, 0:128])).astype(BF)
    da = mm(dua[...], up[:, 128:256], NN).astype(BF)
    dv = mm(duv[...], up[:, 256:384], NN).astype(BF)
    s = mid[:, 384:640]
    dg = (mm(dug[...], up[:, 384:640], NN) * s * (1.0 - s)).astype(BF)
    dd[:, 0:128] = dw
    dd[:, 128:256] = da
    dd[:, 256:384] = dv
    dd[:, 384:640] = dg
    row = lax.broadcasted_iota(jnp.int32, (n, step), 0)
    for k in range(D // step):
        sl = slice(k * step, (k + 1) * step)
        gain, bias = vec[0:1, sl], vec[1:2, sl]
        hat = hat_s[:, sl]
        h = hat * gain + bias
        delta = jnp.where(row == 0, prev[:, sl] * gain + bias, pltpu.roll(h, 1, 0)) * keep - h
        total = ds = None
        for i in range(6):
            if i == 0:
                d = mm(drp[...], sq[0, sl], NT)
            elif i == 1:
                d = mm(dw, low[sl, 0:128], NT)
            elif i == 2:
                d = mm(dkp[...], sq[1, sl], NT)
            elif i == 3:
                d = mm(dvp[...], sq[2, sl], NT) + mm(dv, low[sl, 256:384], NT)
            elif i == 4:
                d = mm(da, low[sl, 128:256], NT)
            else:
                d = mm(dg, low[sl, 384:640], NT)
            gv[i : i + 1, sl] += jnp.sum(d * delta, axis=0, keepdims=True)
            scaled = d * vec[4 + i : 5 + i, sl]
            total = d if total is None else total + d
            ds = scaled if ds is None else ds + scaled
        back = ds * keep
        moved = jnp.where(row == n - 1, carry[0:1, sl], pltpu.roll(back, n - 1, 0))
        carry[0:1, sl] = back[0:1]
        g = total - ds + moved
        dh[:, sl] = g.astype(BF)
        gv[6:7, sl] += jnp.sum(g * hat, axis=0, keepdims=True)
        gv[7:8, sl] += jnp.sum(g, axis=0, keepdims=True)


def hidden_kernel(x, g, key, value, q, dk, dx):
    k = jnp.maximum(mm(x[...], key[...], NN), 0.0)
    q[...] = (k * k).astype(BF)
    d = (mm(g[...], value[...], NT) * (2.0 * k)).astype(BF)
    dk[...] = d
    dx[...] = mm(d, key[...], NT).astype(BF)


def hidden(x, g, key, value):
    n, D = x.shape
    H = key.shape[1]
    tok = lambda m: pl.BlockSpec((256, m), lambda i: (i, 0))
    fix = lambda s: pl.BlockSpec(s, lambda i: (0, 0))
    sd = lambda m: jax.ShapeDtypeStruct((n, m), BF)
    return pl.pallas_call(
        hidden_kernel,
        grid=(n // 256,),
        in_specs=[tok(D), tok(D), fix(key.shape), fix(value.shape)],
        out_specs=[tok(H), tok(H), tok(D)],
        out_shape=[sd(H), sd(H), sd(D)],
        cost_estimate=takes(30),
        compiler_params=params(),
    )(x, g, key, value)


def weight_kernel(x0, x1, x2, x3, x4, x5, drp, dkp, dvp, dd, duw, dua, duv, dug, mid, z, dt, sq, down, up, sq3):
    sq[0] = mm(x0[...], drp[...], TN).astype(BF)
    sq[1] = mm(x2[...], dkp[...], TN).astype(BF)
    sq[2] = mm(x3[...], dvp[...], TN).astype(BF)
    for x, lo, hi in ((x1, 0, 128), (x4, 128, 256), (x3, 256, 384), (x5, 384, 640)):
        down[:, lo:hi] = mm(x[...], dd[:, lo:hi], TN).astype(BF)
    sq3[...] = mm(z[...], dt[...], TN).astype(BF)

    @pl.when(pl.program_id(0) == 0)
    def _():
        for d, lo, hi in ((duw, 0, 128), (dua, 128, 256), (duv, 256, 384), (dug, 384, 640)):
            up[:, lo:hi] = mm(d[...], mid[:, lo:hi], TN).astype(BF)


def weight_grads(xm, grads, dd, mid, z, dt):
    L, D = xm[0].shape
    C, wide = grads[0].shape[1], mid.shape[1]
    n = 256 if L <= 1024 else 128
    tok, own = z.shape
    feat = pl.BlockSpec((L, n), lambda i: (0, i))
    fix = lambda m: pl.BlockSpec((L, m), lambda i: (0, 0))
    sd = jax.ShapeDtypeStruct
    return pl.pallas_call(
        weight_kernel,
        grid=(D // n,),
        in_specs=[feat] * 6 + [fix(C)] * 3 + [fix(wide)] + [fix(C)] * 4 + [fix(wide), pl.BlockSpec((tok, own), lambda i: (0, 0)), pl.BlockSpec((tok, n), lambda i: (0, i))],
        out_specs=[
            pl.BlockSpec((3, n, C), lambda i: (0, i, 0)),
            pl.BlockSpec((n, wide), lambda i: (i, 0)),
            pl.BlockSpec((C, wide), lambda i: (0, 0)),
            pl.BlockSpec((own, n), lambda i: (0, i)),
        ],
        out_shape=[sd((3, D, C), BF), sd((D, wide), BF), sd((C, wide), BF), sd((own, D), BF)],
        cost_estimate=takes(26),
        compiler_params=params(),
    )(*xm, *grads[:3], dd, *grads[3:], mid, z, dt)


TILE = 256


def mix_forward(x, meta, vec, sq, low, up):
    L, D = x.shape
    C = up.shape[0]
    wide = up.shape[1]
    tok = lambda n: pl.BlockSpec((TILE, n), lambda i: (i, 0))
    fix = lambda s: pl.BlockSpec(s, lambda i: (0,) * len(s))
    sd = jax.ShapeDtypeStruct
    out = pl.pallas_call(
        mix_forward_kernel,
        grid=(L // TILE,),
        in_specs=[tok(D), tok(meta.shape[1]), fix(vec.shape), fix(sq.shape), fix((D, wide)), fix(up.shape)],
        out_specs=[tok(D)] * 6 + [tok(C)] * 7 + [tok(wide)] * 2,
        out_shape=[sd((L, D), BF)] * 6 + [sd((L, C), F32)] * 7 + [sd((L, wide), F32), sd((L, wide), BF)],
        scratch_shapes=[pltpu.VMEM((8, D), F32)],
        cost_estimate=takes(30),
        compiler_params=params(),
    )(x, meta, vec, sq, low, up)
    return out[:6], out[6:13], out[13], out[14]


def mix_backward(grads, x, meta, mid, vec, sq, low, up):
    L, D = x.shape
    C = up.shape[0]
    wide = up.shape[1]
    n = L // TILE
    rev = lambda i: n - 1 - i
    tok = lambda m: pl.BlockSpec((TILE, m), lambda i: (rev(i), 0))
    fix = lambda s: pl.BlockSpec(s, lambda i: (0,) * len(s))
    above = pl.BlockSpec((16, D), lambda i: (jnp.maximum(rev(i) * (TILE // 16) - 1, 0), 0))
    sd = jax.ShapeDtypeStruct
    return pl.pallas_call(
        mix_backward_kernel,
        grid=(n,),
        in_specs=[tok(C)] * 7
        + [tok(D), above, tok(meta.shape[1]), tok(wide), fix(vec.shape), fix(sq.shape), fix((D, wide)), fix(up.shape)],
        out_specs=[tok(D), tok(wide), fix((8, D))],
        out_shape=[sd((L, D), BF), sd((L, wide), BF), sd((8, D), F32)],
        scratch_shapes=[pltpu.VMEM((8, D), F32), pltpu.VMEM((TILE, D), F32)],
        cost_estimate=takes(35),
        compiler_params=params(),
    )(*grads, x, x, meta, mid, vec, sq, low, up)


AXES = ("sa", "sb", "ra", "rc")
PLANE = ("sb", "ra", "rc")
MESH = pl.DeviceIdType.MESH
HBM = pl.BlockSpec(memory_space=pl.ANY)


class Net:
    def __init__(self, local_sem, send_sem, recv_sem):
        self.sems = local_sem, send_sem, recv_sem
        self.size = tuple(lax.axis_size(k) for k in AXES)
        self.me = tuple(lax.axis_index(k) for k in AXES)
        self.locals, self.n, self.k = [], 0, 0

    def at(self, shift):
        return tuple(lax.rem(m + d, n) if d else m for m, d, n in zip(self.me, shift, self.size))

    def greet(self, shifts):
        bar = pltpu.get_barrier_semaphore()
        for s in shifts:
            pl.semaphore_signal(bar, inc=1, device_id=self.at(s), device_id_type=MESH)
        pl.semaphore_wait(bar, len(shifts))

    def keep(self, src, dst):
        copy = pltpu.make_async_copy(src, dst, self.sems[0].at[self.k])
        self.k += 1
        copy.start()
        self.locals.append(copy)

    def send(self, src, dst, shift):
        copy = pltpu.make_async_remote_copy(
            src, dst, self.sems[1].at[self.n], self.sems[2].at[self.n], device_id=self.at(shift), device_id_type=MESH
        )
        self.n += 1
        copy.start()
        return copy

    def settle(self):
        for copy in self.locals:
            copy.wait()


def call_net(body, arrays, out_shapes, cid, n_local, n_send, scratch=()):
    n = len(arrays)
    m = n + len(out_shapes)

    def kernel(*refs):
        body(refs[:n], refs[n:m], refs[m + 3 :], Net(*refs[m : m + 3]))

    return pl.pallas_call(
        kernel,
        out_shape=out_shapes,
        in_specs=[HBM] * n,
        out_specs=[HBM] * len(out_shapes),
        scratch_shapes=[
            pltpu.SemaphoreType.DMA((max(n_local, 1),)),
            pltpu.SemaphoreType.DMA((n_send,)),
            pltpu.SemaphoreType.DMA((n_send,)),
            *scratch,
        ],
        compiler_params=pltpu.CompilerParams(collective_id=cid, has_side_effects=True, vmem_limit_bytes=VM),
    )(*arrays)


def line_shifts():
    return [(d, 0, 0, 0) for d in range(1, lax.axis_size("sa"))]


CHIPS = [(0, 1, 0, 0), (0, 0, 1, 0), (0, 1, 1, 0)]
OTHER_CORE = (0, 0, 0, 1)


class Gather:
    def __init__(self, net, src, view, half=None):
        self.net, self.src, self.view, self.half = net, src, view, half

    def slot(self, shift):
        return self.net.at(shift)[1:]

    def hand(self, view, shift):
        copy = self.net.send(view, view, shift)
        self.out.append(copy)
        return copy

    def first(self):
        net = self.net
        here = self.view(*net.me[1:])
        net.keep(self.src, here)
        self.near = [net.send(self.src, here, s) for s in CHIPS[:2]]
        self.far = [] if self.half else [net.send(self.src, here, CHIPS[2])]
        self.out = self.near + self.far
        self.core = [net.send(self.src, here, OTHER_CORE)]

    def to_core(self, shift):
        view = self.view(*self.slot(shift))
        self.core.append(self.net.send(view, view, OTHER_CORE))

    def second(self):
        for h, copy in enumerate(self.near):
            copy.wait_recv()
            if self.half:
                self.far.append(self.hand(self.half(*self.slot(CHIPS[h]), h), CHIPS[1 - h]))
            self.to_core(CHIPS[h])

    def third(self):
        for copy in self.far:
            copy.wait_recv()
        self.to_core(CHIPS[2])

    def end(self):
        for copy in self.out:
            copy.wait_send()
        for copy in self.core:
            copy.wait()


def gather_body(net, gathers):
    for step in ("second", "third", "end"):
        for g in gathers:
            getattr(g, step)()


def line_exchange(arrays, gathers, cid, shares=()):
    m = len(arrays)
    n = m + len(gathers)

    def body(ins, outs, _, net):
        shifts = line_shifts()
        net.greet(shifts + (plane_shifts() if shares else CHIPS[:2] + [OTHER_CORE] if gathers else []))
        a = net.me[0]
        open_ = []
        for x, o in zip(ins[:m], outs):
            open_ += [net.send(x.at[net.at(s)[0]], o.at[a], s) for s in shifts]
            net.keep(x.at[a], o.at[a])
        planes = [
            Gather(net, x, functools.partial(g[2], o), functools.partial(g[3], o))
            for x, o, g in zip(ins[m:], outs[m:], gathers)
        ]
        for g in planes:
            g.first()
        mine = net.me[1:]
        for x, o in zip(ins[n:], outs[n:]):
            open_ += [net.send(x.at[net.at(s)[1:]], o.at[mine], s) for s in plane_shifts()]
            net.keep(x.at[mine], o.at[mine])
        gather_body(net, planes)
        for copy in open_:
            copy.wait()
        net.settle()

    sd = jax.ShapeDtypeStruct
    shapes = [sd(x.shape, x.dtype) for x in arrays] + [sd(g[1], g[0].dtype) for g in gathers]
    shapes += [sd(x.shape, x.dtype) for x in shares]
    n_send = (lax.axis_size("sa") - 1) * m + 8 * len(gathers) + 7 * len(shares)
    operands = [*arrays, *(g[0] for g in gathers), *shares]
    return call_net(body, operands, shapes, cid, len(operands), n_send)


def rows_gather(x):
    sizes = tuple(lax.axis_size(k) for k in PLANE)
    half = x.shape[0] // 2
    return (
        x,
        sizes + x.shape,
        lambda o, b, y, c: o.at[b, y, c],
        lambda o, b, y, c, h: o.at[b, y, c, pl.ds(h * half, half)],
    )


def swap_first(net, x, o):
    b = net.me[1]
    net.keep(x.at[b], o.at[b])
    return [net.send(x.at[net.at(CHIPS[0])[1]], o.at[b], CHIPS[0])]


def plane_shifts():
    return [(0, i // 4, i // 2 % 2, i % 2) for i in range(1, 8)]


def start_exchange(tokens, sq, low, up, key, cid):
    A, B = lax.axis_size("sa"), lax.axis_size("sb")
    S, hops = A * B, A - 1
    sizes = tuple(lax.axis_size(k) for k in PLANE)
    n_fixed = 2 * hops + 8 + 8 + 7 + 7 + 1

    def body(ins, outs, scratch, net):
        x, q, lo, u, ke = ins
        xo, qo, loo, uo, ko, q_line, lo_line = outs
        line = line_shifts()
        net.greet(line + plane_shifts())
        a, b, y, c = net.me
        me = a * B + b
        ssem, rsem = net.sems[1:]

        def block(i, k):
            return xo.at[i * B + (b if k == 0 else 1 - b)]

        def index(way, t, k):
            return n_fixed + (way * hops + t) * 2 + k

        def origin(way, t):
            return a - t if way == 0 else a + t

        def have(way, t):
            return a >= t if way == 0 else a <= A - 1 - t

        def can(way):
            return a < A - 1 if way == 0 else a > 0

        def relay(way, t, k):
            dst = block(origin(way, t), k)
            i = index(way, t, k)
            to = (a + 1 if way == 0 else a - 1, b, y, c)
            src = x.at[b] if t == 0 and k == 0 else dst
            return pltpu.make_async_remote_copy(src, dst, ssem.at[i], rsem.at[i], device_id=to, device_id_type=MESH)

        def relay_start(t, k):
            for way in range(2):

                @pl.when(have(way, t) & can(way))
                def _(way=way):
                    relay(way, t, k).start()

        def relay_arrived(t, k):
            for way in range(2):

                @pl.when(have(way, t))
                def _(way=way):
                    dst, i = block(origin(way, t), k), index(way, t - 1, k)
                    pltpu.make_async_remote_copy(
                        dst, dst, ssem.at[i], rsem.at[i], device_id=net.at(OTHER_CORE), device_id_type=MESH
                    ).wait_recv()

        first = []
        for s in line:
            first.append(net.send(q.at[net.at(s)[0]], q_line.at[:, a], s))
            first.append(net.send(lo, lo_line.at[a], s))
        relay_start(0, 0)
        across = net.send(x.at[1 - b], xo.at[me], CHIPS[0])
        net.keep(q.at[a], q_line.at[:, a])
        net.keep(lo, lo_line.at[a])
        planes = [Gather(net, u, lambda i, j, k: uo.at[i, j, k])]
        planes[0].first()
        across.wait_recv()
        relay_start(0, 1)
        for copy in first:
            copy.wait()
        net.settle()
        net.locals = []
        net.keep(x.at[b], xo.at[me])
        h = A // 2
        planes.append(
            Gather(net, q_line, lambda i, j, k: qo.at[:, :, i, j, k], lambda i, j, k, p: qo.at[:, pl.ds(p * h, h), i, j, k])
        )
        planes.append(Gather(net, lo_line, lambda i, j, k: loo.at[:, i, j, k], lambda i, j, k, p: loo.at[pl.ds(p * h, h), i, j, k]))
        planes[1].first()
        planes[2].first()
        mine = net.me[1:]
        rest = [net.send(ke.at[net.at(s)[1:]], ko.at[mine], s) for s in plane_shifts()]
        net.keep(ke.at[mine], ko.at[mine])
        for t in range(1, hops):
            for k in range(2):
                relay_arrived(t, k)
                relay_start(t, k)
            if t == 1:
                for g in planes:
                    g.second()
        for g in planes:
            g.third()
        for k in range(2):
            relay_arrived(hops, k)
        for t in range(hops):
            for k in range(2):
                for way in range(2):

                    @pl.when(have(way, t) & can(way))
                    def _(way=way, t=t, k=k):
                        relay(way, t, k).wait_send()

        across.wait_send()
        for g in planes:
            g.end()
        for copy in rest:
            copy.wait()
        net.settle()

    sd = lambda shape, like: jax.ShapeDtypeStruct(shape, like.dtype)
    shapes = [
        sd((S,) + tokens.shape[1:], tokens),
        sd(sq.shape[1:2] + (A,) + sizes + sq.shape[2:], sq),
        sd((A,) + sizes + low.shape, low),
        sd(sizes + up.shape, up),
        sd(key.shape, key),
        sd(sq.shape[1:2] + (A,) + sq.shape[2:], sq),
        sd((A,) + low.shape, low),
    ]
    return call_net(body, [tokens, sq, low, up, key], shapes, cid, 9, n_fixed + 4 * hops)[:5]


def tail_exchange(dh, sq3, sq, down, wide, up, narrow, ffn, cid):
    A = lax.axis_size("sa")
    leads = [2, 1, 1, 0, 0, 0]
    halved = [1, 0, 0, None, None, 0]
    arrays = [sq, down, wide, up, narrow, ffn]
    blocks = [x.shape[:n] + x.shape[n + 3 :] for x, n in zip(arrays, leads)]
    n = len(arrays)

    def body(ins, outs, scratch, net):
        ps, pos = ins[2:], outs[2:]
        own, other, chips = scratch[:n], scratch[n : 2 * n], scratch[2 * n :]
        line = line_shifts()
        net.greet(line + CHIPS + [OTHER_CORE])
        a, b, y, c = net.me
        there = net.at(OTHER_CORE)[3]
        pairs = [(i // 2, i % 2) for i in range(4)]

        def block(t, i, j, k):
            return ps[t].at[(slice(None),) * leads[t] + (i, j, k)]

        cores, mine = [], []
        for t in range(n):
            cores.append([net.send(block(t, i, j, there), other[t].at[2 * i + j], OTHER_CORE) for i, j in pairs])
            for i, j in pairs:
                net.keep(block(t, i, j, c), own[t].at[2 * i + j])
            mine.append(net.locals)
            net.locals = []
        open_ = []
        for x, o in zip(ins[:2], outs[:2]):
            open_ += [net.send(x.at[net.at(s)[0]], o.at[a], s) for s in line]
            net.keep(x.at[a], o.at[a])

        def part(t, h):
            if h is None or halved[t] is None:
                return ()
            size = blocks[t][halved[t]] // 2
            return (slice(None),) * halved[t] + (pl.ds(h * size, size),)

        def add(t, k, terms, h=None):
            shape, start = list(blocks[t]), [0] * len(blocks[t])
            if h is not None:
                shape[halved[t]] //= 2
                start[halved[t]] = h * shape[halved[t]]
            step = min(shape[-2], 16)
            per = shape[-2] // step
            count = per
            for size in shape[:-2]:
                count = count * size

            @pl.loop(0, count)
            def _(r):
                index = []
                rest = r // per
                for size, first in zip(reversed(shape[:-2]), reversed(start[:-2])):
                    index.insert(0, first + rest % size)
                    rest = rest // size
                at = (*index, pl.ds(pl.multiple_of(start[-2] + r % per * step, step), step))
                total = own[t][(k, *at)].astype(F32)
                for ref, i in terms:
                    total = total + ref[(i, *at)].astype(F32)
                own[t][(k, *at)] = total.astype(BF)

        def slot(i, j):
            return 2 * i + j

        nb, ny = net.at(CHIPS[0])[1], net.at(CHIPS[1])[2]
        ways = [
            (CHIPS[0], CHIPS[1], lambda j: slot(nb, j), lambda j: slot(b, j), slot(b, ny)),
            (CHIPS[1], CHIPS[0], lambda j: slot(j, ny), lambda j: slot(j, y), slot(nb, y)),
        ]
        me = slot(b, y)
        sent = [[] for _ in range(n)]
        for t in range(n):
            for copy in cores[t] + mine[t]:
                copy.wait()
            for k in range(4):
                add(t, k, [(other[t], k)])
            if halved[t] is None:
                for k, s in enumerate(CHIPS):
                    to = net.at(s)
                    sent[t].append(net.send(own[t].at[slot(to[1], to[2])], chips[t].at[k], s))
                continue
            for h, (s, _, theirs, _, _) in enumerate(ways):
                for j in range(2):
                    src, dst = own[t].at[(theirs(j), *part(t, h))], chips[t].at[(j, *part(t, h))]
                    sent[t].append(net.send(src, dst, s))
        second = [[] for _ in range(n)]
        for t in range(n):
            if halved[t] is None:
                continue
            for h, (_, s, _, ours, across) in enumerate(ways):
                for j in range(2):
                    sent[t][2 * h + j].wait_recv()
                    add(t, ours(j), [(chips[t], j)], h)
                src, dst = own[t].at[(across, *part(t, h))], chips[t].at[(2, *part(t, h))]
                second[t].append(net.send(src, dst, s))
        for t in range(n):
            for copy in second[t] if second[t] else sent[t]:
                copy.wait_recv()
            if halved[t] is None:
                add(t, me, [(chips[t], k) for k in range(3)])
            else:
                add(t, me, [(chips[t], 2)])
            net.keep(own[t].at[me], pos[t])
        for t in range(n):
            for copy in sent[t] + second[t]:
                copy.wait_send()
        for copy in open_:
            copy.wait()
        net.settle()

    sd = jax.ShapeDtypeStruct
    shapes = [sd(dh.shape, BF), sd(sq3.shape, BF)] + [sd(s, BF) for s in blocks]
    scratch = [pltpu.VMEM((m,) + s, BF) for m in (4, 4, 3) for s in blocks]
    n_send = 2 * (A - 1) + 10 * n
    return call_net(body, [dh, sq3, *arrays], shapes, cid, 2 + 5 * n, n_send, scratch)


def last_exchange(swaps, sq, lines, key, cid):
    m = len(swaps)
    n = m + 1 + len(lines)

    def body(ins, outs, _, net):
        line, plane = line_shifts(), plane_shifts()
        net.greet(line + plane)
        a = net.me[0]
        mine = net.me[1:]
        open_ = []
        for i, (x, o) in enumerate(zip(ins[:n], outs)):
            if i < m:
                open_ += swap_first(net, x, o)
                continue
            view = (lambda x, k: x.at[:, k]) if i == m else (lambda x, k: x.at[k])
            open_ += [net.send(view(x, net.at(s)[0]), o.at[a], s) for s in line]
            net.keep(view(x, a), o.at[a])
        open_ += [net.send(ins[n].at[net.at(s)[1:]], outs[n].at[mine], s) for s in plane]
        net.keep(ins[n].at[mine], outs[n].at[mine])
        for copy in open_:
            copy.wait()
        net.settle()

    sd = jax.ShapeDtypeStruct
    arrays = [*swaps, sq, *lines, key]
    shapes = [sd(x.shape, x.dtype) for x in arrays]
    shapes[m] = sd((sq.shape[1], sq.shape[0]) + sq.shape[2:], sq.dtype)
    n_send = m + (1 + len(lines)) * (lax.axis_size("sa") - 1) + 7
    return call_net(body, arrays, shapes, cid, len(arrays), n_send)


def layer_norm(x, gain, bias):
    cen = x - jnp.mean(x, axis=-1, keepdims=True)
    var = jnp.mean(cen * cen, axis=-1, keepdims=True)
    return cen * lax.rsqrt(var + 1e-05) * gain + bias


def next_line(value, steps):
    count = lax.axis_size("sa")
    first, last = max(0, -steps), min(count, count - steps)
    return lax.ppermute(value, "sa", [(i, i + steps) for i in range(first, last)])


def after(value, *others):
    return lax.optimization_barrier((value, *others))[0]


def per_device(tokens, first_values, lengths, vectors, down, up, square, key_w, value_w, out_grad):
    rows_here, seg, D = tokens.shape
    SA, SB, RA, RC = (lax.axis_size(k) for k in AXES)
    a, b = lax.axis_index("sa"), lax.axis_index("sb")
    S, F = SA * SB, SB * RA * RC
    L = seg * S
    C = D // SA
    NB = L // BLK
    gc = min(C, 256)
    T = SB * seg
    w = square.shape[1]
    n_low, n_vec = down.shape[1], vectors.shape[0]
    FS = key_w.shape[1] // (S * RA * RC)

    lens = lax.dynamic_index_in_dim(lengths, b, 0, keepdims=False)
    count = lens.shape[0]
    lower = jnp.arange(count)[:, None] > jnp.arange(count)[None, :]
    starts = jnp.sum(jnp.where(lower, lens[None, :], 0), axis=1)
    pos = jnp.arange(L, dtype=jnp.int32)
    reset = jnp.any(pos[:, None] == starts[None, :], axis=1).astype(F32)
    segid = jnp.sum((pos[:, None] >= starts[None, :]).astype(F32), axis=1) - 1.0
    blocks = segid.reshape(NB, BLK)
    before = blocks[:, :1] - reset.reshape(NB, BLK)[:, :1]
    carried = (blocks == before).astype(F32).reshape(L)
    live = (blocks == blocks[:, -1:]).astype(F32).reshape(L)
    meta = jnp.stack([segid, carried, live, 1.0 - reset], axis=1)
    segrow = jnp.tile(blocks.reshape(NB, 1, BLK), (1, 1, gc // SD))
    keep_row = (1.0 - reset)[:, None]
    keep_own = lax.dynamic_slice(keep_row, (a * T, 0), (T, 1))

    first_sliced = first_values.reshape(rows_here, seg, SA, C).transpose(2, 0, 1, 3).reshape(S, seg, C)
    first_row = lax.all_to_all(first_sliced, ("sa", "sb"), split_axis=0, concat_axis=0, tiled=True).reshape(L, C)
    cuts = [0, DECAY_INNER, DECAY_INNER + LA, DECAY_INNER + LA + LV, n_low]

    wide_at = [0, 128, 256, 384]
    spot = jnp.concatenate([at + jnp.arange(q - p) for at, p, q in zip(wide_at, cuts[:-1], cuts[1:])])
    place = (spot[:, None] == jnp.arange(768)[None, :]).astype(BF)
    place_vec = (640 + jnp.arange(n_vec)[:, None] == jnp.arange(768)[None, :]).astype(BF)
    low_mine = (mm(down, place, NN) + mm(vectors, place_vec, TN)).astype(BF)
    up_mine = mm(up, place[:, :640], TN).astype(BF)
    sq_mine = square[:3].reshape(3, w, SA, C).transpose(2, 0, 1, 3)
    half = SA * FS
    key_mine = key_w.reshape(w, SA, F, FS).transpose(2, 0, 1, 3).reshape(SB, RA, RC, w, half)
    x_row, sq, low, up_heads, key_line = start_exchange(tokens, sq_mine, low_mine, up_mine, key_mine, 1)
    sq3 = lax.all_gather(after(square[3], x_row), AXES, axis=0, tiled=True)
    x_row = x_row.reshape(L, D)
    sq = sq.reshape(3, D, C)
    low = low.reshape(D, 768)
    up_w = up_heads.reshape(C, 640)
    vec = low[:, 640 : 640 + n_vec].astype(F32).T
    vec_heads = lax.dynamic_slice(vec, (10, a * C), (8, C))
    FW = F * w
    halves = [slice(i * half, (i + 1) * half) for i in range(D // half)]
    kv = jnp.concatenate([key_line.reshape(FW, half), *(value_w[:, s] for s in halves)], axis=0)

    xm, (rp, kp, vp, uw, ua, uv, ug), mid, mid_low = mix_forward(x_row, meta, vec, sq, low, up_w)
    ins = (rp, kp, vp, uw, ua, uv, first_row)
    y, saved = recurrence_forward(ins, vec_heads, meta, segrow)
    kv_all = lax.all_gather(after(kv, sq3, saved[9]), "sa", axis=0)
    key_all = kv_all[:, :FW].reshape(D, half)
    value_all = jnp.concatenate(
        [kv_all[:, FW + i * FS : FW + (i + 1) * FS].reshape(half, half) for i in range(D // half)], axis=1
    )
    z = (y.astype(F32) * ug).astype(BF)
    before = jnp.concatenate([jnp.zeros((1, 16, C), BF), z.reshape(SA, T, C)[:-1, T - 16 :]], axis=0)
    z_blocks = jnp.concatenate([before, z.reshape(SA, T, C)], axis=1)
    gather_g = (
        out_grad,
        (SB, RA, RC, SB, seg, D),
        lambda o, i, j, k: o.at[:, j, k, i],
        lambda o, i, j, k, h: o.at[h, j, k, i],
    )
    z_own, g_all = line_exchange([z_blocks], [gather_g], 2)
    g_all = g_all.reshape(F * T, D)
    z_more = z_own.transpose(1, 0, 2).reshape(T + 16, D)
    z_own = z_more[16:]
    z_share = z_own.reshape(T, SA, F, w).transpose(2, 0, 1, 3).reshape(SB, RA, RC, T, SA * w)

    x_own = lax.dynamic_slice(x_row, (a * T, 0), (T, D)).astype(F32)
    x_before = lax.dynamic_slice(x_row, (jnp.maximum(a * T - 16, 0), 0), (16, D)).astype(F32)
    x1_more = jnp.concatenate([x_before, x_own], axis=0) + mm(z_more, sq3, NN)
    x1 = x1_more[16:]
    h2, norm2_pull = jax.vjp(layer_norm, x1, vec[2], vec[3])
    edge2 = layer_norm(x1_more[15:16], vec[2], vec[3])

    def channel_mix(h, edge, mix):
        s = jnp.concatenate([edge, h[:-1]], axis=0) * keep_own
        return h + (s - h) * mix

    xc, cmix_pull = jax.vjp(channel_mix, h2, edge2, vec[18])
    (xc_all,) = line_exchange([], [rows_gather(xc.astype(BF))], 3)
    xc_all = xc_all.reshape(F * T, D)
    q, dkc, dxc_part = hidden(xc_all, g_all, key_all, value_all)
    dxc = lax.psum_scatter(dxc_part, PLANE, scatter_dimension=0, tiled=True)
    ffn_part = mm(q, value_all, NN).astype(BF)
    value_part = mm(q, g_all, TN).astype(BF).reshape(SA, FS, D)
    key_part = mm(xc_all, dkc, TN).astype(BF).reshape(SA, FW, half)
    kv_part = jnp.concatenate([key_part, *(value_part[:, :, s] for s in halves)], axis=1)
    dxc, kv_part, ffn_part = lax.optimization_barrier((dxc, kv_part, ffn_part))

    dh2, dedge2, g18 = cmix_pull(dxc.astype(F32))
    dh2 = dh2.at[-1:].add(next_line(dedge2, -1))
    dx1n, g2, g3 = norm2_pull(dh2)
    slot = (b * RA + lax.axis_index("ra")) * RC + lax.axis_index("rc")
    dx1 = lax.dynamic_slice(g_all, (slot * T, 0), (T, D)).astype(F32) + dx1n
    dt = dx1.astype(BF)
    dz = mm(dt, sq3, NT).astype(BF)
    dz_row, dt_all, z_share = line_exchange(
        [dz.reshape(T, SA, C).transpose(1, 0, 2)], [rows_gather(dt)], 4, [z_share]
    )
    kv_grad = lax.psum_scatter(kv_part.reshape(-1, half), "sa", scatter_dimension=0, tiled=True)
    dz_row = dz_row.reshape(L, C).astype(F32)

    dy = (dz_row * ug).astype(BF)
    dug = (dz_row * y.astype(F32)).astype(BF)
    drp, dkp, dvp, duw, dua, duv, dfl, dvec = recurrence_backward(dy, saved, ins, vec_heads, meta, segrow)
    dfl = lax.all_to_all(dfl.reshape(S, seg, C), ("sa", "sb"), split_axis=0, concat_axis=0, tiled=True)
    dh1, dd, gmix = mix_backward((drp, dkp, dvp, duw, dua, duv, dug), x_row, meta, mid, vec, sq, low, up_w)
    g0, g1 = gmix[6], gmix[7]

    sq_part, down_part, up_part, sq3_part = weight_grads(
        xm, (drp, dkp, dvp, duw, dua, duv, dug), dd, mid_low, z_share.reshape(F * T, SA * w), dt_all.reshape(F * T, D)
    )
    dfl, sq_part = lax.optimization_barrier((dfl, sq_part))
    first_grad = dfl.reshape(SA, SB, seg, C).transpose(1, 2, 0, 3).reshape(rows_here, seg, D)
    wide = jnp.stack([g0, g1, g2, g3, *(gmix[i] for i in range(6)), g18] + [jnp.zeros_like(g0)] * 5).astype(BF)
    wide = jnp.pad(wide.T, ((0, 0), (0, 112)))
    narrow = jnp.pad(dvec.astype(BF).T, ((0, 0), (0, 120)))
    plane = (SB, RA, RC, w)
    dh1_own, sq3_sum, sq_sum, down_sum, wide_sum, up_sum, narrow_sum, ffn = tail_exchange(
        dh1.reshape(SA, T, D),
        sq3_part.reshape(SA, w, D),
        sq_part.reshape((3, SA) + plane + (C,)),
        down_part.reshape((SA,) + plane + (640,)),
        wide.reshape((SA,) + plane + (128,)),
        up_part.reshape(plane + (640,)),
        narrow.reshape(plane + (128,)),
        ffn_part.reshape(SB, RA, RC, T, D),
        5,
    )
    dh1_own = jnp.sum(dh1_own.astype(F32), axis=0)
    _, norm1_pull = jax.vjp(lambda x: layer_norm(x, vec[0], vec[1]), x_own)
    (dx0,) = norm1_pull(dh1_own)
    mixed = (x1 + ffn.astype(F32)).astype(BF)
    tokens_grad, mixed_out, sq_sum, down_sum, wide_sum, key_grad = last_exchange(
        [(dx1 + dx0).astype(BF).reshape(SB, seg, D), mixed.reshape(SB, seg, D)],
        sq_sum,
        [down_sum, wide_sum],
        kv_grad[:FW].reshape(SB, RA, RC, w, half),
        6,
    )
    sq3_sum = jnp.sum(sq3_sum.astype(F32), axis=0)
    square_grad = jnp.concatenate([sq_sum.transpose(1, 2, 0, 3).reshape(3, w, D).astype(F32), sq3_sum[None]], axis=0)
    narrow_pieces = lambda m: [m[:, i : i + q - p] for i, p, q in zip(wide_at, cuts[:-1], cuts[1:])]
    down_grad = jnp.concatenate(narrow_pieces(jnp.sum(down_sum.astype(F32), axis=0)), axis=1)
    up_grad = jnp.concatenate(narrow_pieces(up_sum.astype(F32)), axis=1).T
    wide_t = jnp.sum(wide_sum.astype(F32), axis=0)[:, :16].T
    narrow_t = narrow_sum[:, :8].astype(F32).T
    vectors_gradient = jnp.concatenate([wide_t[:10], narrow_t, wide_t[10:11]], axis=0)
    value_grad = jnp.concatenate([kv_grad[FW + i * FS : FW + (i + 1) * FS] for i in range(D // half)], axis=1)
    value_grad = value_grad.astype(F32)
    key_grad = key_grad.reshape(F, w, SA, FS).transpose(1, 2, 0, 3).reshape(w, -1).astype(F32)
    return (
        mixed_out,
        tokens_grad,
        first_grad,
        vectors_gradient,
        down_grad,
        up_grad,
        square_grad,
        key_grad,
        value_grad,
    )


def solution(mesh):
    seq, row = mesh.shape["seq"], mesh.shape["row"]
    fine = Mesh(mesh.devices.reshape(seq // 2, 2, row // 2, 2), AXES)
    S, R = ("sa", "sb"), ("ra", "rc")
    in_specs = (
        P(R, S, None),
        P(R, S, None),
        P(R, None),
        P(None, S + R),
        P(S + R, None),
        P(None, S + R),
        P(None, S + R, None),
        P(S + R, None),
        P(S + R, None),
        P(R, S, None),
    )
    out_specs = (
        P(R, S, None),
        P(R, S, None),
        P(R, S, None),
        P(None, S + R),
        P(S + R, None),
        P(None, S + R),
        P(None, S + R, None),
        P(S + R, None),
        P(S + R, None),
    )
    return jax.shard_map(per_device, mesh=fine, in_specs=in_specs, out_specs=out_specs, check_vma=False)
```

```python
import functools

import jax
import jax.numpy as jnp
from jax import lax
from jax.experimental import pallas as pl
from jax.experimental.pallas import tpu as pltpu
from jax.sharding import Mesh, PartitionSpec as P

DECAY_INNER = 96
LA = 96
LV = 64

BF=jnp.bfloat16; F32=jnp.float32
SD=64; BLK=64
NN=(((1,),(0,)),((),())); NT=(((1,),(1,)),((),())); TN=(((0,),(0,)),((),()))

def mm(a,b,d): return lax.dot_general(a,b,d,preferred_element_type=F32)

class Geo:
    def __init__(s, gc):
        s.gc=gc; s.gh=gc//SD
        lane=lax.broadcasted_iota(jnp.int32,(1,gc),1)
        s.head=lane//SD
        s.lm=[(s.head==h).astype(BF) for h in range(s.gh)]
        row=lax.broadcasted_iota(jnp.int32,(BLK,gc),0)
        col=lax.broadcasted_iota(jnp.int32,(BLK,gc),1)%SD
        s.below=row>col; s.upto=row>=col
    def blk(s,x):
        return jnp.concatenate([x*m for m in s.lm],axis=0) if s.gh>1 else x
    def ext(s,x):
        out=x[:BLK]
        for h in range(1,s.gh):
            out=jnp.where(s.head==h,x[h*BLK:(h+1)*BLK],out)
        return out

def headsums(ones, *xs):
    hi = [x.astype(BF) for x in xs]
    lo = [(x - h.astype(F32)).astype(BF) for x, h in zip(xs, hi)]
    s = mm(jnp.concatenate(hi + lo, axis=0), ones, NN)
    n = len(xs) * BLK
    return [s[i * BLK : (i + 1) * BLK] + s[n + i * BLK : n + (i + 1) * BLK] for i in range(len(xs))]

def decayed(geo,ws,tri):
    w=ws.astype(F32)
    cum=mm(tri,ws,NN)
    return w,cum,jnp.exp(cum-w),jnp.exp(cum),jnp.exp(-cum)

def first_block(rp,kp,vp,uw,ua,uv,fl,vec,meta,segrow,tri,ones,rs,ws,ks,vs,qs,as_,ri_out,ab):
    C=rp.shape[1]; gc=min(C,256); geo=Geo(gc)
    same=meta[:,0:1]==segrow[0]
    strict=geo.below&same
    for g in range(C//gc):
        sl=slice(g*gc,(g+1)*gc)
        V=lambda i: vec[i:i+1,sl]
        k0=kp[:,sl]; v0=vp[:,sl]
        lw=-0.606531*jax.nn.sigmoid(V(0)+uw[:,sl])
        al=jax.nn.sigmoid(V(1)+ua[:,sl])
        vm=jax.nn.sigmoid(V(2)+uv[:,sl])
        v=v0+(fl[:,sl].astype(F32)-v0)*vm
        kn=k0*V(3)
        ri=lax.rsqrt(headsums(ones[...],kn*kn)[0]+1e-6)
        ri_out[:,sl]=ri
        kk=kn*ri
        km=k0*(1.0+(al-1.0)*V(4))
        q_=kk.astype(BF); w_=lw.astype(BF); a_=al.astype(BF)
        rs[:,sl]=rp[:,sl].astype(BF); ws[:,sl]=w_; ks[:,sl]=km.astype(BF)
        vs[:,sl]=v.astype(BF); qs[:,sl]=q_; as_[:,sl]=a_
        w,cum,eP,eC,eN=decayed(geo,w_,tri[...])
        q=q_.astype(F32)
        qu=(q*eP).astype(BF); bb=(q*a_.astype(F32)*eN).astype(BF)
        put128(ab,g,jnp.where(strict,mm(qu,geo.blk(bb),NT),0.0))

def put128(ref, g, x):
    if x.shape[1] < 128:
        x = jnp.concatenate([x, jnp.zeros_like(x)], axis=1)
    n = x.shape[1] // 128
    for k in range(n):
        ref[g * n + k] = x[:, k * 128 : (k + 1) * 128]


def get128(ref, g, gc):
    n = max(gc // 128, 1)
    x = jnp.concatenate([ref[g * n + k] for k in range(n)], axis=1) if n > 1 else ref[g]
    return x[:, :gc].astype(BF)


def solve_kernel(ab, tt, a, t):
    G, L, _ = ab.shape
    NB = L // BLK
    B = NB * G * 2

    @pl.loop(0, BLK, unroll=8)
    def _(i):
        rows = [ab[g, pl.ds(i, NB, stride=BLK), :] for g in range(G)]
        a[i] = jnp.concatenate([r[:, k * SD : (k + 1) * SD] for r in rows for k in range(2)], axis=0).T

    t[...] = jnp.zeros_like(t)
    cidx = lax.broadcasted_iota(jnp.int32, (SD, B), 0)

    @pl.loop(0, BLK)
    def _(i):
        def inner(jb, acc):
            for jj in range(8):
                j = jb * 8 + jj
                acc = acc - a[i, pl.ds(j, 1), :] * t[j]
            return acc

        t[i] = lax.fori_loop(0, i // 8 + 1, inner, (cidx == i).astype(F32))

    @pl.loop(0, BLK, unroll=8)
    def _(i):
        rows = t[i].T
        for g in range(G):
            pair = [rows[(2 * g + k) * NB : (2 * g + k + 1) * NB] for k in range(2)]
            tt[g, pl.ds(i, NB, stride=BLK), :] = jnp.concatenate(pair, axis=1)


def forward_block(rs,ws,ks,vs,qs,as_,tt,vec,meta,segrow,tri,ones,y,nrm_out,rstd_out,extra_out,u_out,al_out,lb_out,s_out,state):
    C=rs.shape[1]; gc=min(C,256); geo=Geo(gc)
    same=meta[:,0:1]==segrow[0]
    carried=meta[:,1:2]; live=meta[:,2:3]; last=meta[BLK-1:BLK,1:2]
    strict=geo.below&same; incl=geo.upto&same
    for g in range(C//gc):
        sl=slice(g*gc,(g+1)*gc)
        V=lambda i: vec[i:i+1,sl]
        w,cum,eP,eC,eN=decayed(geo,ws[:,sl],tri[...])
        q=qs[:,sl].astype(F32); r=rs[:,sl].astype(F32); k=ks[:,sl].astype(F32)
        vb=vs[:,sl]; v=vb.astype(F32); a=as_[:,sl].astype(F32)
        qq=jnp.concatenate([(q*eP).astype(BF),(r*eC).astype(BF)],axis=0)
        kb=(k*eN).astype(BF); bb=(q*a*eN).astype(BF)
        mk=mm(qq,geo.blk(kb),NT)
        al=jnp.concatenate([jnp.where(strict,mk[:BLK],0.0).astype(BF),jnp.where(incl,mk[BLK:],0.0).astype(BF)],axis=0)
        lb=jnp.where(incl,mm(qq[BLK:],geo.blk(bb),NT),0.0).astype(BF)
        s0=state[g]; sb=s0.astype(BF)
        s_out[0,g]=sb
        qst=mm(qq,sb,NT)
        av=mm(al,geo.blk(vb),NN)
        rhs=carried*qst[:BLK]+av[:BLK]
        u=mm(get128(tt,g,gc),geo.blk(rhs.astype(BF)),NN)
        ub=u.astype(BF)
        u_out[:,sl]=ub
        o=carried*qst[BLK:]+av[BLK:]-mm(lb,geo.blk(ub),NN)
        vu=jnp.concatenate([(v*live).astype(BF),(u*(-live)).astype(BF)],axis=0)
        ds=mm(vu,jnp.concatenate([kb,bb],axis=0),TN)
        tail=eC[BLK-1:BLK]
        state[g]=(last*s0+ds*ones[...].astype(F32))*tail
        al_out[:,sl]=al; lb_out[:,sl]=lb
        mean,extra=headsums(ones[...],o,r*k*V(5))
        cen=o-mean*(1.0/SD)
        rstd=lax.rsqrt(headsums(ones[...],cen*cen)[0]*(1.0/SD)+1.0)
        nrm=cen*rstd
        nrm_out[:,sl]=nrm; rstd_out[:,sl]=rstd; extra_out[:,sl]=extra
        y[:,sl]=(nrm*V(6)+V(7)+extra*v).astype(BF)

def backward_block(dy,nrm_in,rstd_in,extra_in,rs,ws,ks,vs,qs,as_,tt,u_in,al_in,lb_in,s_in,ri_in,rp,kp,vp,uw,ua,uv,fl,vec,meta,segrow,tri,tru,ones,
                    drp,dkp,dvp,duw,dua,duv,dfl,dvec,state):
    C=rs.shape[1]; gc=min(C,256); geo=Geo(gc)
    same=meta[:,0:1]==segrow[0]
    carried=meta[:,1:2]; live=meta[:,2:3]; last=meta[BLK-1:BLK,1:2]
    strict=geo.below&same; incl=geo.upto&same
    cat=lambda *x: jnp.concatenate(x,axis=0)
    rsum=lambda x: jnp.sum(x,axis=0,keepdims=True)
    for g in range(C//gc):
        sl=slice(g*gc,(g+1)*gc)
        V=lambda i: vec[i:i+1,sl]
        on=ones[...]
        w,cum,eP,eC,eN=decayed(geo,ws[:,sl],tri[...])
        q=qs[:,sl].astype(F32); r=rs[:,sl].astype(F32); k=ks[:,sl].astype(F32)
        vb=vs[:,sl]; v=vb.astype(F32); a=as_[:,sl].astype(F32)
        d=dy[:,sl].astype(F32); nrm=nrm_in[:,sl]; extra=extra_in[:,sl]
        dn=d*V(6)
        de,dn1,dn2=headsums(on,d*v,dn,dn*nrm)
        do=rstd_in[:,sl]*(dn-dn1*(1.0/SD)-nrm*(dn2*(1.0/SD)))
        g17=rsum(d); g16=rsum(d*nrm); g15=rsum(de*r*k)
        dr=de*k*V(5); dk=de*r*V(5); dv=d*extra
        qq=cat((q*eP).astype(BF),(r*eC).astype(BF))
        kb=(k*eN).astype(BF); bb=(q*a*eN).astype(BF)
        kblk=geo.blk(kb); bblk=geo.blk(bb)
        al=al_in[:,sl]; lb=lb_in[:,sl]
        ub=u_in[:,sl]; s0=s_in[0,g]
        tail=eC[BLK-1:BLK]
        ds1=state[g]*tail; dsb=ds1.astype(BF)
        kbs=mm(cat(kb,bb),dsb,NT)
        dob=do.astype(BF)
        du=-geo.ext(mm(lb,dob,TN))-live*kbs[BLK:]
        yy=geo.ext(mm(get128(tt,g,gc),du.astype(BF),TN))
        yo=cat(yy.astype(BF),dob)
        cyo=cat((carried*yy).astype(BF),(carried*do).astype(BF))
        mv=mm(yo,geo.blk(vb),NT); mu=mm(yo,geo.blk(ub),NT)
        dkm=cat(jnp.where(strict,mv[:BLK],0.0).astype(BF),jnp.where(incl,mv[BLK:],0.0).astype(BF))
        dbm=cat(jnp.where(strict,-mu[:BLK],0.0).astype(BF),jnp.where(incl,-mu[BLK:],0.0).astype(BF))
        dqq=mm(cyo,s0,NN)+mm(dkm,kblk,NN)+mm(dbm,bblk,NN)
        vus=mm(cat(vb,ub),dsb,NN)
        kst=live*vus[:BLK]; bst=-(live*vus[BLK:])
        dkb=geo.ext(mm(dkm,qq,TN))+kst
        dbb=geo.ext(mm(dbm,qq,TN))+bst
        dv=dv+geo.ext(mm(al,yo,TN))+live*kbs[:BLK]
        kf=kb.astype(F32); bf=bb.astype(F32); qf=qq.astype(F32)
        dlast=last*rsum(ds1*s0.astype(F32))+rsum(kf*kst+bf*bst)
        state[g]=mm(cyo,qq,TN)*on.astype(F32)+last*ds1
        dqu=dqq[:BLK]*qf[:BLK]
        dcum=dqu+dqq[BLK:]*qf[BLK:]-dkb*kf-dbb*bf
        hi=dcum.astype(BF); rest=dcum-hi.astype(F32); lo=rest.astype(BF)
        lo2=(rest-lo.astype(F32)).astype(BF)
        dw=mm(tru[...],hi,NN)+mm(tru[...],lo,NN)+mm(tru[...],lo2,NN)+dlast-dqu
        dben=dbb*eN
        dq=dqq[:BLK]*eP+dben*a
        da=dben*q
        dr=dr+dqq[BLK:]*eC
        dk=dk+dkb*eN
        k0=kp[:,sl]; v0=vp[:,sl]
        sg=jax.nn.sigmoid(V(0)+uw[:,sl]); af=jax.nn.sigmoid(V(1)+ua[:,sl]); vm=jax.nn.sigmoid(V(2)+uv[:,sl])
        kn=k0*V(3)
        ri=ri_in[:,sl]
        kk=kn*ri
        gw=(-0.606531)*dw*sg*(1.0-sg)
        gv=dv*(fl[:,sl].astype(F32)-v0)*vm*(1.0-vm)
        da=da+dk*k0*V(4)
        ga=da*af*(1.0-af)
        dkn=ri*(dq-kk*headsums(on,dq*kk)[0])
        drp[:,sl]=dr.astype(BF)
        dkp[:,sl]=(dk*(1.0+(af-1.0)*V(4))+dkn*V(3)).astype(BF)
        dvp[:,sl]=(dv*(1.0-vm)).astype(BF)
        duw[:,sl]=gw.astype(BF); dua[:,sl]=ga.astype(BF); duv[:,sl]=gv.astype(BF)
        dfl[:,sl]=(dv*vm).astype(BF)
        dvec[:,sl]+=cat(rsum(gw),rsum(ga),rsum(gv),rsum(dkn*k0),rsum(dk*k0*(af-1.0)),g15,g16,g17)

def per_block(ref, kind, i):
    if kind is None:
        return ref
    size = {"n": 1, "pair": 2 * BLK}.get(kind, BLK)
    at = pl.ds(i * size, size)
    return ref.at[:, at] if kind == "inv" else ref.at[at]


def blocks_kernel(body, kinds, order, zeroed, *refs):
    @pl.when(pl.program_id(0) == 0)
    def _():
        for i in zeroed:
            refs[i][...] = jnp.zeros_like(refs[i])

    for i in order:
        body(*(per_block(r, k, i) for r, k in zip(refs, kinds)))


def consts(C):
    gc=min(C,256)
    i=jnp.arange(BLK); tri=(i[:,None]>=i[None,:]).astype(BF); tru=(i[:,None]<=i[None,:]).astype(BF)
    j=jnp.arange(gc)//SD; ones=(j[:,None]==j[None,:]).astype(BF)
    return tri,tru,ones

VM=60*2**20
def takes(us): return pl.CostEstimate(flops=int(us*6e8), bytes_accessed=1<<20, transcendentals=0)
UNROLL=2
def params(): return pltpu.CompilerParams(vmem_limit_bytes=VM)

def recurrence_forward(ins, vec, meta, segrow):
    L, C = ins[0].shape
    NB, gc = L // BLK, min(C, 256)
    G = C // gc
    tri, tru, ones = consts(C)
    inv = jax.ShapeDtypeStruct((-(-C // 128), L, 128), F32)
    n = UNROLL
    rowb = pl.BlockSpec((n * BLK, C), lambda i: (i, 0))
    fix = lambda s: pl.BlockSpec(s, lambda i: (0,) * len(s))
    metab = pl.BlockSpec((n * BLK, meta.shape[1]), lambda i: (i, 0))
    segb = pl.BlockSpec((n, 1, gc), lambda i: (i, 0, 0))
    invb = pl.BlockSpec((inv.shape[0], n * BLK, 128), lambda i: (0, i, 0))
    sd = lambda dt: jax.ShapeDtypeStruct((L, C), dt)
    tail = [fix((8, C)), metab, segb, fix((BLK, BLK)), fix((gc, gc))]
    tail_kinds = [None, "row", "n", None, None]
    *six, ri, ab = pl.pallas_call(
        functools.partial(blocks_kernel, first_block, ["row"] * 7 + tail_kinds + ["row"] * 7 + ["inv"], range(n), ()),
        grid=(NB // n,),
        in_specs=[rowb] * 7 + tail,
        out_specs=[rowb] * 7 + [invb],
        out_shape=[sd(BF)] * 6 + [sd(F32), inv],
        compiler_params=params(),
    )(*ins, vec, meta, segrow, tri, ones)
    lanes = inv.shape[0] * 2 * NB
    tt = pl.pallas_call(
        solve_kernel, out_shape=inv, scratch_shapes=[pltpu.VMEM((BLK, SD, lanes), F32)] * 2, compiler_params=params()
    )(ab)
    kinds = ["row"] * 6 + ["inv"] + tail_kinds + ["row"] * 5 + ["pair", "row", "n", None]
    pairb = pl.BlockSpec((2 * n * BLK, C), lambda i: (i, 0))
    y, nrm, rstd, extra, u, al, lb, s = pl.pallas_call(
        functools.partial(blocks_kernel, forward_block, kinds, range(n), (len(kinds) - 1,)),
        grid=(NB // n,),
        in_specs=[rowb] * 6 + [invb] + tail,
        out_specs=[rowb] * 5 + [pairb, rowb, pl.BlockSpec((n, G, gc, gc), lambda i: (i, 0, 0, 0))],
        out_shape=[sd(BF)] + [sd(F32)] * 3 + [sd(BF), jax.ShapeDtypeStruct((2 * L, C), BF), sd(BF), jax.ShapeDtypeStruct((NB, G, gc, gc), BF)],
        scratch_shapes=[pltpu.VMEM((G, gc, gc), F32)],
        compiler_params=params(),
    )(*six, tt, vec, meta, segrow, tri, ones)
    return y, (nrm, rstd, extra, *six, tt, u, al, lb, s, ri)


def recurrence_backward(dy, saved, ins, vec, meta, segrow):
    L, C = ins[0].shape
    NB, gc = L // BLK, min(C, 256)
    G = C // gc
    tri, tru, ones = consts(C)
    n = UNROLL
    rev = lambda i: NB // n - 1 - i
    rowb = pl.BlockSpec((n * BLK, C), lambda i: (rev(i), 0))
    fix = lambda s: pl.BlockSpec(s, lambda i: (0,) * len(s))
    metab = pl.BlockSpec((n * BLK, meta.shape[1]), lambda i: (rev(i), 0))
    segb = pl.BlockSpec((n, 1, gc), lambda i: (rev(i), 0, 0))
    sb = pl.BlockSpec((n, G, gc, gc), lambda i: (rev(i), 0, 0, 0))
    invb = pl.BlockSpec((-(-C // 128), n * BLK, 128), lambda i: (0, rev(i), 0))
    kinds = ["row"] * 10 + ["inv", "row", "pair", "row", "n"] + ["row"] * 8 + [None, "row", "n", None, None, None] + ["row"] * 7 + [None] * 2
    last = len(kinds) - 1
    return pl.pallas_call(
        functools.partial(blocks_kernel, backward_block, kinds, range(n - 1, -1, -1), (last - 1, last)),
        grid=(NB // n,),
        in_specs=[rowb] * 10
        + [invb, rowb, pl.BlockSpec((2 * n * BLK, C), lambda i: (rev(i), 0)), rowb, sb]
        + [rowb] * 8
        + [fix((8, C)), metab, segb, fix((BLK, BLK)), fix((BLK, BLK)), fix((gc, gc))],
        out_specs=[rowb] * 7 + [fix((8, C))],
        out_shape=[jax.ShapeDtypeStruct((L, C), BF)] * 7 + [jax.ShapeDtypeStruct((8, C), F32)],
        scratch_shapes=[pltpu.VMEM((G, gc, gc), F32)],
        compiler_params=params(),
    )(dy, *saved, *ins, vec, meta, segrow, tri, tru, ones)


def mix_tile(x, vec, first_row, keep):
    cen = x - jnp.mean(x, axis=-1, keepdims=True)
    hat = cen * lax.rsqrt(jnp.mean(cen * cen, axis=-1, keepdims=True) + 1e-05)
    h = hat * vec[0:1] + vec[1:2]
    row = lax.broadcasted_iota(jnp.int32, h.shape, 0)
    shifted = jnp.where(row == 0, first_row, pltpu.roll(h, 1, 0))
    return hat, h, shifted * keep - h


def mix_forward_kernel(x, meta, vec, sq, low, up, *refs):
    xm, (rp, kp, vp, uw, ua, uv, ug, mid, midb, carry) = refs[:6], refs[6:]

    @pl.when(pl.program_id(0) == 0)
    def _():
        carry[...] = jnp.zeros_like(carry)

    _, h, delta = mix_tile(x[...].astype(F32), vec, carry[0:1], meta[:, 3:4])
    carry[0:1] = h[h.shape[0] - 1 :]
    m = []
    for i in range(6):
        m.append((h + delta * vec[4 + i : 5 + i]).astype(BF))
        xm[i][...] = m[i]
    rp[...] = mm(m[0], sq[0], NN)
    kp[...] = mm(m[2], sq[1], NN)
    vp[...] = mm(m[3], sq[2], NN)
    for out, i, lo, hi, act in ((uw, 1, 0, 128, jnp.tanh), (ua, 4, 128, 256, None), (uv, 3, 256, 384, None), (ug, 5, 384, 640, jax.nn.sigmoid)):
        d = mm(m[i], low[:, lo:hi], NN)
        if act is not None:
            d = act(d)
        b = d.astype(BF)
        mid[:, lo:hi] = d
        midb[:, lo:hi] = b
        out[...] = mm(b, up[:, lo:hi], NT)


def mix_backward_kernel(drp, dkp, dvp, duw, dua, duv, dug, x, above, meta, mid, vec, sq, low, up, dh, dd, gv, carry, hat_s):
    n, D = x.shape
    step = min(D, 512)

    @pl.when(pl.program_id(0) == 0)
    def _():
        carry[...] = jnp.zeros_like(carry)
        gv[...] = jnp.zeros_like(gv)

    def normalized(v):
        v = v.astype(F32)
        cen = v - jnp.mean(v, axis=-1, keepdims=True)
        return cen * lax.rsqrt(jnp.mean(cen * cen, axis=-1, keepdims=True) + 1e-05)

    hat_s[...] = normalized(x[...])
    prev = normalized(above[...])[above.shape[0] - 1 :]
    keep = meta[:, 3:4]
    dw = (mm(duw[...], up[:, 0:128], NN) * (1.0 - mid[:, 0:128] * mid[:, 0:128])).astype(BF)
    da = mm(dua[...], up[:, 128:256], NN).astype(BF)
    dv = mm(duv[...], up[:, 256:384], NN).astype(BF)
    s = mid[:, 384:640]
    dg = (mm(dug[...], up[:, 384:640], NN) * s * (1.0 - s)).astype(BF)
    dd[:, 0:128] = dw
    dd[:, 128:256] = da
    dd[:, 256:384] = dv
    dd[:, 384:640] = dg
    row = lax.broadcasted_iota(jnp.int32, (n, step), 0)
    for k in range(D // step):
        sl = slice(k * step, (k + 1) * step)
        gain, bias = vec[0:1, sl], vec[1:2, sl]
        hat = hat_s[:, sl]
        h = hat * gain + bias
        delta = jnp.where(row == 0, prev[:, sl] * gain + bias, pltpu.roll(h, 1, 0)) * keep - h
        total = ds = None
        for i in range(6):
            if i == 0:
                d = mm(drp[...], sq[0, sl], NT)
            elif i == 1:
                d = mm(dw, low[sl, 0:128], NT)
            elif i == 2:
                d = mm(dkp[...], sq[1, sl], NT)
            elif i == 3:
                d = mm(dvp[...], sq[2, sl], NT) + mm(dv, low[sl, 256:384], NT)
            elif i == 4:
                d = mm(da, low[sl, 128:256], NT)
            else:
                d = mm(dg, low[sl, 384:640], NT)
            gv[i : i + 1, sl] += jnp.sum(d * delta, axis=0, keepdims=True)
            scaled = d * vec[4 + i : 5 + i, sl]
            total = d if total is None else total + d
            ds = scaled if ds is None else ds + scaled
        back = ds * keep
        moved = jnp.where(row == n - 1, carry[0:1, sl], pltpu.roll(back, n - 1, 0))
        carry[0:1, sl] = back[0:1]
        g = total - ds + moved
        dh[:, sl] = g.astype(BF)
        gv[6:7, sl] += jnp.sum(g * hat, axis=0, keepdims=True)
        gv[7:8, sl] += jnp.sum(g, axis=0, keepdims=True)


def hidden_kernel(x, g, key, value, q, dk, dx):
    k = jnp.maximum(mm(x[...], key[...], NN), 0.0)
    q[...] = (k * k).astype(BF)
    d = (mm(g[...], value[...], NT) * (2.0 * k)).astype(BF)
    dk[...] = d
    dx[...] = mm(d, key[...], NT).astype(BF)


def hidden(x, g, key, value):
    n, D = x.shape
    H = key.shape[1]
    tok = lambda m: pl.BlockSpec((256, m), lambda i: (i, 0))
    fix = lambda s: pl.BlockSpec(s, lambda i: (0, 0))
    sd = lambda m: jax.ShapeDtypeStruct((n, m), BF)
    return pl.pallas_call(
        hidden_kernel,
        grid=(n // 256,),
        in_specs=[tok(D), tok(D), fix(key.shape), fix(value.shape)],
        out_specs=[tok(H), tok(H), tok(D)],
        out_shape=[sd(H), sd(H), sd(D)],
        cost_estimate=takes(30),
        compiler_params=params(),
    )(x, g, key, value)


def weight_kernel(x0, x1, x2, x3, x4, x5, drp, dkp, dvp, dd, duw, dua, duv, dug, mid, z, dt, sq, down, up, sq3):
    sq[0] = mm(x0[...], drp[...], TN).astype(BF)
    sq[1] = mm(x2[...], dkp[...], TN).astype(BF)
    sq[2] = mm(x3[...], dvp[...], TN).astype(BF)
    for x, lo, hi in ((x1, 0, 128), (x4, 128, 256), (x3, 256, 384), (x5, 384, 640)):
        down[:, lo:hi] = mm(x[...], dd[:, lo:hi], TN).astype(BF)
    sq3[...] = mm(z[...], dt[...], TN).astype(BF)

    @pl.when(pl.program_id(0) == 0)
    def _():
        for d, lo, hi in ((duw, 0, 128), (dua, 128, 256), (duv, 256, 384), (dug, 384, 640)):
            up[:, lo:hi] = mm(d[...], mid[:, lo:hi], TN).astype(BF)


def weight_grads(xm, grads, dd, mid, z, dt):
    L, D = xm[0].shape
    C, wide = grads[0].shape[1], mid.shape[1]
    n = 256 if L <= 1024 else 128
    tok, own = z.shape
    feat = pl.BlockSpec((L, n), lambda i: (0, i))
    fix = lambda m: pl.BlockSpec((L, m), lambda i: (0, 0))
    sd = jax.ShapeDtypeStruct
    return pl.pallas_call(
        weight_kernel,
        grid=(D // n,),
        in_specs=[feat] * 6 + [fix(C)] * 3 + [fix(wide)] + [fix(C)] * 4 + [fix(wide), pl.BlockSpec((tok, own), lambda i: (0, 0)), pl.BlockSpec((tok, n), lambda i: (0, i))],
        out_specs=[
            pl.BlockSpec((3, n, C), lambda i: (0, i, 0)),
            pl.BlockSpec((n, wide), lambda i: (i, 0)),
            pl.BlockSpec((C, wide), lambda i: (0, 0)),
            pl.BlockSpec((own, n), lambda i: (0, i)),
        ],
        out_shape=[sd((3, D, C), BF), sd((D, wide), BF), sd((C, wide), BF), sd((own, D), BF)],
        cost_estimate=takes(26),
        compiler_params=params(),
    )(*xm, *grads[:3], dd, *grads[3:], mid, z, dt)


TILE = 256


def mix_forward(x, meta, vec, sq, low, up):
    L, D = x.shape
    C = up.shape[0]
    wide = up.shape[1]
    tok = lambda n: pl.BlockSpec((TILE, n), lambda i: (i, 0))
    fix = lambda s: pl.BlockSpec(s, lambda i: (0,) * len(s))
    sd = jax.ShapeDtypeStruct
    out = pl.pallas_call(
        mix_forward_kernel,
        grid=(L // TILE,),
        in_specs=[tok(D), tok(meta.shape[1]), fix(vec.shape), fix(sq.shape), fix((D, wide)), fix(up.shape)],
        out_specs=[tok(D)] * 6 + [tok(C)] * 7 + [tok(wide)] * 2,
        out_shape=[sd((L, D), BF)] * 6 + [sd((L, C), F32)] * 7 + [sd((L, wide), F32), sd((L, wide), BF)],
        scratch_shapes=[pltpu.VMEM((8, D), F32)],
        cost_estimate=takes(30),
        compiler_params=params(),
    )(x, meta, vec, sq, low, up)
    return out[:6], out[6:13], out[13], out[14]


def mix_backward(grads, x, meta, mid, vec, sq, low, up):
    L, D = x.shape
    C = up.shape[0]
    wide = up.shape[1]
    n = L // TILE
    rev = lambda i: n - 1 - i
    tok = lambda m: pl.BlockSpec((TILE, m), lambda i: (rev(i), 0))
    fix = lambda s: pl.BlockSpec(s, lambda i: (0,) * len(s))
    above = pl.BlockSpec((16, D), lambda i: (jnp.maximum(rev(i) * (TILE // 16) - 1, 0), 0))
    sd = jax.ShapeDtypeStruct
    return pl.pallas_call(
        mix_backward_kernel,
        grid=(n,),
        in_specs=[tok(C)] * 7
        + [tok(D), above, tok(meta.shape[1]), tok(wide), fix(vec.shape), fix(sq.shape), fix((D, wide)), fix(up.shape)],
        out_specs=[tok(D), tok(wide), fix((8, D))],
        out_shape=[sd((L, D), BF), sd((L, wide), BF), sd((8, D), F32)],
        scratch_shapes=[pltpu.VMEM((8, D), F32), pltpu.VMEM((TILE, D), F32)],
        cost_estimate=takes(35),
        compiler_params=params(),
    )(*grads, x, x, meta, mid, vec, sq, low, up)


AXES = ("sa", "sb", "ra", "rc")
PLANE = ("sb", "ra", "rc")
MESH = pl.DeviceIdType.MESH
HBM = pl.BlockSpec(memory_space=pl.ANY)


class Net:
    def __init__(self, local_sem, send_sem, recv_sem):
        self.sems = local_sem, send_sem, recv_sem
        self.size = tuple(lax.axis_size(k) for k in AXES)
        self.me = tuple(lax.axis_index(k) for k in AXES)
        self.locals, self.n, self.k = [], 0, 0

    def at(self, shift):
        return tuple(lax.rem(m + d, n) if d else m for m, d, n in zip(self.me, shift, self.size))

    def greet(self, shifts):
        bar = pltpu.get_barrier_semaphore()
        for s in shifts:
            pl.semaphore_signal(bar, inc=1, device_id=self.at(s), device_id_type=MESH)
        pl.semaphore_wait(bar, len(shifts))

    def keep(self, src, dst):
        copy = pltpu.make_async_copy(src, dst, self.sems[0].at[self.k])
        self.k += 1
        copy.start()
        self.locals.append(copy)

    def send(self, src, dst, shift):
        copy = pltpu.make_async_remote_copy(
            src, dst, self.sems[1].at[self.n], self.sems[2].at[self.n], device_id=self.at(shift), device_id_type=MESH
        )
        self.n += 1
        copy.start()
        return copy

    def settle(self):
        for copy in self.locals:
            copy.wait()


def call_net(body, arrays, out_shapes, cid, n_local, n_send, scratch=()):
    n = len(arrays)
    m = n + len(out_shapes)

    def kernel(*refs):
        body(refs[:n], refs[n:m], refs[m + 3 :], Net(*refs[m : m + 3]))

    return pl.pallas_call(
        kernel,
        out_shape=out_shapes,
        in_specs=[HBM] * n,
        out_specs=[HBM] * len(out_shapes),
        scratch_shapes=[
            pltpu.SemaphoreType.DMA((max(n_local, 1),)),
            pltpu.SemaphoreType.DMA((n_send,)),
            pltpu.SemaphoreType.DMA((n_send,)),
            *scratch,
        ],
        compiler_params=pltpu.CompilerParams(collective_id=cid, has_side_effects=True, vmem_limit_bytes=VM),
    )(*arrays)


def line_shifts():
    return [(d, 0, 0, 0) for d in range(1, lax.axis_size("sa"))]


CHIPS = [(0, 1, 0, 0), (0, 0, 1, 0), (0, 1, 1, 0)]
OTHER_CORE = (0, 0, 0, 1)


class Gather:
    def __init__(self, net, src, view, half=None):
        self.net, self.src, self.view, self.half = net, src, view, half

    def slot(self, shift):
        return self.net.at(shift)[1:]

    def hand(self, view, shift):
        copy = self.net.send(view, view, shift)
        self.out.append(copy)
        return copy

    def first(self):
        net = self.net
        here = self.view(*net.me[1:])
        net.keep(self.src, here)
        self.near = [net.send(self.src, here, s) for s in CHIPS[:2]]
        self.far = [] if self.half else [net.send(self.src, here, CHIPS[2])]
        self.out = self.near + self.far
        self.core = [net.send(self.src, here, OTHER_CORE)]

    def to_core(self, shift):
        view = self.view(*self.slot(shift))
        self.core.append(self.net.send(view, view, OTHER_CORE))

    def second(self):
        for h, copy in enumerate(self.near):
            copy.wait_recv()
            if self.half:
                self.far.append(self.hand(self.half(*self.slot(CHIPS[h]), h), CHIPS[1 - h]))
            self.to_core(CHIPS[h])

    def third(self):
        for copy in self.far:
            copy.wait_recv()
        self.to_core(CHIPS[2])

    def end(self):
        for copy in self.out:
            copy.wait_send()
        for copy in self.core:
            copy.wait()


def gather_body(net, gathers):
    for step in ("second", "third", "end"):
        for g in gathers:
            getattr(g, step)()


def line_exchange(arrays, gathers, cid, shares=()):
    m = len(arrays)
    n = m + len(gathers)

    def body(ins, outs, _, net):
        shifts = line_shifts()
        net.greet(shifts + (plane_shifts() if shares else CHIPS[:2] + [OTHER_CORE] if gathers else []))
        a = net.me[0]
        open_ = []
        for x, o in zip(ins[:m], outs):
            open_ += [net.send(x.at[net.at(s)[0]], o.at[a], s) for s in shifts]
            net.keep(x.at[a], o.at[a])
        planes = [
            Gather(net, x, functools.partial(g[2], o), functools.partial(g[3], o))
            for x, o, g in zip(ins[m:], outs[m:], gathers)
        ]
        for g in planes:
            g.first()
        mine = net.me[1:]
        for x, o in zip(ins[n:], outs[n:]):
            open_ += [net.send(x.at[net.at(s)[1:]], o.at[mine], s) for s in plane_shifts()]
            net.keep(x.at[mine], o.at[mine])
        gather_body(net, planes)
        for copy in open_:
            copy.wait()
        net.settle()

    sd = jax.ShapeDtypeStruct
    shapes = [sd(x.shape, x.dtype) for x in arrays] + [sd(g[1], g[0].dtype) for g in gathers]
    shapes += [sd(x.shape, x.dtype) for x in shares]
    n_send = (lax.axis_size("sa") - 1) * m + 8 * len(gathers) + 7 * len(shares)
    operands = [*arrays, *(g[0] for g in gathers), *shares]
    return call_net(body, operands, shapes, cid, len(operands), n_send)


def rows_gather(x):
    sizes = tuple(lax.axis_size(k) for k in PLANE)
    half = x.shape[0] // 2
    return (
        x,
        sizes + x.shape,
        lambda o, b, y, c: o.at[b, y, c],
        lambda o, b, y, c, h: o.at[b, y, c, pl.ds(h * half, half)],
    )


def swap_first(net, x, o):
    b = net.me[1]
    net.keep(x.at[b], o.at[b])
    return [net.send(x.at[net.at(CHIPS[0])[1]], o.at[b], CHIPS[0])]


def plane_shifts():
    return [(0, i // 4, i // 2 % 2, i % 2) for i in range(1, 8)]


def start_exchange(tokens, sq, low, up, key, cid):
    A, B = lax.axis_size("sa"), lax.axis_size("sb")
    S, hops = A * B, A - 1
    sizes = tuple(lax.axis_size(k) for k in PLANE)
    n_fixed = 2 * hops + 8 + 8 + 7 + 7 + 1

    def body(ins, outs, scratch, net):
        x, q, lo, u, ke = ins
        xo, qo, loo, uo, ko, q_line, lo_line = outs
        line = line_shifts()
        net.greet(line + plane_shifts())
        a, b, y, c = net.me
        me = a * B + b
        ssem, rsem = net.sems[1:]

        def block(i, k):
            return xo.at[i * B + (b if k == 0 else 1 - b)]

        def index(way, t, k):
            return n_fixed + (way * hops + t) * 2 + k

        def origin(way, t):
            return a - t if way == 0 else a + t

        def have(way, t):
            return a >= t if way == 0 else a <= A - 1 - t

        def can(way):
            return a < A - 1 if way == 0 else a > 0

        def relay(way, t, k):
            dst = block(origin(way, t), k)
            i = index(way, t, k)
            to = (a + 1 if way == 0 else a - 1, b, y, c)
            src = x.at[b] if t == 0 and k == 0 else dst
            return pltpu.make_async_remote_copy(src, dst, ssem.at[i], rsem.at[i], device_id=to, device_id_type=MESH)

        def relay_start(t, k):
            for way in range(2):

                @pl.when(have(way, t) & can(way))
                def _(way=way):
                    relay(way, t, k).start()

        def relay_arrived(t, k):
            for way in range(2):

                @pl.when(have(way, t))
                def _(way=way):
                    dst, i = block(origin(way, t), k), index(way, t - 1, k)
                    pltpu.make_async_remote_copy(
                        dst, dst, ssem.at[i], rsem.at[i], device_id=net.at(OTHER_CORE), device_id_type=MESH
                    ).wait_recv()

        first = []
        for s in line:
            first.append(net.send(q.at[net.at(s)[0]], q_line.at[:, a], s))
            first.append(net.send(lo, lo_line.at[a], s))
        relay_start(0, 0)
        across = net.send(x.at[1 - b], xo.at[me], CHIPS[0])
        net.keep(q.at[a], q_line.at[:, a])
        net.keep(lo, lo_line.at[a])
        planes = [Gather(net, u, lambda i, j, k: uo.at[i, j, k])]
        planes[0].first()
        across.wait_recv()
        relay_start(0, 1)
        for copy in first:
            copy.wait()
        net.settle()
        net.locals = []
        net.keep(x.at[b], xo.at[me])
        h = A // 2
        planes.append(
            Gather(net, q_line, lambda i, j, k: qo.at[:, :, i, j, k], lambda i, j, k, p: qo.at[:, pl.ds(p * h, h), i, j, k])
        )
        planes.append(Gather(net, lo_line, lambda i, j, k: loo.at[:, i, j, k], lambda i, j, k, p: loo.at[pl.ds(p * h, h), i, j, k]))
        planes[1].first()
        planes[2].first()
        mine = net.me[1:]
        rest = [net.send(ke.at[net.at(s)[1:]], ko.at[mine], s) for s in plane_shifts()]
        net.keep(ke.at[mine], ko.at[mine])
        for t in range(1, hops):
            for k in range(2):
                relay_arrived(t, k)
                relay_start(t, k)
            if t == 1:
                for g in planes:
                    g.second()
        for g in planes:
            g.third()
        for k in range(2):
            relay_arrived(hops, k)
        for t in range(hops):
            for k in range(2):
                for way in range(2):

                    @pl.when(have(way, t) & can(way))
                    def _(way=way, t=t, k=k):
                        relay(way, t, k).wait_send()

        across.wait_send()
        for g in planes:
            g.end()
        for copy in rest:
            copy.wait()
        net.settle()

    sd = lambda shape, like: jax.ShapeDtypeStruct(shape, like.dtype)
    shapes = [
        sd((S,) + tokens.shape[1:], tokens),
        sd(sq.shape[1:2] + (A,) + sizes + sq.shape[2:], sq),
        sd((A,) + sizes + low.shape, low),
        sd(sizes + up.shape, up),
        sd(key.shape, key),
        sd(sq.shape[1:2] + (A,) + sq.shape[2:], sq),
        sd((A,) + low.shape, low),
    ]
    return call_net(body, [tokens, sq, low, up, key], shapes, cid, 9, n_fixed + 4 * hops)[:5]


def tail_exchange(dh, sq, down, wide, up, narrow, ffn, cid):
    A = lax.axis_size("sa")
    leads = [2, 1, 1, 0, 0, 0]
    halved = [1, 0, 0, None, None, 0]
    arrays = [sq, down, wide, up, narrow, ffn]
    blocks = [x.shape[:n] + x.shape[n + 3 :] for x, n in zip(arrays, leads)]
    n = len(arrays)

    def body(ins, outs, scratch, net):
        ps, pos = ins[1:], outs[1:]
        own, other, chips = scratch[:n], scratch[n : 2 * n], scratch[2 * n :]
        line = line_shifts()
        net.greet(line + CHIPS + [OTHER_CORE])
        a, b, y, c = net.me
        there = net.at(OTHER_CORE)[3]
        pairs = [(i // 2, i % 2) for i in range(4)]

        def block(t, i, j, k):
            return ps[t].at[(slice(None),) * leads[t] + (i, j, k)]

        cores, mine = [], []
        for t in range(n):
            cores.append([net.send(block(t, i, j, there), other[t].at[2 * i + j], OTHER_CORE) for i, j in pairs])
            for i, j in pairs:
                net.keep(block(t, i, j, c), own[t].at[2 * i + j])
            mine.append(net.locals)
            net.locals = []
        open_ = []
        for x, o in zip(ins[:1], outs[:1]):
            open_ += [net.send(x.at[net.at(s)[0]], o.at[a], s) for s in line]
            net.keep(x.at[a], o.at[a])

        def part(t, h):
            if h is None or halved[t] is None:
                return ()
            size = blocks[t][halved[t]] // 2
            return (slice(None),) * halved[t] + (pl.ds(h * size, size),)

        def add(t, k, terms, h=None):
            shape, start = list(blocks[t]), [0] * len(blocks[t])
            if h is not None:
                shape[halved[t]] //= 2
                start[halved[t]] = h * shape[halved[t]]
            step = min(shape[-2], 16)
            per = shape[-2] // step
            count = per
            for size in shape[:-2]:
                count = count * size

            @pl.loop(0, count)
            def _(r):
                index = []
                rest = r // per
                for size, first in zip(reversed(shape[:-2]), reversed(start[:-2])):
                    index.insert(0, first + rest % size)
                    rest = rest // size
                at = (*index, pl.ds(pl.multiple_of(start[-2] + r % per * step, step), step))
                total = own[t][(k, *at)].astype(F32)
                for ref, i in terms:
                    total = total + ref[(i, *at)].astype(F32)
                own[t][(k, *at)] = total.astype(BF)

        def slot(i, j):
            return 2 * i + j

        nb, ny = net.at(CHIPS[0])[1], net.at(CHIPS[1])[2]
        ways = [
            (CHIPS[0], CHIPS[1], lambda j: slot(nb, j), lambda j: slot(b, j), slot(b, ny)),
            (CHIPS[1], CHIPS[0], lambda j: slot(j, ny), lambda j: slot(j, y), slot(nb, y)),
        ]
        me = slot(b, y)
        sent = [[] for _ in range(n)]
        for t in range(n):
            for copy in cores[t] + mine[t]:
                copy.wait()
            for k in range(4):
                add(t, k, [(other[t], k)])
            if halved[t] is None:
                for k, s in enumerate(CHIPS):
                    to = net.at(s)
                    sent[t].append(net.send(own[t].at[slot(to[1], to[2])], chips[t].at[k], s))
                continue
            for h, (s, _, theirs, _, _) in enumerate(ways):
                for j in range(2):
                    src, dst = own[t].at[(theirs(j), *part(t, h))], chips[t].at[(j, *part(t, h))]
                    sent[t].append(net.send(src, dst, s))
        second = [[] for _ in range(n)]
        for t in range(n):
            if halved[t] is None:
                continue
            for h, (_, s, _, ours, across) in enumerate(ways):
                for j in range(2):
                    sent[t][2 * h + j].wait_recv()
                    add(t, ours(j), [(chips[t], j)], h)
                src, dst = own[t].at[(across, *part(t, h))], chips[t].at[(2, *part(t, h))]
                second[t].append(net.send(src, dst, s))
        for t in range(n):
            for copy in second[t] if second[t] else sent[t]:
                copy.wait_recv()
            if halved[t] is None:
                add(t, me, [(chips[t], k) for k in range(3)])
            else:
                add(t, me, [(chips[t], 2)])
            net.keep(own[t].at[me], pos[t])
        for t in range(n):
            for copy in sent[t] + second[t]:
                copy.wait_send()
        for copy in open_:
            copy.wait()
        net.settle()

    sd = jax.ShapeDtypeStruct
    shapes = [sd(dh.shape, BF)] + [sd(s, BF) for s in blocks]
    scratch = [pltpu.VMEM((m,) + s, BF) for m in (4, 4, 3) for s in blocks]
    n_send = (A - 1) + 10 * n
    return call_net(body, [dh, *arrays], shapes, cid, 1 + 5 * n, n_send, scratch)


def last_exchange(swaps, sq, lines, key, cid):
    m = len(swaps)
    n = m + 1 + len(lines)

    def body(ins, outs, _, net):
        line, plane = line_shifts(), plane_shifts()
        net.greet(line + plane)
        a = net.me[0]
        mine = net.me[1:]
        open_ = []
        for i, (x, o) in enumerate(zip(ins[:n], outs)):
            if i < m:
                open_ += swap_first(net, x, o)
                continue
            view = (lambda x, k: x.at[:, k]) if i == m else (lambda x, k: x.at[k])
            open_ += [net.send(view(x, net.at(s)[0]), o.at[a], s) for s in line]
            net.keep(view(x, a), o.at[a])
        open_ += [net.send(ins[n].at[net.at(s)[1:]], outs[n].at[mine], s) for s in plane]
        net.keep(ins[n].at[mine], outs[n].at[mine])
        for copy in open_:
            copy.wait()
        net.settle()

    sd = jax.ShapeDtypeStruct
    arrays = [*swaps, sq, *lines, key]
    shapes = [sd(x.shape, x.dtype) for x in arrays]
    shapes[m] = sd((sq.shape[1], sq.shape[0]) + sq.shape[2:], sq.dtype)
    n_send = m + (1 + len(lines)) * (lax.axis_size("sa") - 1) + 7
    return call_net(body, arrays, shapes, cid, len(arrays), n_send)


def layer_norm(x, gain, bias):
    cen = x - jnp.mean(x, axis=-1, keepdims=True)
    var = jnp.mean(cen * cen, axis=-1, keepdims=True)
    return cen * lax.rsqrt(var + 1e-05) * gain + bias


def next_line(value, steps):
    count = lax.axis_size("sa")
    first, last = max(0, -steps), min(count, count - steps)
    return lax.ppermute(value, "sa", [(i, i + steps) for i in range(first, last)])


def after(value, *others):
    return lax.optimization_barrier((value, *others))[0]


def per_device(tokens, first_values, lengths, vectors, down, up, square, key_w, value_w, out_grad):
    rows_here, seg, D = tokens.shape
    SA, SB, RA, RC = (lax.axis_size(k) for k in AXES)
    a, b = lax.axis_index("sa"), lax.axis_index("sb")
    S, F = SA * SB, SB * RA * RC
    L = seg * S
    C = D // SA
    NB = L // BLK
    gc = min(C, 256)
    T = SB * seg
    w = square.shape[1]
    n_low, n_vec = down.shape[1], vectors.shape[0]
    FS = key_w.shape[1] // (S * RA * RC)

    lens = lax.dynamic_index_in_dim(lengths, b, 0, keepdims=False)
    count = lens.shape[0]
    lower = jnp.arange(count)[:, None] > jnp.arange(count)[None, :]
    starts = jnp.sum(jnp.where(lower, lens[None, :], 0), axis=1)
    pos = jnp.arange(L, dtype=jnp.int32)
    reset = jnp.any(pos[:, None] == starts[None, :], axis=1).astype(F32)
    segid = jnp.sum((pos[:, None] >= starts[None, :]).astype(F32), axis=1) - 1.0
    blocks = segid.reshape(NB, BLK)
    before = blocks[:, :1] - reset.reshape(NB, BLK)[:, :1]
    carried = (blocks == before).astype(F32).reshape(L)
    live = (blocks == blocks[:, -1:]).astype(F32).reshape(L)
    meta = jnp.stack([segid, carried, live, 1.0 - reset], axis=1)
    segrow = jnp.tile(blocks.reshape(NB, 1, BLK), (1, 1, gc // SD))
    keep_row = (1.0 - reset)[:, None]
    keep_own = lax.dynamic_slice(keep_row, (a * T, 0), (T, 1))

    first_sliced = first_values.reshape(rows_here, seg, SA, C).transpose(2, 0, 1, 3).reshape(S, seg, C)
    first_row = lax.all_to_all(first_sliced, ("sa", "sb"), split_axis=0, concat_axis=0, tiled=True).reshape(L, C)
    cuts = [0, DECAY_INNER, DECAY_INNER + LA, DECAY_INNER + LA + LV, n_low]

    wide_at = [0, 128, 256, 384]
    spot = jnp.concatenate([at + jnp.arange(q - p) for at, p, q in zip(wide_at, cuts[:-1], cuts[1:])])
    place = (spot[:, None] == jnp.arange(768)[None, :]).astype(BF)
    place_vec = (640 + jnp.arange(n_vec)[:, None] == jnp.arange(768)[None, :]).astype(BF)
    low_mine = (mm(down, place, NN) + mm(vectors, place_vec, TN)).astype(BF)
    up_mine = mm(up, place[:, :640], TN).astype(BF)
    sq_mine = square[:3].reshape(3, w, SA, C).transpose(2, 0, 1, 3)
    half = SA * FS
    key_mine = key_w.reshape(w, SA, F, FS).transpose(2, 0, 1, 3).reshape(SB, RA, RC, w, half)
    x_row, sq, low, up_heads, key_line = start_exchange(tokens, sq_mine, low_mine, up_mine, key_mine, 1)
    sq3 = lax.all_gather(after(square[3], x_row), AXES, axis=0, tiled=True)
    x_row = x_row.reshape(L, D)
    sq = sq.reshape(3, D, C)
    low = low.reshape(D, 768)
    up_w = up_heads.reshape(C, 640)
    vec = low[:, 640 : 640 + n_vec].astype(F32).T
    vec_heads = lax.dynamic_slice(vec, (10, a * C), (8, C))
    FW = F * w
    halves = [slice(i * half, (i + 1) * half) for i in range(D // half)]
    kv = jnp.concatenate([key_line.reshape(FW, half), *(value_w[:, s] for s in halves)], axis=0)

    xm, (rp, kp, vp, uw, ua, uv, ug), mid, mid_low = mix_forward(x_row, meta, vec, sq, low, up_w)
    ins = (rp, kp, vp, uw, ua, uv, first_row)
    y, saved = recurrence_forward(ins, vec_heads, meta, segrow)
    kv_all = lax.all_gather(after(kv, sq3, saved[9]), "sa", axis=0)
    key_all = kv_all[:, :FW].reshape(D, half)
    value_all = jnp.concatenate(
        [kv_all[:, FW + i * FS : FW + (i + 1) * FS].reshape(half, half) for i in range(D // half)], axis=1
    )
    z = (y.astype(F32) * ug).astype(BF)
    before = jnp.concatenate([jnp.zeros((1, 16, C), BF), z.reshape(SA, T, C)[:-1, T - 16 :]], axis=0)
    z_blocks = jnp.concatenate([before, z.reshape(SA, T, C)], axis=1)
    gather_g = (
        out_grad,
        (SB, RA, RC, SB, seg, D),
        lambda o, i, j, k: o.at[:, j, k, i],
        lambda o, i, j, k, h: o.at[h, j, k, i],
    )
    z_own, g_all = line_exchange([z_blocks], [gather_g], 2)
    g_all = g_all.reshape(F * T, D)
    z_more = z_own.transpose(1, 0, 2).reshape(T + 16, D)
    z_own = z_more[16:]
    z_share = z_own.reshape(T, SA, F, w).transpose(2, 0, 1, 3).reshape(SB, RA, RC, T, SA * w)

    x_own = lax.dynamic_slice(x_row, (a * T, 0), (T, D)).astype(F32)
    x_before = lax.dynamic_slice(x_row, (jnp.maximum(a * T - 16, 0), 0), (16, D)).astype(F32)
    x1_more = jnp.concatenate([x_before, x_own], axis=0) + mm(z_more, sq3, NN)
    x1 = x1_more[16:]
    h2, norm2_pull = jax.vjp(layer_norm, x1, vec[2], vec[3])
    edge2 = layer_norm(x1_more[15:16], vec[2], vec[3])

    def channel_mix(h, edge, mix):
        s = jnp.concatenate([edge, h[:-1]], axis=0) * keep_own
        return h + (s - h) * mix

    xc, cmix_pull = jax.vjp(channel_mix, h2, edge2, vec[18])
    (xc_all,) = line_exchange([], [rows_gather(xc.astype(BF))], 3)
    xc_all = xc_all.reshape(F * T, D)
    q, dkc, dxc_part = hidden(xc_all, g_all, key_all, value_all)
    dxc = lax.psum_scatter(dxc_part, PLANE, scatter_dimension=0, tiled=True)
    ffn_part = mm(q, value_all, NN).astype(BF)
    value_part = mm(q, g_all, TN).astype(BF).reshape(SA, FS, D)
    key_part = mm(xc_all, dkc, TN).astype(BF).reshape(SA, FW, half)
    kv_part = jnp.concatenate([key_part, *(value_part[:, :, s] for s in halves)], axis=1)
    dxc, kv_part, ffn_part = lax.optimization_barrier((dxc, kv_part, ffn_part))

    dh2, dedge2, g18 = cmix_pull(dxc.astype(F32))
    dh2 = dh2.at[-1:].add(next_line(dedge2, -1))
    dx1n, g2, g3 = norm2_pull(dh2)
    slot = (b * RA + lax.axis_index("ra")) * RC + lax.axis_index("rc")
    dx1 = lax.dynamic_slice(g_all, (slot * T, 0), (T, D)).astype(F32) + dx1n
    dt = dx1.astype(BF)
    dz = mm(dt, sq3, NT).astype(BF)
    dz_row, dt_all, z_share = line_exchange(
        [dz.reshape(T, SA, C).transpose(1, 0, 2)], [rows_gather(dt)], 4, [z_share]
    )
    kv_grad = lax.psum_scatter(kv_part.reshape(-1, half), "sa", scatter_dimension=0, tiled=True)
    dz_row = dz_row.reshape(L, C).astype(F32)

    dy = (dz_row * ug).astype(BF)
    dug = (dz_row * y.astype(F32)).astype(BF)
    drp, dkp, dvp, duw, dua, duv, dfl, dvec = recurrence_backward(dy, saved, ins, vec_heads, meta, segrow)
    dfl = lax.all_to_all(dfl.reshape(S, seg, C), ("sa", "sb"), split_axis=0, concat_axis=0, tiled=True)
    dh1, dd, gmix = mix_backward((drp, dkp, dvp, duw, dua, duv, dug), x_row, meta, mid, vec, sq, low, up_w)
    g0, g1 = gmix[6], gmix[7]

    sq_part, down_part, up_part, sq3_part = weight_grads(
        xm, (drp, dkp, dvp, duw, dua, duv, dug), dd, mid_low, z_share.reshape(F * T, SA * w), dt_all.reshape(F * T, D)
    )
    dfl, sq_part = lax.optimization_barrier((dfl, sq_part))
    first_grad = dfl.reshape(SA, SB, seg, C).transpose(1, 2, 0, 3).reshape(rows_here, seg, D)
    wide = jnp.stack([g0, g1, g2, g3, *(gmix[i] for i in range(6)), g18] + [jnp.zeros_like(g0)] * 5).astype(BF)
    wide = jnp.pad(wide.T, ((0, 0), (0, 112)))
    narrow = jnp.pad(dvec.astype(BF).T, ((0, 0), (0, 120)))
    plane = (SB, RA, RC, w)
    dh1_own, sq_sum, down_sum, wide_sum, up_sum, narrow_sum, ffn = tail_exchange(
        dh1.reshape(SA, T, D),
        sq_part.reshape((3, SA) + plane + (C,)),
        down_part.reshape((SA,) + plane + (640,)),
        wide.reshape((SA,) + plane + (128,)),
        up_part.reshape(plane + (640,)),
        narrow.reshape(plane + (128,)),
        ffn_part.reshape(SB, RA, RC, T, D),
        5,
    )
    dh1_own = jnp.sum(dh1_own.astype(F32), axis=0)
    _, norm1_pull = jax.vjp(lambda x: layer_norm(x, vec[0], vec[1]), x_own)
    (dx0,) = norm1_pull(dh1_own)
    mixed = (x1 + ffn.astype(F32)).astype(BF)
    tokens_grad, mixed_out, sq_sum, down_sum, wide_sum, sq3_sum, key_grad = last_exchange(
        [(dx1 + dx0).astype(BF).reshape(SB, seg, D), mixed.reshape(SB, seg, D)],
        sq_sum,
        [down_sum, wide_sum, sq3_part.reshape(SA, w, D)],
        kv_grad[:FW].reshape(SB, RA, RC, w, half),
        6,
    )
    sq3_sum = jnp.sum(sq3_sum.astype(F32), axis=0)
    square_grad = jnp.concatenate([sq_sum.transpose(1, 2, 0, 3).reshape(3, w, D).astype(F32), sq3_sum[None]], axis=0)
    narrow_pieces = lambda m: [m[:, i : i + q - p] for i, p, q in zip(wide_at, cuts[:-1], cuts[1:])]
    down_grad = jnp.concatenate(narrow_pieces(jnp.sum(down_sum.astype(F32), axis=0)), axis=1)
    up_grad = jnp.concatenate(narrow_pieces(up_sum.astype(F32)), axis=1).T
    wide_t = jnp.sum(wide_sum.astype(F32), axis=0)[:, :16].T
    narrow_t = narrow_sum[:, :8].astype(F32).T
    vectors_gradient = jnp.concatenate([wide_t[:10], narrow_t, wide_t[10:11]], axis=0)
    value_grad = jnp.concatenate([kv_grad[FW + i * FS : FW + (i + 1) * FS] for i in range(D // half)], axis=1)
    value_grad = value_grad.astype(F32)
    key_grad = key_grad.reshape(F, w, SA, FS).transpose(1, 2, 0, 3).reshape(w, -1).astype(F32)
    return (
        mixed_out,
        tokens_grad,
        first_grad,
        vectors_gradient,
        down_grad,
        up_grad,
        square_grad,
        key_grad,
        value_grad,
    )


def solution(mesh):
    seq, row = mesh.shape["seq"], mesh.shape["row"]
    fine = Mesh(mesh.devices.reshape(seq // 2, 2, row // 2, 2), AXES)
    S, R = ("sa", "sb"), ("ra", "rc")
    in_specs = (
        P(R, S, None),
        P(R, S, None),
        P(R, None),
        P(None, S + R),
        P(S + R, None),
        P(None, S + R),
        P(None, S + R, None),
        P(S + R, None),
        P(S + R, None),
        P(R, S, None),
    )
    out_specs = (
        P(R, S, None),
        P(R, S, None),
        P(R, S, None),
        P(None, S + R),
        P(S + R, None),
        P(None, S + R),
        P(None, S + R, None),
        P(S + R, None),
        P(S + R, None),
    )
    return jax.shard_map(per_device, mesh=fine, in_specs=in_specs, out_specs=out_specs, check_vma=False)
```
